256 devices in a mesh: gx: 16 (over x, z_lo), gy: 16 (over y, z_hi, core).
Axes of the slice: x: 4, y: 4, z: 8 (z_hi: 2, z_lo: 4; z = z_hi * 4 + z_lo), core: 2. Of those that a mesh axis runs over, the one named last changes fastest.
Arguments:
- features: bfloat16 [32, 64, 128, 256], P('gx', 'gy'), may hold values from -6 to 6
- coords: bfloat16 [32, 64, 3, 128], P('gx', 'gy'), may hold values from 0 to 1
- nbr_cells: int32 [32, 64, 9], P('gx', 'gy'), may hold values from 0 to 2047, as said below
- nbr_count: int32 [32, 64], P('gx', 'gy'), may hold values from 1 to 9
- miller: int32 [3, 1024], replicated, may hold values from -8 to 8
- gammas: float32 [8], replicated, may hold values from 0.3 to 6
- radial_filter: bfloat16 [8, 256], replicated, may hold values from -0.09375 to 0.09375
- reciprocal_filter: bfloat16 [1024, 256], P(('gx', 'gy')), may hold values from -0.00024414062 to 0.00024414062
- norm_gain: float32 [256], replicated, may hold values from 0.1 to 1.9
- w_in: bfloat16 [256, 512], replicated, may hold values from -0.375 to 0.375
- w_out: bfloat16 [512, 256], replicated, may hold values from -0.25 to 0.25
Outputs:
- updated: bfloat16 [32, 64, 128, 256], P('gx', 'gy')
The draws below stay inside these ranges and needn't reach their ends.
Inputs may be any that keep to these rules, and one draw needn't show every extreme that they name: Every entry of nbr_cells names a cell at most one cell away in each of the first two directions, counting periodically; the first nbr_count entries of a list are distinct; the entries after them name the cell itself.
All inputs are finite; a program needn't handle non-finite values.
Results may differ from the reference program's by a relative error of at most 0.009.
Values may be sent and summed in bfloat16 or wider, within the bound.
No kernel may reach another device: no remote copies, remote signals or barrier semaphores. Data moves between devices by JAX's collectives and lax.ppermute only.
A program may use at most 64 MiB of HBM per device.

```python
import math
import jax
import jax.numpy as jnp
from jax import lax

FEATURE_CHANNELS = 256
HID = 512
K = 8
ATOMS_PER_CELL = 128
RECIPROCAL_COUNT = 1024
CELLS_FIRST_AXIS = 32
CELLS_SECOND_AXIS = 64


def neighbour_draw(key):
    key_order = jax.random.fold_in(key, 11)
    key_count = jax.random.fold_in(key, 12)
    slots = jnp.arange(9, dtype=jnp.int32)
    scores = jax.random.randint(key_order, (CELLS_FIRST_AXIS, CELLS_SECOND_AXIS, 9), 0, 1 << 20).astype(jnp.int32) * 16 + slots
    order = jnp.argsort(scores, axis=-1).astype(jnp.int32)
    atom_counts = jax.random.randint(key_count, (CELLS_FIRST_AXIS, CELLS_SECOND_AXIS), 1, 10).astype(jnp.int32)
    atom_counts = atom_counts.at[0, 0].set(9).at[0, 1].set(1)
    step_x = order // 3 - 1
    step_y = order % 3 - 1
    cell_x = jnp.arange(CELLS_FIRST_AXIS, dtype=jnp.int32)[:, None, None]
    cell_y = jnp.arange(CELLS_SECOND_AXIS, dtype=jnp.int32)[None, :, None]
    nearby = (cell_x + step_x) % CELLS_FIRST_AXIS * CELLS_SECOND_AXIS + (cell_y + step_y) % CELLS_SECOND_AXIS
    alive = slots[None, None, :] < atom_counts[:, :, None]
    table = jnp.where(alive, nearby, cell_x * CELLS_SECOND_AXIS + cell_y).astype(jnp.int32)
    return (table, atom_counts)


def draw_nbr_cells(key, part):
    return neighbour_draw(key)[0]


def draw_nbr_count(key, part):
    return neighbour_draw(key)[1]


def with_ends(values, key, least, largest):
    longest = values.shape.index(max(values.shape))
    spots = []
    for shift in (0, 1):
        where = [jax.random.randint(jax.random.fold_in(key, axis), (), 0, length) for axis, length in enumerate(values.shape)]
        where[longest] = (where[longest] + shift) % values.shape[longest]
        spots.append(tuple(where))
    return values.at[spots[0]].set(least).at[spots[1]].set(largest)


def block_scale(key, shape, cuts, least, high):
    factor_of, own = 1.0, jax.random.fold_in(key, 6)
    for dim, blocks in cuts:
        steps = jnp.exp(jax.random.uniform(jax.random.fold_in(own, dim), (blocks,), jnp.float32, least / len(cuts), high / len(cuts)))
        factor_of = factor_of * jnp.repeat(steps, shape[dim] // blocks).reshape([-1 if axis == dim else 1 for axis in range(len(shape))])
    return factor_of


def centred(own_key, shape, scale, limit, shards=(), held_as=jnp.bfloat16):
    drawn = jax.random.normal(own_key, shape, jnp.float32) * scale
    if len(shards) > 0:
        drawn = block_scale(own_key, shape, shards, -0.22, 0.18) * drawn
    return jnp.clip(drawn, min=-limit, max=limit).astype(held_as)


def setup_inputs(seed: int = 0) -> dict:
    keys = jax.random.split(jax.random.key(seed), 12)
    features = centred(keys[0], (CELLS_FIRST_AXIS, CELLS_SECOND_AXIS, ATOMS_PER_CELL, FEATURE_CHANNELS), 1.0, 6.0, ((0, 16), (1, 16)))
    coords = jnp.clip(1.0 * jax.random.uniform(keys[1], (CELLS_FIRST_AXIS, CELLS_SECOND_AXIS, 3, ATOMS_PER_CELL), jnp.float32) ** block_scale(keys[1], (CELLS_FIRST_AXIS, CELLS_SECOND_AXIS, 3, ATOMS_PER_CELL), ((0, 16), (1, 16)), -0.2, 0.2), 0.0, 1.0).astype(jnp.bfloat16)
    nbr_cells = draw_nbr_cells(jax.random.fold_in(keys[11], 71), 0)
    nbr_count = draw_nbr_count(jax.random.fold_in(keys[11], 71), 0)
    miller = with_ends(jax.random.randint(keys[4], (3, RECIPROCAL_COUNT), -8, 9), jax.random.fold_in(keys[4], 1), -8, 8).astype(jnp.int32)
    gammas = jnp.clip(jnp.exp(jax.random.uniform(keys[5], (K,), jnp.float32, math.log(0.3), math.log(6.0))), 0.3, 6.0)
    radial_filter = centred(keys[6], (K, FEATURE_CHANNELS), (K * ATOMS_PER_CELL * 4) ** -0.5, 0.09375)
    reciprocal_filter = centred(keys[7], (RECIPROCAL_COUNT, FEATURE_CHANNELS), (2 * RECIPROCAL_COUNT * ATOMS_PER_CELL * CELLS_FIRST_AXIS * CELLS_SECOND_AXIS) ** -0.5, 0.00024414062, ((0, 256),))
    norm_gain = jnp.clip(1.0 + 0.18 * jax.random.normal(keys[8], (FEATURE_CHANNELS,), jnp.float32), 0.1, 1.9)
    w_in = centred(keys[9], (FEATURE_CHANNELS, HID), FEATURE_CHANNELS ** -0.5, 0.375)
    w_out = centred(keys[10], (HID, FEATURE_CHANNELS), HID ** -0.5, 0.25)
    return dict(features=features, coords=coords, nbr_cells=nbr_cells, nbr_count=nbr_count, miller=miller, gammas=gammas, radial_filter=radial_filter, reciprocal_filter=reciprocal_filter, norm_gain=norm_gain, w_in=w_in, w_out=w_out)


TWO_PI = 6.283185307179586
slab_depth = 2.0
epsilon = 1e-06

def neighbour_weights(nbr_cells, nbr_count, cell_x, cell_y, total_x, total_y):
    slots = jnp.arange(9, dtype=jnp.int32)
    near_x = nbr_cells // total_y
    near_y = nbr_cells % total_y
    step_x = (near_x - cell_x[:, None, None] + 1) % total_x - 1
    step_y = (near_y - cell_y[None, :, None] + 1) % total_y - 1
    offset_code = (step_x + 1) * 3 + (step_y + 1)
    alive = slots[None, None, :] < nbr_count[:, :, None]
    match = (offset_code[..., None] == slots) & alive[..., None]
    return lax.optimization_barrier(jnp.sum(jnp.where(match, 1.0, 0.0).astype(jnp.float32), axis=2))

def phase_lookup_tables(miller, along_x, along_y, along_z, total_x, total_y):
    indices = miller.astype(jnp.float32)
    angle = TWO_PI * (indices[0][:, None] * (along_x / total_x)[None, :] + indices[1][:, None] * (along_y / total_y)[None, :] + indices[2][:, None] * (along_z / slab_depth)[None, :])
    return (jnp.cos(angle).astype(jnp.bfloat16), jnp.sin(angle).astype(jnp.bfloat16))

def radial(own_coords, near_feat, near_coords, weight, step_x, step_y, gammas, radial_filter):
    mine = own_coords.astype(jnp.float32)
    theirs = near_coords.astype(jnp.float32)
    delta_x = step_x + theirs[..., 0, None, :] - mine[..., 0, :, None]
    delta_y = step_y + theirs[..., 1, None, :] - mine[..., 1, :, None]
    delta_z = theirs[..., 2, None, :] - mine[..., 2, :, None]
    dist_sq = delta_x * delta_x + delta_y * delta_y + delta_z * delta_z
    kernel = jnp.exp(-gammas[:, None, None] * dist_sq[..., None, :, :]).astype(jnp.bfloat16)
    summed = jnp.einsum('...kij,...jc->...kic', kernel.astype(jnp.float32), near_feat.astype(jnp.float32))
    filtered = lax.optimization_barrier(jnp.sum(summed * radial_filter.astype(jnp.float32)[:, None, :], axis=-3))
    return filtered * weight[..., None, None]

def reference(features, coords, nbr_cells, nbr_count, miller, gammas, radial_filter, reciprocal_filter, norm_gain, w_in, w_out):
    total_x, total_y, atoms, width = features.shape
    cell_x = jnp.arange(total_x, dtype=jnp.int32)
    cell_y = jnp.arange(total_y, dtype=jnp.int32)
    weights = neighbour_weights(nbr_cells, nbr_count, cell_x, cell_y, total_x, total_y)
    radial_sum = jnp.zeros(features.shape, jnp.float32)
    for offset in range(9):
        step_x = offset // 3 - 1
        step_y = offset % 3 - 1
        near_feat = jnp.roll(features, (-step_x, -step_y), axis=(0, 1))
        near_coords = jnp.roll(coords, (-step_x, -step_y), axis=(0, 1))

        def one_row(entries, step_x=step_x, step_y=step_y):
            return radial(entries[0], entries[1], entries[2], entries[3], step_x, step_y, gammas, radial_filter)
        radial_sum = radial_sum + lax.map(one_row, (coords, near_feat, near_coords, weights[:, :, offset]))
    coord_float = coords.astype(jnp.float32)

    def row_tables(row_index, row_coords):
        along_x = (row_index.astype(jnp.float32) + row_coords[:, 0, :]).reshape(-1)
        along_y = (cell_y.astype(jnp.float32)[:, None] + row_coords[:, 1, :]).reshape(-1)
        along_z = row_coords[:, 2, :].reshape(-1)
        return phase_lookup_tables(miller, along_x, along_y, along_z, total_x, total_y)

    def accumulate(carry, entries):
        cos_table, sin_table = row_tables(entries[0], entries[1])
        rows = entries[2].reshape(-1, width)
        part = jnp.stack([jnp.dot(cos_table, rows, preferred_element_type=jnp.float32), jnp.dot(sin_table, rows, preferred_element_type=jnp.float32)], axis=1)
        return (carry + part, None)
    sums, _ = lax.scan(accumulate, jnp.zeros((miller.shape[1], 2, width), jnp.float32), (cell_x, coord_float, features))
    coefficients = (sums * reciprocal_filter.astype(jnp.float32)[:, None, :]).astype(jnp.bfloat16)

    def messages_row(entries):
        cos_table, sin_table = row_tables(entries[0], entries[1])
        dims = (((0,), (0,)), ((), ()))
        wave = lax.dot_general(cos_table, coefficients[:, 0], dims, preferred_element_type=jnp.float32)
        wave = wave + lax.dot_general(sin_table, coefficients[:, 1], dims, preferred_element_type=jnp.float32)
        return wave.reshape(total_y, atoms, width)
    recip = lax.map(messages_row, (cell_x, coord_float))
    mixed = (features.astype(jnp.float32) + radial_sum + recip).reshape(-1, width)
    normed = (mixed * lax.rsqrt(lax.optimization_barrier(jnp.mean(mixed * mixed, axis=-1, keepdims=True)) + epsilon) * norm_gain).astype(jnp.bfloat16)
    hidden = jax.nn.silu(jnp.dot(normed, w_in, preferred_element_type=jnp.float32)).astype(jnp.bfloat16)
    updated = mixed + jnp.dot(hidden, w_out, preferred_element_type=jnp.float32)
    return updated.astype(jnp.bfloat16).reshape(features.shape)
```

```python
import functools

import jax
import jax.numpy as jnp
from jax import lax
from jax.experimental import pallas as pl
from jax.experimental.pallas import tpu as pltpu
from jax.sharding import PartitionSpec as P

slab_depth = 2.0
epsilon = 1e-06
LOG2E = 1.4426950408889634
AXES = ("gx", "gy")
F32 = jnp.float32
BF16 = jnp.bfloat16
CX, CY, ATOMS, WIDTH = 2, 4, 128, 256
PACK = 136
VMEM = pltpu.VMEM

SIN_COEF = (3.14159264, -5.16771008, 2.55007752, -0.59829129, 0.07765766)
COS_COEF = (0.99999995, -4.93479283, 4.05841135, -1.33187657, 0.21968961)


def linear(x, y, z, core):
    return (x * 4 + z % 4) * 16 + y * 4 + (z // 4) * 2 + core


def partner_list(step):
    pairs = []
    for x in range(4):
        for y in range(4):
            for z in range(8):
                for core in range(2):
                    pairs.append((linear(x, y, z, core), linear(*step(x, y, z, core))))
    return pairs


def flip_core(x, y, z, core):
    return x, y, z, 1 - core


def flip_plane(first, second):
    def step(x, y, z, core):
        if core == 0:
            return x ^ first, y ^ second, z, core
        return x ^ second, y ^ first, z, core

    return step


def flip_z(which):
    table = ((1, 0, 3, 2, 5, 4, 7, 6), (7, 2, 1, 4, 3, 6, 5, 0), (3, 6, 5, 0, 7, 2, 1, 4))[which]

    def step(x, y, z, core):
        return x, y, table[z], core

    return step


HALVING = (flip_core, flip_plane(1, 0), flip_plane(3, 0), flip_plane(0, 1))
DOUBLING = (flip_plane(0, 3), flip_z(0), flip_z(1), flip_z(2))
CHUNK = 64


def permute(value, step):
    return lax.ppermute(value, AXES, partner_list(step))


def my_place():
    gx, gy = lax.axis_index("gx"), lax.axis_index("gy")
    return gx // 4, gy // 4, (gx % 4) + 4 * ((gy // 2) % 2), gy % 2


def vector_order():
    x, y, z, core = my_place()
    pos = lax.broadcasted_iota(jnp.int32, (1, 1024), 1)
    rest = pos % 4
    mz = (pos // 4) % 8
    mb = (pos // 32) % 2
    b3 = (pos // 64) % 2
    b2 = (pos // 128) % 2
    b1 = (pos // 256) % 2
    owner = core ^ (pos // 512)
    main = jnp.where(owner == 0, x, y) ^ b1 ^ (3 * b2)
    other = jnp.where(owner == 0, y, x)
    coset = (other ^ (other >> 1)) & 1
    side = (coset ^ b3) ^ (3 * mb)
    ox = jnp.where(owner == 0, main, side)
    oy = jnp.where(owner == 0, side, main)
    return linear(ox, oy, mz, owner) * 4 + rest


def wave_kernel(place, coords, features, miller, order, cos_ref, sin_ref, send_ref, keep_ref, turned):
    number = miller[...].astype(F32)
    five = jnp.concatenate([number, number[0:2], jnp.zeros((3, 1024), F32)], axis=0).astype(BF16)
    natural = lax.broadcasted_iota(jnp.int32, (1024, 1024), 0)
    pick = jnp.where(natural == order[...], 1.0, 0.0).astype(BF16)
    placed = jnp.dot(five, pick, preferred_element_type=F32).astype(BF16)
    turned[...] = features[...].astype(F32).T.astype(BF16)
    ones = jnp.ones((1, ATOMS), F32)

    for cell in range(CX * CY):
        block = coords[cell].astype(F32)
        along = (place[0] * CX + cell // CY).astype(F32) / 32.0
        across = (place[1] * CY + cell % CY).astype(F32) / 64.0
        rows = jnp.concatenate(
            [
                block[0:1] / 32.0,
                block[1:2] / 64.0,
                block[2:3] / slab_depth,
                along * ones,
                across * ones,
                jnp.zeros((3, ATOMS), F32),
            ],
            axis=0,
        )
        columns = rows.T.astype(BF16)

        for j in range(4):
            lanes = slice(j * 256, (j + 1) * 256)
            angle = jnp.dot(columns, placed[:, lanes], preferred_element_type=F32)
            r = angle - jnp.round(angle)
            s = r * r
            sine = SIN_COEF[4]
            cosine = COS_COEF[4]
            for a in (3, 2, 1, 0):
                sine = sine * s + SIN_COEF[a]
            for a in (3, 2, 1, 0):
                cosine = cosine * s + COS_COEF[a]
            sine = sine * r
            double = sine + sine
            rows_at = pl.ds(cell * ATOMS, ATOMS)
            cos_ref[rows_at, lanes] = (1.0 - double * sine).astype(BF16)
            sin_ref[rows_at, lanes] = (double * cosine).astype(BF16)

    for half, target in ((0, keep_ref), (1, send_ref)):
        lanes = slice(half * 512, half * 512 + 512)
        for col, table in ((0, cos_ref), (1, sin_ref)):
            total = jnp.dot(turned[...], table[:, lanes], preferred_element_type=F32)
            target[:, col * WIDTH : (col + 1) * WIDTH] = total.T.astype(target.dtype)


def waves(place, coords, features, miller, order):
    vm = pl.BlockSpec(memory_space=VMEM)
    return pl.pallas_call(
        wave_kernel,
        out_shape=(
            jax.ShapeDtypeStruct((1024, 1024), BF16),
            jax.ShapeDtypeStruct((1024, 1024), BF16),
            jax.ShapeDtypeStruct((512, 512), BF16),
            jax.ShapeDtypeStruct((512, 512), F32),
        ),
        in_specs=[pl.BlockSpec(memory_space=pltpu.SMEM), vm, vm, vm, vm],
        out_specs=(vm, vm, vm, vm),
        scratch_shapes=[VMEM((WIDTH, 1024), BF16)],
        compiler_params=pltpu.CompilerParams(vmem_limit_bytes=40 * 1024 * 1024),
        cost_estimate=pl.CostEstimate(flops=4_000_000_000, bytes_accessed=6_000_000, transcendentals=0),
        name="wave_tables",
    )(place, coords, features, miller, order)


def mark_live(place, near_list, near_count, live):
    def clear(i, carry):
        live[i] = 0
        return carry

    lax.fori_loop(0, 72, clear, 0)

    def mark(i, carry):
        cell = i // 9
        entry = near_list[i]
        step_x = ((entry >> 6) - (place[0] * CX + cell // CY) + 1) & 31
        step_y = ((entry & 63) - (place[1] * CY + cell % CY) + 1) & 63

        @pl.when(i % 9 < near_count[cell])
        def _():
            live[cell * 9 + step_x * 3 + step_y] = 1

        return carry

    lax.fori_loop(0, 72, mark, 0)


def own_columns(own, mine):
    for cell in range(CX * CY):
        rows = own[cell // CY, cell % CY, ATOMS:PACK, 0:ATOMS].astype(F32)
        mine[cell] = rows.T


def scaled_features(block, filters, scaled):
    values = block[0:ATOMS, :].astype(F32)
    for k in range(8):
        scaled[k * ATOMS : (k + 1) * ATOMS, :] = (values * filters[k : k + 1, :].astype(F32)).astype(BF16)


def pair(acc, mine, scaled, near, rates, cell, u, v):
    here = mine[cell]
    dx = (near[0:1] + u) - here[:, 0:1]
    dy = (near[1:2] + v) - here[:, 1:2]
    dz = near[2:3] - here[:, 2:3]
    dist = dx * dx + dy * dy + dz * dz
    kernel = jnp.concatenate([jnp.exp2(dist * (rates[k] * -LOG2E)).astype(BF16) for k in range(8)], axis=1)
    acc[cell] += jnp.dot(kernel, scaled[...], preferred_element_type=F32)


def near_rows(block):
    return block[ATOMS:PACK, 0:ATOMS].astype(F32)


def inner_kernel(place, near_list, near_count, rates, filters, own, acc, live, mine, scaled):
    mark_live(place, near_list, near_count, live)
    own_columns(own, mine)
    acc[...] = jnp.zeros_like(acc)

    def one(nb, carry):
        ja, jb = nb // CY, nb % CY
        block = own.at[ja, jb]
        scaled_features(block, filters, scaled)
        near = near_rows(block)

        def inner(p, carry):
            ia, v = p // 3, p % 3 - 1
            ib = jb - v
            u = ja - ia
            cell = jnp.clip(ia * CY + ib, 0, CX * CY - 1)
            ok = (ib >= 0) & (ib < CY) & (live[cell * 9 + (u + 1) * 3 + v + 1] > 0)

            @pl.when(ok)
            def _():
                pair(acc, mine, scaled, near_rows(block), rates, cell, u.astype(F32), v.astype(F32))

            return carry

        return lax.fori_loop(0, 6, inner, carry)

    lax.fori_loop(0, CX * CY, one, 0)


def outer_kernel(along_x, place, near_list, near_count, rates, filters, own, low, high, start, acc, live, mine, scaled):
    mark_live(place, near_list, near_count, live)
    own_columns(own, mine)
    acc[...] = start[...]
    for side, ref in ((-1, low), (1, high)):

        def one(j, carry, side=side, ref=ref):
            block = ref.at[0, j] if along_x else ref.at[j, 0]
            scaled_features(block, filters, scaled)

            def inner(p, carry):
                t = p - 1
                if along_x:
                    u, v = side, t
                    ia, ib = (0 if side < 0 else CX - 1), j - t
                    inside = (ib >= 0) & (ib < CY)
                else:
                    u, v = t, side
                    ia, ib = j - 1 - t, (0 if side < 0 else CY - 1)
                    inside = (ia >= 0) & (ia < CX)
                cell = jnp.clip(ia * CY + ib, 0, CX * CY - 1)
                ok = inside & (live[cell * 9 + (u + 1) * 3 + v + 1] > 0)

                @pl.when(ok)
                def _():
                    pair(acc, mine, scaled, near_rows(block), rates, cell,
                         jnp.asarray(u, F32), jnp.asarray(v, F32))

                return carry

            return lax.fori_loop(0, 3, inner, carry)

        lax.fori_loop(0, CY, one, 0)


def radial_call(kernel, scalars, arrays, name, pairs, alias):
    vm = pl.BlockSpec(memory_space=VMEM)
    sm = pl.BlockSpec(memory_space=pltpu.SMEM)
    count = len(scalars) + len(arrays)
    return pl.pallas_call(
        kernel,
        out_shape=jax.ShapeDtypeStruct((CX * CY, ATOMS, WIDTH), F32),
        in_specs=[sm] * len(scalars) + [vm] * len(arrays),
        out_specs=vm,
        scratch_shapes=[
            pltpu.SMEM((72,), jnp.int32),
            VMEM((CX * CY, ATOMS, 8), F32),
            VMEM((8 * ATOMS, WIDTH), BF16),
        ],
        input_output_aliases={count - 1: 0} if alias else {},
        compiler_params=pltpu.CompilerParams(vmem_limit_bytes=24 * 1024 * 1024),
        cost_estimate=pl.CostEstimate(flops=pairs * 200_000_000, bytes_accessed=2_000_000, transcendentals=0),
        name=name,
    )(*scalars, *arrays)


def final_kernel(cos_ref, sin_ref, first, second, features, radial, gain, w_in, w_out, out):
    recip = jnp.dot(cos_ref[:, 0:512], first[:, 0:WIDTH], preferred_element_type=F32)
    recip += jnp.dot(sin_ref[:, 0:512], first[:, WIDTH:], preferred_element_type=F32)
    recip += jnp.dot(cos_ref[:, 512:], second[:, 0:WIDTH], preferred_element_type=F32)
    recip += jnp.dot(sin_ref[:, 512:], second[:, WIDTH:], preferred_element_type=F32)
    mixed = features[...].astype(F32) + radial[...] + recip
    power = jnp.mean(mixed * mixed, axis=-1, keepdims=True)
    normed = (mixed * lax.rsqrt(power + epsilon) * gain[...]).astype(BF16)
    v = jnp.dot(normed, w_in[...], preferred_element_type=F32)
    hidden = (v / (1.0 + jnp.exp(-v))).astype(BF16)
    out[...] = (mixed + jnp.dot(hidden, w_out[...], preferred_element_type=F32)).astype(BF16)


def final(cos_table, sin_table, first, second, features, radial, gain, w_in, w_out):
    rows = 256
    whole = pl.BlockSpec(memory_space=VMEM)
    table = pl.BlockSpec((rows, 1024), lambda i: (i, 0))
    block = pl.BlockSpec((rows, WIDTH), lambda i: (i, 0))
    return pl.pallas_call(
        final_kernel,
        grid=(1024 // rows,),
        out_shape=jax.ShapeDtypeStruct((1024, WIDTH), BF16),
        in_specs=[table, table, whole, whole, block, block, whole, whole, whole],
        out_specs=block,
        compiler_params=pltpu.CompilerParams(vmem_limit_bytes=32 * 1024 * 1024),
        cost_estimate=pl.CostEstimate(flops=3_000_000_000, bytes_accessed=8_000_000, transcendentals=0),
        name="mix_and_network",
    )(cos_table, sin_table, first, second, features, radial, gain, w_in, w_out)


def shifted(value, axis, by):
    count = lax.axis_size(axis)
    return lax.ppermute(value, axis, [(i, (i + by) % count) for i in range(count)])


def per_device(
    features,
    coords,
    nbr_cells,
    nbr_count,
    miller,
    gammas,
    radial_filter,
    reciprocal_filter,
    norm_gain,
    w_in,
    w_out,
):
    packed = jnp.concatenate([features, jnp.pad(coords, ((0, 0), (0, 0), (0, 5), (0, 128)))], axis=2)
    low = shifted(packed[1:2], "gx", 1)
    high = shifted(packed[0:1], "gx", -1)

    gx, gy = lax.axis_index("gx"), lax.axis_index("gy")
    place = jnp.stack([gx, gy]).astype(jnp.int32)
    own_rows = features.reshape(1024, WIDTH)
    cos_table, sin_table, send, keep = waves(
        place, coords.reshape(CX * CY, 3, ATOMS), own_rows, miller, vector_order()
    )

    got = permute(send, HALVING[0])
    for step, height in ((1, 256), (2, 128), (3, 64)):
        send = (keep[height:].astype(F32) + got[height:].astype(F32)).astype(BF16)
        fresh = permute(send, HALVING[step])
        keep = keep[:height] + got[:height].astype(F32)
        got = fresh
    x, y, z, core = my_place()
    other = jnp.where(core == 0, y, x)
    member = (other >> 1) * 8 + z
    slots = lax.broadcasted_iota(jnp.int32, (CHUNK, WIDTH), 0) // 4
    filters = jnp.where(slots == member, jnp.tile(reciprocal_filter, (CHUNK // 4, 1)).astype(F32), 0.0)
    total = jnp.concatenate([keep + got.astype(F32), filters], axis=1)
    for step in range(4):
        total = total + permute(total.astype(BF16), DOUBLING[step]).astype(F32)
    scale = total[:, 2 * WIDTH :]
    chunk = jnp.concatenate([total[:, :WIDTH] * scale, total[:, WIDTH : 2 * WIDTH] * scale], axis=1).astype(BF16)
    for step in (3, 2, 1):
        chunk = jnp.concatenate([chunk, permute(chunk, HALVING[step])], axis=0)
    second = permute(chunk, HALVING[0])

    left = shifted(jnp.concatenate([low[:, 3:4], packed[:, 3:4], high[:, 3:4]], axis=0), "gy", 1)
    right = shifted(jnp.concatenate([low[:, 0:1], packed[:, 0:1], high[:, 0:1]], axis=0), "gy", -1)

    scalars = (place, nbr_cells.reshape(72), nbr_count.reshape(8), gammas)
    acc = radial_call(inner_kernel, scalars, (radial_filter, packed), "radial_own", 40, False)
    acc = radial_call(
        functools.partial(outer_kernel, True), scalars, (radial_filter, packed, low, high, acc), "radial_rows", 20, True
    )
    acc = radial_call(
        functools.partial(outer_kernel, False), scalars, (radial_filter, packed, left, right, acc), "radial_columns", 12, True
    )

    out = final(
        cos_table,
        sin_table,
        chunk,
        second,
        own_rows,
        acc.reshape(1024, WIDTH),
        norm_gain.reshape(1, WIDTH),
        w_in,
        w_out,
    )
    return out.reshape(features.shape)


def solution(mesh):
    in_specs = (
        P("gx", "gy", None, None),
        P("gx", "gy", None, None),
        P("gx", "gy", None),
        P("gx", "gy"),
        P(),
        P(),
        P(),
        P(("gx", "gy"), None),
        P(),
        P(),
        P(),
    )
    out_specs = P("gx", "gy", None, None)
    return jax.shard_map(
        per_device, mesh=mesh, in_specs=in_specs, out_specs=out_specs, check_vma=False
    )
```

```python
import functools

import jax
import jax.numpy as jnp
from jax import lax
from jax.experimental import pallas as pl
from jax.experimental.pallas import tpu as pltpu
from jax.sharding import PartitionSpec as P

slab_depth = 2.0
epsilon = 1e-06
LOG2E = 1.4426950408889634
AXES = ("gx", "gy")
F32 = jnp.float32
BF16 = jnp.bfloat16
CX, CY, ATOMS, WIDTH = 2, 4, 128, 256
PACK = 136
VMEM = pltpu.VMEM

SIN_COEF = (3.14159264, -5.16771008, 2.55007752, -0.59829129, 0.07765766)
COS_COEF = (0.99999995, -4.93479283, 4.05841135, -1.33187657, 0.21968961)


def linear(x, y, z, core):
    return (x * 4 + z % 4) * 16 + y * 4 + (z // 4) * 2 + core


def partner_list(step):
    pairs = []
    for x in range(4):
        for y in range(4):
            for z in range(8):
                for core in range(2):
                    pairs.append((linear(x, y, z, core), linear(*step(x, y, z, core))))
    return pairs


def flip_core(x, y, z, core):
    return x, y, z, 1 - core


def flip_plane(first, second):
    def step(x, y, z, core):
        if core == 0:
            return x ^ first, y ^ second, z, core
        return x ^ second, y ^ first, z, core

    return step


def flip_z(which):
    table = ((1, 0, 3, 2, 5, 4, 7, 6), (7, 2, 1, 4, 3, 6, 5, 0), (3, 6, 5, 0, 7, 2, 1, 4))[which]

    def step(x, y, z, core):
        return x, y, table[z], core

    return step


HALVING = (flip_core, flip_plane(1, 0), flip_plane(3, 0), flip_plane(0, 1))
DOUBLING = (flip_plane(0, 3), flip_z(0), flip_z(1), flip_z(2))
CHUNK = 64


def permute(value, step):
    return lax.ppermute(value, AXES, partner_list(step))


def my_place():
    gx, gy = lax.axis_index("gx"), lax.axis_index("gy")
    return gx // 4, gy // 4, (gx % 4) + 4 * ((gy // 2) % 2), gy % 2


def vector_order():
    x, y, z, core = my_place()
    pos = lax.broadcasted_iota(jnp.int32, (1, 1024), 1)
    rest = pos % 4
    mz = (pos // 4) % 8
    mb = (pos // 32) % 2
    b3 = (pos // 64) % 2
    b2 = (pos // 128) % 2
    b1 = (pos // 256) % 2
    owner = core ^ (pos // 512)
    main = jnp.where(owner == 0, x, y) ^ b1 ^ (3 * b2)
    other = jnp.where(owner == 0, y, x)
    coset = (other ^ (other >> 1)) & 1
    side = (coset ^ b3) ^ (3 * mb)
    ox = jnp.where(owner == 0, main, side)
    oy = jnp.where(owner == 0, side, main)
    return linear(ox, oy, mz, owner) * 4 + rest


def wave_kernel(
    place, coords, features, miller, order, cos_out, sin_out, send_ref, keep_ref, turned, cos_ref, sin_ref, sems
):
    number = miller[...].astype(F32)
    five = jnp.concatenate([number, number[0:2], jnp.zeros((3, 1024), F32)], axis=0).astype(BF16)
    natural = lax.broadcasted_iota(jnp.int32, (1024, 1024), 0)
    pick = jnp.where(natural == order[...], 1.0, 0.0).astype(BF16)
    placed = jnp.dot(five, pick, preferred_element_type=F32).astype(BF16)
    turned[...] = features[...].astype(F32).T.astype(BF16)
    ones = jnp.ones((1, ATOMS), F32)
    copies = []

    for cell in range(CX * CY):
        ia, ib = cell // CY, cell % CY
        block = [coords[ia, d, ib : ib + 1, :].astype(F32) for d in range(3)]
        along = (place[0] * CX + cell // CY).astype(F32) / 32.0
        across = (place[1] * CY + cell % CY).astype(F32) / 64.0
        rows = jnp.concatenate(
            [
                block[0] / 32.0,
                block[1] / 64.0,
                block[2] / slab_depth,
                along * ones,
                across * ones,
                jnp.zeros((3, ATOMS), F32),
            ],
            axis=0,
        )
        columns = rows.T.astype(BF16)

        for j in range(4):
            lanes = slice(j * 256, (j + 1) * 256)
            angle = jnp.dot(columns, placed[:, lanes], preferred_element_type=F32)
            r = angle - jnp.round(angle)
            s = r * r
            sine = SIN_COEF[4]
            cosine = COS_COEF[4]
            for a in (3, 2, 1, 0):
                sine = sine * s + SIN_COEF[a]
            for a in (3, 2, 1, 0):
                cosine = cosine * s + COS_COEF[a]
            sine = sine * r
            double = sine + sine
            rows_at = pl.ds(cell * ATOMS, ATOMS)
            cos_ref[rows_at, lanes] = (1.0 - double * sine).astype(BF16)
            sin_ref[rows_at, lanes] = (double * cosine).astype(BF16)
        for i, (source, target) in enumerate(((cos_ref, cos_out), (sin_ref, sin_out))):
            rows_at = pl.ds(cell * ATOMS, ATOMS)
            copy = pltpu.make_async_copy(source.at[rows_at], target.at[rows_at], sems.at[i, cell])
            copy.start()
            copies.append(copy)

    for half, target in ((0, keep_ref), (1, send_ref)):
        lanes = slice(half * 512, half * 512 + 512)
        for col, table in ((0, cos_ref), (1, sin_ref)):
            total = jnp.dot(turned[...], table[:, lanes], preferred_element_type=F32)
            target[:, col * WIDTH : (col + 1) * WIDTH] = total.T.astype(target.dtype)
    for copy in copies:
        copy.wait()


def waves(place, coords, features, miller, order):
    vm = pl.BlockSpec(memory_space=VMEM)
    hbm = pl.BlockSpec(memory_space=pltpu.MemorySpace.HBM)
    return pl.pallas_call(
        wave_kernel,
        out_shape=(
            pltpu.MemorySpace.HBM((1024, 1024), BF16),
            pltpu.MemorySpace.HBM((1024, 1024), BF16),
            jax.ShapeDtypeStruct((512, 512), BF16),
            jax.ShapeDtypeStruct((512, 512), F32),
        ),
        in_specs=[pl.BlockSpec(memory_space=pltpu.SMEM), vm, vm, vm, vm],
        out_specs=(hbm, hbm, vm, vm),
        scratch_shapes=[
            VMEM((WIDTH, 1024), BF16),
            VMEM((1024, 1024), BF16),
            VMEM((1024, 1024), BF16),
            pltpu.SemaphoreType.DMA((2, CX * CY)),
        ],
        compiler_params=pltpu.CompilerParams(vmem_limit_bytes=16 * 1024 * 1024),
        cost_estimate=pl.CostEstimate(flops=4_000_000_000, bytes_accessed=6_000_000, transcendentals=0),
        name="wave_tables",
    )(place, coords, features, miller, order)


def mark_live(place, near_list, near_count, live):
    def clear(i, carry):
        live[i] = 0
        return carry

    lax.fori_loop(0, 72, clear, 0)

    def mark(i, carry):
        cell = i // 9
        entry = near_list[i]
        step_x = ((entry >> 6) - (place[0] * CX + cell // CY) + 1) & 31
        step_y = ((entry & 63) - (place[1] * CY + cell % CY) + 1) & 63

        @pl.when(i % 9 < near_count[cell])
        def _():
            live[cell * 9 + step_x * 3 + step_y] = 1

        return carry

    lax.fori_loop(0, 72, mark, 0)


def prepare_kernel(place, near_list, near_count, coords, live, mine):
    mark_live(place, near_list, near_count, live)
    for cell in range(CX * CY):
        ia, ib = cell // CY, cell % CY
        rows = [coords[ia, d, ib : ib + 1, :].astype(F32) for d in range(3)]
        mine[cell] = jnp.concatenate(rows + [jnp.zeros((5, ATOMS), F32)], axis=0).T


def prepare(place, near_list, near_count, coords):
    vm = pl.BlockSpec(memory_space=VMEM)
    sm = pl.BlockSpec(memory_space=pltpu.SMEM)
    return pl.pallas_call(
        prepare_kernel,
        out_shape=(
            jax.ShapeDtypeStruct((72,), jnp.int32),
            jax.ShapeDtypeStruct((CX * CY, ATOMS, 8), F32),
        ),
        in_specs=[sm, sm, sm, vm],
        out_specs=(sm, vm),
        compiler_params=pltpu.CompilerParams(vmem_limit_bytes=4 * 1024 * 1024),
        cost_estimate=pl.CostEstimate(flops=500_000_000, bytes_accessed=100_000, transcendentals=0),
        name="radial_prepare",
    )(place, near_list, near_count, coords)


def scaled_features(block, filters, scaled):
    values = block[0:ATOMS, :].astype(F32)
    for k in range(8):
        scaled[k * ATOMS : (k + 1) * ATOMS, :] = (values * filters[k : k + 1, :].astype(F32)).astype(BF16)


def pair(acc, mine, scaled, near, rates, cell, u, v):
    here = mine[cell]
    dx = (near[0:1] + u) - here[:, 0:1]
    dy = (near[1:2] + v) - here[:, 1:2]
    dz = near[2:3] - here[:, 2:3]
    dist = dx * dx + dy * dy + dz * dz
    kernel = jnp.concatenate([jnp.exp2(dist * (rates[k] * -LOG2E)).astype(BF16) for k in range(8)], axis=1)
    acc[cell] += jnp.dot(kernel, scaled[...], preferred_element_type=F32)


def near_rows(block):
    return block[ATOMS:PACK, 0:ATOMS].astype(F32)


def inner_kernel(jb, live, rates, filters, mine, own, *rest):
    acc, scaled = rest[-2:]
    acc[...] = jnp.zeros_like(acc) if jb == 0 else rest[0][...]

    def one(ja, carry):
        block = own.at[ja, jb]
        scaled_features(block, filters, scaled)

        def inner(p, carry):
            ia, v = p // 3, p % 3 - 1
            ib = jb - v
            u = ja - ia
            cell = jnp.clip(ia * CY + ib, 0, CX * CY - 1)
            ok = (ib >= 0) & (ib < CY) & (live[cell * 9 + (u + 1) * 3 + v + 1] > 0)

            @pl.when(ok)
            def _():
                pair(acc, mine, scaled, near_rows(block), rates, cell, u.astype(F32), v.astype(F32))

            return carry

        return lax.fori_loop(0, 6, inner, carry)

    lax.fori_loop(0, CX, one, 0)


def outer_kernel(along_x, side, live, rates, filters, mine, edge, start, acc, scaled):
    acc[...] = start[...]

    def one(j, carry):
        block = edge.at[0, j] if along_x else edge.at[j, 0]
        scaled_features(block, filters, scaled)

        def inner(p, carry):
            t = p - 1
            if along_x:
                u, v = side, t
                ia, ib = (0 if side < 0 else CX - 1), j - t
                inside = (ib >= 0) & (ib < CY)
            else:
                u, v = t, side
                ia, ib = j - 1 - t, (0 if side < 0 else CY - 1)
                inside = (ia >= 0) & (ia < CX)
            cell = jnp.clip(ia * CY + ib, 0, CX * CY - 1)
            ok = inside & (live[cell * 9 + (u + 1) * 3 + v + 1] > 0)

            @pl.when(ok)
            def _():
                pair(acc, mine, scaled, near_rows(block), rates, cell, jnp.asarray(u, F32), jnp.asarray(v, F32))

            return carry

        return lax.fori_loop(0, 3, inner, carry)

    lax.fori_loop(0, CY, one, 0)


def radial_call(kernel, scalars, arrays, name, pairs, alias):
    vm = pl.BlockSpec(memory_space=VMEM)
    sm = pl.BlockSpec(memory_space=pltpu.SMEM)
    count = len(scalars) + len(arrays)
    return pl.pallas_call(
        kernel,
        out_shape=jax.ShapeDtypeStruct((CX * CY, ATOMS, WIDTH), F32),
        in_specs=[sm] * len(scalars) + [vm] * len(arrays),
        out_specs=vm,
        scratch_shapes=[VMEM((8 * ATOMS, WIDTH), BF16)],
        input_output_aliases={count - 1: 0} if alias else {},
        compiler_params=pltpu.CompilerParams(vmem_limit_bytes=8 * 1024 * 1024),
        cost_estimate=pl.CostEstimate(flops=pairs * 200_000_000, bytes_accessed=2_000_000, transcendentals=0),
        name=name,
    )(*scalars, *arrays)


def final_kernel(cos_ref, sin_ref, first, second, features, radial, gain, w_in, w_out, out):
    recip = jnp.dot(cos_ref[:, 0:512], first[:, 0:WIDTH], preferred_element_type=F32)
    recip += jnp.dot(sin_ref[:, 0:512], first[:, WIDTH:], preferred_element_type=F32)
    recip += jnp.dot(cos_ref[:, 512:], second[:, 0:WIDTH], preferred_element_type=F32)
    recip += jnp.dot(sin_ref[:, 512:], second[:, WIDTH:], preferred_element_type=F32)
    mixed = features[...].astype(F32) + radial[...] + recip
    power = jnp.mean(mixed * mixed, axis=-1, keepdims=True)
    normed = (mixed * lax.rsqrt(power + epsilon) * gain[...]).astype(BF16)
    v = jnp.dot(normed, w_in[...], preferred_element_type=F32)
    hidden = (v / (1.0 + jnp.exp(-v))).astype(BF16)
    out[...] = (mixed + jnp.dot(hidden, w_out[...], preferred_element_type=F32)).astype(BF16)


def final(cos_table, sin_table, first, second, features, radial, gain, w_in, w_out):
    rows = 256
    whole = pl.BlockSpec(memory_space=VMEM)
    table = pl.BlockSpec((rows, 1024), lambda i: (i, 0))
    block = pl.BlockSpec((rows, WIDTH), lambda i: (i, 0))
    return pl.pallas_call(
        final_kernel,
        grid=(1024 // rows,),
        out_shape=jax.ShapeDtypeStruct((1024, WIDTH), BF16),
        in_specs=[table, table, whole, whole, block, block, whole, whole, whole],
        out_specs=block,
        compiler_params=pltpu.CompilerParams(vmem_limit_bytes=16 * 1024 * 1024),
        cost_estimate=pl.CostEstimate(flops=3_000_000_000, bytes_accessed=8_000_000, transcendentals=0),
        name="mix_and_network",
    )(cos_table, sin_table, first, second, features, radial, gain, w_in, w_out)


def shifted(value, axis, by):
    count = lax.axis_size(axis)
    return lax.ppermute(value, axis, [(i, (i + by) % count) for i in range(count)])


def per_device(
    features,
    coords,
    nbr_cells,
    nbr_count,
    miller,
    gammas,
    radial_filter,
    reciprocal_filter,
    norm_gain,
    w_in,
    w_out,
):
    packed = jnp.concatenate([features, jnp.pad(coords, ((0, 0), (0, 0), (0, 5), (0, 128)))], axis=2)
    low = shifted(packed[1:2], "gx", 1)
    high = shifted(packed[0:1], "gx", -1)

    gx, gy = lax.axis_index("gx"), lax.axis_index("gy")
    place = jnp.stack([gx, gy]).astype(jnp.int32)
    own_rows = features.reshape(1024, WIDTH)
    turned = coords.transpose(0, 2, 1, 3)
    cos_table, sin_table, send, keep = waves(place, turned, own_rows, miller, vector_order())

    scalars, acc = None, None

    def own_piece(jb, acc):
        arrays = (radial_filter, mine, packed) + (() if jb == 0 else (acc,))
        return radial_call(
            functools.partial(inner_kernel, jb), scalars, arrays, "radial_own", 10 if jb in (0, 3) else 12, jb > 0
        )

    def edge_piece(along_x, side, edge, acc):
        return radial_call(
            functools.partial(outer_kernel, along_x, side),
            scalars,
            (radial_filter, mine, edge, acc),
            "radial_edge",
            10 if along_x else 6,
            True,
        )

    send, low, high = lax.optimization_barrier((send, low, high))
    got = permute(send, HALVING[0])
    place, send = lax.optimization_barrier((place, send))
    live, mine = prepare(place, nbr_cells.reshape(72), nbr_count.reshape(8), turned)
    scalars = (live, gammas)
    left = shifted(jnp.concatenate([low[:, 3:4], packed[:, 3:4], high[:, 3:4]], axis=0), "gy", 1)
    right = shifted(jnp.concatenate([low[:, 0:1], packed[:, 0:1], high[:, 0:1]], axis=0), "gy", -1)
    for step, height in ((1, 256), (2, 128), (3, 64)):
        send = (keep[height:].astype(F32) + got[height:].astype(F32)).astype(BF16)
        if step == 1:
            send, mine = lax.optimization_barrier((send, mine))
        else:
            send, acc = lax.optimization_barrier((send, acc))
        fresh = permute(send, HALVING[step])
        acc = own_piece(step - 1, acc)
        keep = keep[:height] + got[:height].astype(F32)
        got = fresh
    x, y, z, core = my_place()
    other = jnp.where(core == 0, y, x)
    member = (other >> 1) * 8 + z
    slots = lax.broadcasted_iota(jnp.int32, (CHUNK, WIDTH), 0) // 4
    filters = jnp.where(slots == member, jnp.tile(reciprocal_filter, (CHUNK // 4, 1)).astype(F32), 0.0)
    total = jnp.concatenate([keep + got.astype(F32), filters], axis=1)
    for step in range(4):
        total, acc = lax.optimization_barrier((total, acc))
        fresh = permute(total.astype(BF16), DOUBLING[step])
        if step == 0:
            acc = own_piece(3, acc)
        elif step == 1:
            acc = edge_piece(True, -1, low, acc)
        elif step == 2:
            acc = edge_piece(True, 1, high, acc)
        else:
            left, right, acc = lax.optimization_barrier((left, right, acc))
            acc = edge_piece(False, -1, left, acc)
        total = total + fresh.astype(F32)
    scale = total[:, 2 * WIDTH :]
    chunk = jnp.concatenate([total[:, :WIDTH] * scale, total[:, WIDTH : 2 * WIDTH] * scale], axis=1).astype(BF16)
    for step in (3, 2, 1):
        chunk, acc = lax.optimization_barrier((chunk, acc))
        fresh = permute(chunk, HALVING[step])
        if step == 3:
            acc = edge_piece(False, 1, right, acc)
        chunk = jnp.concatenate([chunk, fresh], axis=0)
    second = permute(chunk, HALVING[0])

    out = final(
        cos_table,
        sin_table,
        chunk,
        second,
        own_rows,
        acc.reshape(1024, WIDTH),
        norm_gain.reshape(1, WIDTH),
        w_in,
        w_out,
    )
    return out.reshape(features.shape)


def solution(mesh):
    in_specs = (
        P("gx", "gy", None, None),
        P("gx", "gy", None, None),
        P("gx", "gy", None),
        P("gx", "gy"),
        P(),
        P(),
        P(),
        P(("gx", "gy"), None),
        P(),
        P(),
        P(),
    )
    out_specs = P("gx", "gy", None, None)
    return jax.shard_map(
        per_device, mesh=mesh, in_specs=in_specs, out_specs=out_specs, check_vma=False
    )
```

```python
import functools

import jax
import jax.numpy as jnp
from jax import lax
from jax.experimental import pallas as pl
from jax.experimental.pallas import tpu as pltpu
from jax.sharding import PartitionSpec as P

slab_depth = 2.0
epsilon = 1e-06
LOG2E = 1.4426950408889634
AXES = ("gx", "gy")
F32 = jnp.float32
BF16 = jnp.bfloat16
CX, CY, ATOMS, WIDTH = 2, 4, 128, 256
PACK = 144
VMEM = pltpu.VMEM

SIN_COEF = (3.14159264, -5.16771008, 2.55007752, -0.59829129, 0.07765766)
COS_COEF = (0.99999995, -4.93479283, 4.05841135, -1.33187657, 0.21968961)


def linear(x, y, z, core):
    return (x * 4 + z % 4) * 16 + y * 4 + (z // 4) * 2 + core


def partner_list(step):
    pairs = []
    for x in range(4):
        for y in range(4):
            for z in range(8):
                for core in range(2):
                    pairs.append((linear(x, y, z, core), linear(*step(x, y, z, core))))
    return pairs


def flip_core(x, y, z, core):
    return x, y, z, 1 - core


def flip_plane(first, second):
    def step(x, y, z, core):
        if core == 0:
            return x ^ first, y ^ second, z, core
        return x ^ second, y ^ first, z, core

    return step


def flip_z(which):
    table = ((1, 0, 3, 2, 5, 4, 7, 6), (7, 2, 1, 4, 3, 6, 5, 0), (3, 6, 5, 0, 7, 2, 1, 4))[which]

    def step(x, y, z, core):
        return x, y, table[z], core

    return step


HALVING = (flip_core, flip_plane(1, 0), flip_plane(3, 0), flip_plane(0, 1))
DOUBLING = (flip_plane(0, 3), flip_z(0), flip_z(1), flip_z(2))
CHUNK = 64


def permute(value, step):
    return lax.ppermute(value, AXES, partner_list(step))


def my_place():
    gx, gy = lax.axis_index("gx"), lax.axis_index("gy")
    return gx // 4, gy // 4, (gx % 4) + 4 * ((gy // 2) % 2), gy % 2


def vector_order():
    x, y, z, core = my_place()
    pos = lax.broadcasted_iota(jnp.int32, (1, 1024), 1)
    rest = pos % 4
    mz = (pos // 4) % 8
    mb = (pos // 32) % 2
    b3 = (pos // 64) % 2
    b2 = (pos // 128) % 2
    b1 = (pos // 256) % 2
    owner = core ^ (pos // 512)
    main = jnp.where(owner == 0, x, y) ^ b1 ^ (3 * b2)
    other = jnp.where(owner == 0, y, x)
    coset = (other ^ (other >> 1)) & 1
    side = (coset ^ b3) ^ (3 * mb)
    ox = jnp.where(owner == 0, main, side)
    oy = jnp.where(owner == 0, side, main)
    return linear(ox, oy, mz, owner) * 4 + rest


HALF = 512


def wave_kernel(first, place, coords, miller, order, source, cos_out, sin_out, sums, *rest):
    cos_ref, sin_ref, sems = rest[-3:]
    if first:
        turned, packed, features = rest[0], rest[1:3], rest[3]
        load = pltpu.make_async_copy(source, features, sems.at[2, 0])
        load.start()
    else:
        turned = source
    number = miller[...].astype(F32)
    five = jnp.concatenate([number, number[0:2], jnp.zeros((3, 1024), F32)], axis=0).astype(BF16)
    natural = lax.broadcasted_iota(jnp.int32, (1024, HALF), 0)
    pick = jnp.where(natural == order[...], 1.0, 0.0).astype(BF16)
    placed = jnp.dot(five, pick, preferred_element_type=F32).astype(BF16)
    ones = jnp.ones((1, ATOMS), F32)
    copies = []

    for cell in range(CX * CY):
        ia, ib = cell // CY, cell % CY
        block = [coords[ia, d, ib : ib + 1, :].astype(F32) for d in range(3)]
        along = (place[0] * CX + ia).astype(F32) / 32.0
        across = (place[1] * CY + ib).astype(F32) / 64.0
        rows = jnp.concatenate(
            [
                block[0] / 32.0,
                block[1] / 64.0,
                block[2] / slab_depth,
                along * ones,
                across * ones,
                jnp.zeros((3, ATOMS), F32),
            ],
            axis=0,
        )
        columns = rows.T.astype(BF16)
        rows_at = pl.ds(cell * ATOMS, ATOMS)
        for j in range(HALF // 256):
            lanes = slice(j * 256, (j + 1) * 256)
            angle = jnp.dot(columns, placed[:, lanes], preferred_element_type=F32)
            r = angle - jnp.round(angle)
            s = r * r
            sine = SIN_COEF[4]
            cosine = COS_COEF[4]
            for a in (3, 2, 1, 0):
                sine = sine * s + SIN_COEF[a]
            for a in (3, 2, 1, 0):
                cosine = cosine * s + COS_COEF[a]
            sine = sine * r
            double = sine + sine
            cos_ref[rows_at, lanes] = (1.0 - double * sine).astype(BF16)
            sin_ref[rows_at, lanes] = (double * cosine).astype(BF16)
        for i, (source, target) in enumerate(((cos_ref, cos_out), (sin_ref, sin_out))):
            copy = pltpu.make_async_copy(source.at[rows_at], target.at[rows_at], sems.at[i, cell])
            copy.start()
            copies.append(copy)

    if first:
        load.wait()
        turned[...] = features[...].astype(F32).T.astype(BF16)
        for cell in range(CX * CY):
            ia, ib = cell // CY, cell % CY
            packed[ia][ib, 0:ATOMS, :] = features[cell * ATOMS : (cell + 1) * ATOMS, :]
            rows = [coords[ia, d, ib : ib + 1, :].astype(F32) for d in range(3)]
            rows = jnp.concatenate(rows + [jnp.zeros((PACK - ATOMS - 3, ATOMS), F32)], axis=0).astype(BF16)
            packed[ia][ib, ATOMS:PACK, :] = jnp.concatenate([rows, jnp.zeros_like(rows)], axis=1)
    for col, table in ((0, cos_ref), (1, sin_ref)):
        total = jnp.dot(turned[...], table[...], preferred_element_type=F32)
        sums[:, col * WIDTH : (col + 1) * WIDTH] = total.T.astype(sums.dtype)
    for copy in copies:
        copy.wait()


def waves(place, coords, miller, order, source, first):
    vm = pl.BlockSpec(memory_space=VMEM)
    hbm = pl.BlockSpec(memory_space=pl.ANY)
    out_shape = [
        pltpu.MemorySpace.HBM((1024, HALF), BF16),
        pltpu.MemorySpace.HBM((1024, HALF), BF16),
        jax.ShapeDtypeStruct((HALF, 2 * WIDTH), BF16 if first else F32),
    ]
    scratch = [VMEM((1024, HALF), BF16), VMEM((1024, HALF), BF16), pltpu.SemaphoreType.DMA((3, CX * CY))]
    if first:
        source = pltpu.with_memory_space_constraint(source, pltpu.MemorySpace.HBM)
        out_shape.append(jax.ShapeDtypeStruct((WIDTH, 1024), BF16))
        out_shape += [jax.ShapeDtypeStruct((CY, PACK, WIDTH), BF16)] * CX
        scratch.insert(0, VMEM((1024, WIDTH), BF16))
    return pl.pallas_call(
        functools.partial(wave_kernel, first),
        out_shape=out_shape,
        in_specs=[pl.BlockSpec(memory_space=pltpu.SMEM), vm, vm, vm, hbm if first else vm],
        out_specs=[hbm, hbm] + [vm] * (len(out_shape) - 2),
        scratch_shapes=scratch,
        compiler_params=pltpu.CompilerParams(vmem_limit_bytes=14 * 1024 * 1024),
        cost_estimate=pl.CostEstimate(flops=2_000_000_000, bytes_accessed=3_000_000, transcendentals=0),
        name="wave_tables",
    )(place, coords, miller, order, source)


def prepare_kernel(place, near_count, near_list, coords, row_filter, live, mine, filters):
    shape = (CX * CY, 9)
    cell = lax.broadcasted_iota(jnp.int32, shape, 0)
    slot = lax.broadcasted_iota(jnp.int32, shape, 1)
    entry = near_list[...]
    step_x = ((entry >> 6) - (place[0] * CX + cell // CY) + 1) & 31
    step_y = ((entry & 63) - (place[1] * CY + cell % CY) + 1) & 63
    count = jnp.zeros(shape, jnp.int32)
    for c in range(CX * CY):
        count = jnp.where(cell == c, near_count[c], count)
    code = jnp.where(slot < count, step_x * 3 + step_y, -1)
    for o in range(9):
        live[:, o : o + 1] = jnp.max(jnp.where(code == o, 1.0, 0.0), axis=1, keepdims=True)
    for c in range(CX * CY):
        ia, ib = c // CY, c % CY
        rows = [coords[ia, d, ib : ib + 1, :].astype(F32) for d in range(3)]
        columns = jnp.concatenate(rows + [jnp.zeros((5, ATOMS), F32)], axis=0).T
        for d in range(3):
            mine[c, d] = jnp.broadcast_to(columns[:, d : d + 1], (ATOMS, ATOMS))
    x, z = place[0] // 4, place[0] % 4 + 4 * ((place[1] // 2) % 2)
    y, core = place[1] // 4, place[1] % 2
    member = (jnp.where(core == 0, y, x) // 2) * 8 + z
    whole = jnp.concatenate([row_filter[...].astype(F32)] * (CHUNK // 4), axis=0)
    slots = lax.broadcasted_iota(jnp.int32, (CHUNK, WIDTH), 0) // 4
    filters[...] = jnp.where(slots == member, whole, 0.0)


def prepare(place, near_count, near_list, coords, row_filter):
    vm = pl.BlockSpec(memory_space=VMEM)
    sm = pl.BlockSpec(memory_space=pltpu.SMEM)
    return pl.pallas_call(
        prepare_kernel,
        out_shape=(
            jax.ShapeDtypeStruct((CX * CY, 9), F32),
            jax.ShapeDtypeStruct((CX * CY, 3, ATOMS, ATOMS), F32),
            jax.ShapeDtypeStruct((CHUNK, WIDTH), F32),
        ),
        in_specs=[sm, sm, vm, vm, vm],
        out_specs=(vm, vm, vm),
        compiler_params=pltpu.CompilerParams(vmem_limit_bytes=6 * 1024 * 1024),
        cost_estimate=pl.CostEstimate(flops=500_000_000, bytes_accessed=100_000, transcendentals=0),
        name="radial_prepare",
    )(place, near_count, near_list, coords, row_filter)


def radial_kernel(near_cells, fresh, rates, live, filters, mine, *rest):
    acc, scaled = rest[-2:]
    start = rest[-3]
    done = set()
    for i, ((na, nb), (source, at)) in enumerate(near_cells):
        cell_block = rest[source].at[at]
        values = cell_block[0:ATOMS, :]
        for k in range(8):
            scaled[i % 2, k * ATOMS : (k + 1) * ATOMS, :] = values * filters[k : k + 1, :]
        near = cell_block[ATOMS:PACK, 0:ATOMS].astype(F32)
        for ia in range(max(0, na - 1), min(CX, na + 2)):
            for ib in range(max(0, nb - 1), min(CY, nb + 2)):
                u, v = na - ia, nb - ib
                cell = ia * CY + ib
                dx = (near[0:1] + float(u)) - mine[cell, 0]
                dy = (near[1:2] + float(v)) - mine[cell, 1]
                dz = near[2:3] - mine[cell, 2]
                dist = dx * dx + dy * dy + dz * dz
                kernel = jnp.concatenate(
                    [jnp.exp2(dist * (rates[k] * -LOG2E)).astype(BF16) for k in range(8)], axis=1
                )
                o = (u + 1) * 3 + v + 1
                part = jnp.dot(kernel, scaled[i % 2], preferred_element_type=F32) * live[cell : cell + 1, o : o + 1]
                if cell in done:
                    acc[cell] += part
                elif fresh:
                    acc[cell] = part
                else:
                    acc[cell] = start[cell] + part
                done.add(cell)
    for cell in range(CX * CY):
        if cell not in done:
            acc[cell] = jnp.zeros((ATOMS, WIDTH), F32) if fresh else start[cell]


def radial_piece(near_cells, gammas, live, filters, mine, blocks, acc):
    vm = pl.BlockSpec(memory_space=VMEM)
    sm = pl.BlockSpec(memory_space=pltpu.SMEM)
    fresh = acc is None
    arrays = (gammas, live, filters, mine) + blocks + (() if fresh else (acc,))
    return pl.pallas_call(
        functools.partial(radial_kernel, near_cells, fresh),
        out_shape=jax.ShapeDtypeStruct((CX * CY, ATOMS, WIDTH), F32),
        in_specs=[sm] + [vm] * (len(arrays) - 1),
        out_specs=vm,
        scratch_shapes=[VMEM((2, 8 * ATOMS, WIDTH), BF16)],
        input_output_aliases={} if fresh else {len(arrays) - 1: 0},
        compiler_params=pltpu.CompilerParams(vmem_limit_bytes=10 * 1024 * 1024),
        cost_estimate=pl.CostEstimate(flops=2_000_000_000, bytes_accessed=2_000_000, transcendentals=0),
        name="radial_piece",
    )(*arrays)


def recip_kernel(low, high, cos_ref, sin_ref, coef, start, acc):
    lanes = slice(low, high)
    for row in range(4):
        rows = slice(row * 256, row * 256 + 256)
        acc[rows] = (
            start[rows]
            + jnp.dot(cos_ref[rows, lanes], coef[lanes, 0:WIDTH], preferred_element_type=F32)
            + jnp.dot(sin_ref[rows, lanes], coef[lanes, WIDTH:], preferred_element_type=F32)
        )


def recip_piece(low, high, cos_table, sin_table, coef, acc):
    vm = pl.BlockSpec(memory_space=VMEM)
    return pl.pallas_call(
        functools.partial(recip_kernel, low, high),
        out_shape=jax.ShapeDtypeStruct((1024, WIDTH), F32),
        in_specs=[vm] * 4,
        out_specs=vm,
        input_output_aliases={3: 0},
        compiler_params=pltpu.CompilerParams(vmem_limit_bytes=10 * 1024 * 1024),
        cost_estimate=pl.CostEstimate(flops=1_000_000_000, bytes_accessed=2_000_000, transcendentals=0),
        name="recip_piece",
    )(cos_table, sin_table, coef, acc)


def final_kernel(cos_ref, sin_ref, coef, features, acc, gain, w_in, w_out, out):
    rows = pl.ds(pl.multiple_of(pl.program_id(0) * 256, 256), 256)
    recip = jnp.dot(cos_ref[rows, :], coef[:, 0:WIDTH], preferred_element_type=F32)
    recip += jnp.dot(sin_ref[rows, :], coef[:, WIDTH:], preferred_element_type=F32)
    mixed = features[rows, :].astype(F32) + acc[rows, :] + recip
    power = jnp.mean(mixed * mixed, axis=-1, keepdims=True)
    normed = (mixed * lax.rsqrt(power + epsilon) * gain[...]).astype(BF16)
    v = jnp.dot(normed, w_in[...], preferred_element_type=F32)
    hidden = (v / (1.0 + jnp.exp(-v))).astype(BF16)
    out[...] = (mixed + jnp.dot(hidden, w_out[...], preferred_element_type=F32)).astype(BF16)


def final(cos_table, sin_table, coef, features, acc, gain, w_in, w_out):
    whole = pl.BlockSpec(memory_space=VMEM)
    return pl.pallas_call(
        final_kernel,
        grid=(4,),
        out_shape=jax.ShapeDtypeStruct((1024, WIDTH), BF16),
        in_specs=[whole] * 8,
        out_specs=pl.BlockSpec((256, WIDTH), lambda i: (i, 0)),
        compiler_params=pltpu.CompilerParams(vmem_limit_bytes=14 * 1024 * 1024),
        cost_estimate=pl.CostEstimate(flops=3_000_000_000, bytes_accessed=8_000_000, transcendentals=0),
        name="mix_and_network",
    )(cos_table, sin_table, coef, features, acc, gain, w_in, w_out)


def shifted(value, axis, by):
    count = lax.axis_size(axis)
    return lax.ppermute(value, axis, [(i, (i + by) % count) for i in range(count)])


def per_device(
    features,
    coords,
    nbr_cells,
    nbr_count,
    miller,
    gammas,
    radial_filter,
    reciprocal_filter,
    norm_gain,
    w_in,
    w_out,
):
    gx, gy = lax.axis_index("gx"), lax.axis_index("gy")
    place = jnp.stack([gx, gy]).astype(jnp.int32)
    own_rows = features.reshape(1024, WIDTH)
    turned = coords.transpose(0, 2, 1, 3)
    order = vector_order()
    barrier = lax.optimization_barrier

    cos_far, sin_far, send, across, upper, lower = waves(place, turned, miller, order[:, HALF:], own_rows, True)
    got = permute(send, HALVING[0])
    low = shifted(lower, "gx", 1)
    high = shifted(upper, "gx", -1)
    cos_near, sin_near, keep = waves(place, turned, miller, order[:, :HALF], across, False)

    acc = None

    def piece(near_cells, blocks, acc):
        return radial_piece(near_cells, gammas, live, radial_filter, mine, blocks, acc)

    for step, height in ((1, 256), (2, 128), (3, 64)):
        send = (keep[height:].astype(F32) + got[height:].astype(F32)).astype(BF16)
        if step == 2:
            send, live, mine, filters = barrier((send, live, mine, filters))
        elif step == 3:
            send, acc = barrier((send, acc))
        fresh = permute(send, HALVING[step])
        if step == 1:
            place, send = barrier((place, send))
            live, mine, filters = prepare(
                place, nbr_count.reshape(8), nbr_cells.reshape(8, 9), turned, reciprocal_filter
            )
        else:
            jbs = (0, 1) if step == 2 else (2, 3)
            acc = piece(tuple(((ja, jb), (ja, jb)) for jb in jbs for ja in range(CX)), (upper, lower), acc)
        keep = keep[:height] + got[:height].astype(F32)
        got = fresh
    total = jnp.concatenate([keep + got.astype(F32), filters], axis=1)
    for step in range(4):
        total, acc, low, high = barrier((total, acc, low, high))
        fresh = permute(total.astype(BF16), DOUBLING[step])
        if step == 0:
            left = shifted(jnp.concatenate([low[3:4], upper[3:4], lower[3:4], high[3:4]], axis=0), "gy", 1)
            right = shifted(jnp.concatenate([low[0:1], upper[0:1], lower[0:1], high[0:1]], axis=0), "gy", -1)
            acc = piece(tuple(((-1, jb), (0, jb)) for jb in range(CY)), (low,), acc)
        elif step == 1:
            acc = piece(tuple(((CX, jb), (0, jb)) for jb in range(CY)), (high,), acc)
        total = total + fresh.astype(F32)
    scale = total[:, 2 * WIDTH :]
    chunk = jnp.concatenate([total[:, :WIDTH] * scale, total[:, WIDTH : 2 * WIDTH] * scale], axis=1).astype(BF16)
    flat = (1024, WIDTH)
    for step, low_at, high_at in ((3, 0, 0), (2, 0, 128), (1, 128, 256), (0, 256, 512)):
        chunk, acc = barrier((chunk, acc))
        if step == 3:
            chunk, left = barrier((chunk, left))
        elif step == 2:
            chunk, right = barrier((chunk, right))
        fresh = permute(chunk, HALVING[step])
        if step == 3:
            acc = piece(tuple(((ja - 1, -1), (0, ja)) for ja in range(CX + 2)), (left,), acc)
        elif step == 2:
            acc = piece(tuple(((ja - 1, CY), (0, ja)) for ja in range(CX + 2)), (right,), acc)
            acc = acc.reshape(flat)
        if high_at:
            acc = recip_piece(low_at, high_at, cos_near, sin_near, chunk, acc)
        if step:
            chunk = jnp.concatenate([chunk, fresh], axis=0)

    out = final(
        cos_far, sin_far, fresh, own_rows, acc, norm_gain.reshape(1, WIDTH), w_in, w_out
    )
    return out.reshape(CX, CY, ATOMS, WIDTH)


def solution(mesh):
    in_specs = (
        P("gx", "gy", None, None),
        P("gx", "gy", None, None),
        P("gx", "gy", None),
        P("gx", "gy"),
        P(),
        P(),
        P(),
        P(("gx", "gy"), None),
        P(),
        P(),
        P(),
    )
    out_specs = P("gx", "gy", None, None)
    return jax.shard_map(
        per_device, mesh=mesh, in_specs=in_specs, out_specs=out_specs, check_vma=False
    )
```

```python
import functools

import jax
import jax.numpy as jnp
from jax import lax
from jax.experimental import pallas as pl
from jax.experimental.pallas import tpu as pltpu
from jax.sharding import PartitionSpec as P

slab_depth = 2.0
epsilon = 1e-06
LOG2E = 1.4426950408889634
AXES = ("gx", "gy")
F32 = jnp.float32
BF16 = jnp.bfloat16
CX, CY, ATOMS, WIDTH = 2, 4, 128, 256
PACK = 144
VMEM = pltpu.VMEM

SIN_COEF = (3.14159027, -5.16740673, 2.54401052, -0.55946246)
COS_COEF = (0.99999325, -4.93393467, 4.0412481, -1.22203176)


def linear(x, y, z, core):
    return (x * 4 + z % 4) * 16 + y * 4 + (z // 4) * 2 + core


def partner_list(step):
    pairs = []
    for x in range(4):
        for y in range(4):
            for z in range(8):
                for core in range(2):
                    pairs.append((linear(x, y, z, core), linear(*step(x, y, z, core))))
    return pairs


def flip_core(x, y, z, core):
    return x, y, z, 1 - core


def flip_plane(first, second):
    def step(x, y, z, core):
        if core == 0:
            return x ^ first, y ^ second, z, core
        return x ^ second, y ^ first, z, core

    return step


def flip_z(which):
    table = ((1, 0, 3, 2, 5, 4, 7, 6), (7, 2, 1, 4, 3, 6, 5, 0), (3, 6, 5, 0, 7, 2, 1, 4))[which]

    def step(x, y, z, core):
        return x, y, table[z], core

    return step


HALVING = (flip_core, flip_plane(1, 0), flip_plane(3, 0), flip_plane(0, 1))
DOUBLING = (flip_plane(0, 3), flip_z(0), flip_z(1), flip_z(2))
CHUNK = 64


def permute(value, step):
    return lax.ppermute(value, AXES, partner_list(step))


def my_place():
    gx, gy = lax.axis_index("gx"), lax.axis_index("gy")
    return gx // 4, gy // 4, (gx % 4) + 4 * ((gy // 2) % 2), gy % 2


def vector_order():
    x, y, z, core = my_place()
    pos = lax.broadcasted_iota(jnp.int32, (1, 1024), 1)
    rest = pos % 4
    mz = (pos // 4) % 8
    mb = (pos // 32) % 2
    b3 = (pos // 64) % 2
    b2 = (pos // 128) % 2
    b1 = (pos // 256) % 2
    owner = core ^ (pos // 512)
    main = jnp.where(owner == 0, x, y) ^ b1 ^ (3 * b2)
    other = jnp.where(owner == 0, y, x)
    coset = (other ^ (other >> 1)) & 1
    side = (coset ^ b3) ^ (3 * mb)
    ox = jnp.where(owner == 0, main, side)
    oy = jnp.where(owner == 0, side, main)
    return linear(ox, oy, mz, owner) * 4 + rest


HALF = 512


def wave_kernel(first, place, coords, miller, order, source, cos_out, sin_out, sums, *rest):
    cos_ref, sin_ref, sems = rest[-3:]
    if first:
        turned, packed, features = rest[0], rest[1:3], rest[3]
        load = pltpu.make_async_copy(source, features, sems.at[2, 0])
        load.start()
    else:
        turned = source
    number = miller[...].astype(F32)
    five = jnp.concatenate([number, number[0:2], jnp.zeros((3, 1024), F32)], axis=0).astype(BF16)
    natural = lax.broadcasted_iota(jnp.int32, (1024, HALF), 0)
    pick = jnp.where(natural == order[...], 1.0, 0.0).astype(BF16)
    placed = jnp.dot(five, pick, preferred_element_type=F32).astype(BF16)
    ones = jnp.ones((1, ATOMS), F32)
    copies = []

    for cell in range(CX * CY):
        ia, ib = cell // CY, cell % CY
        block = [coords[ia, d, ib : ib + 1, :].astype(F32) for d in range(3)]
        along = (place[0] * CX + ia).astype(F32) / 32.0
        across = (place[1] * CY + ib).astype(F32) / 64.0
        rows = jnp.concatenate(
            [
                block[0] / 32.0,
                block[1] / 64.0,
                block[2] / slab_depth,
                along * ones,
                across * ones,
                jnp.zeros((3, ATOMS), F32),
            ],
            axis=0,
        )
        columns = rows.T.astype(BF16)
        rows_at = pl.ds(cell * ATOMS, ATOMS)
        for j in range(HALF // 256):
            lanes = slice(j * 256, (j + 1) * 256)
            angle = jnp.dot(columns, placed[:, lanes], preferred_element_type=F32)
            r = angle - jnp.round(angle)
            s = r * r
            sine = SIN_COEF[3]
            cosine = COS_COEF[3]
            for a in (2, 1, 0):
                sine = sine * s + SIN_COEF[a]
                cosine = cosine * s + COS_COEF[a]
            sine = sine * r
            double = sine + sine
            cos_ref[rows_at, lanes] = (1.0 - double * sine).astype(BF16)
            sin_ref[rows_at, lanes] = (double * cosine).astype(BF16)
        for i, (source, target) in enumerate(((cos_ref, cos_out), (sin_ref, sin_out))):
            copy = pltpu.make_async_copy(source.at[rows_at], target.at[rows_at], sems.at[i, cell])
            copy.start()
            copies.append(copy)

    if first:
        load.wait()
        turned[...] = features[...].astype(F32).T.astype(BF16)
        for cell in range(CX * CY):
            ia, ib = cell // CY, cell % CY
            packed[ia][ib, 0:ATOMS, :] = features[cell * ATOMS : (cell + 1) * ATOMS, :]
            rows = [coords[ia, d, ib : ib + 1, :].astype(F32) for d in range(3)]
            rows = jnp.concatenate(rows + [jnp.zeros((PACK - ATOMS - 3, ATOMS), F32)], axis=0).astype(BF16)
            packed[ia][ib, ATOMS:PACK, :] = jnp.concatenate([rows, jnp.zeros_like(rows)], axis=1)
    for col, table in ((0, cos_ref), (1, sin_ref)):
        total = jnp.dot(turned[...], table[...], preferred_element_type=F32)
        sums[:, col * WIDTH : (col + 1) * WIDTH] = total.T.astype(sums.dtype)
    for copy in copies:
        copy.wait()


def waves(place, coords, miller, order, source, first):
    vm = pl.BlockSpec(memory_space=VMEM)
    hbm = pl.BlockSpec(memory_space=pl.ANY)
    out_shape = [
        pltpu.MemorySpace.HBM((1024, HALF), BF16),
        pltpu.MemorySpace.HBM((1024, HALF), BF16),
        jax.ShapeDtypeStruct((HALF, 2 * WIDTH), BF16 if first else F32),
    ]
    scratch = [VMEM((1024, HALF), BF16), VMEM((1024, HALF), BF16), pltpu.SemaphoreType.DMA((3, CX * CY))]
    if first:
        source = pltpu.with_memory_space_constraint(source, pltpu.MemorySpace.HBM)
        out_shape.append(jax.ShapeDtypeStruct((WIDTH, 1024), BF16))
        out_shape += [jax.ShapeDtypeStruct((CY, PACK, WIDTH), BF16)] * CX
        scratch.insert(0, VMEM((1024, WIDTH), BF16))
    return pl.pallas_call(
        functools.partial(wave_kernel, first),
        out_shape=out_shape,
        in_specs=[pl.BlockSpec(memory_space=pltpu.SMEM), vm, vm, vm, hbm if first else vm],
        out_specs=[hbm, hbm] + [vm] * (len(out_shape) - 2),
        scratch_shapes=scratch,
        compiler_params=pltpu.CompilerParams(vmem_limit_bytes=14 * 1024 * 1024),
        cost_estimate=pl.CostEstimate(flops=2_000_000_000, bytes_accessed=3_000_000, transcendentals=0),
        name="wave_tables",
    )(place, coords, miller, order, source)


def prepare_kernel(place, near_count, near_list, coords, row_filter, live, mine, filters):
    shape = (CX * CY, 9)
    cell = lax.broadcasted_iota(jnp.int32, shape, 0)
    slot = lax.broadcasted_iota(jnp.int32, shape, 1)
    entry = near_list[...]
    step_x = ((entry >> 6) - (place[0] * CX + cell // CY) + 1) & 31
    step_y = ((entry & 63) - (place[1] * CY + cell % CY) + 1) & 63
    count = jnp.zeros(shape, jnp.int32)
    for c in range(CX * CY):
        count = jnp.where(cell == c, near_count[c], count)
    code = jnp.where(slot < count, step_x * 3 + step_y, -1)
    for o in range(9):
        live[:, o : o + 1] = jnp.max(jnp.where(code == o, 1.0, 0.0), axis=1, keepdims=True)
    for c in range(CX * CY):
        ia, ib = c // CY, c % CY
        rows = [coords[ia, d, ib : ib + 1, :].astype(F32) for d in range(3)]
        columns = jnp.concatenate(rows + [jnp.zeros((5, ATOMS), F32)], axis=0).T
        for d in range(3):
            mine[c, d] = jnp.broadcast_to(columns[:, d : d + 1], (ATOMS, ATOMS))
    x, z = place[0] // 4, place[0] % 4 + 4 * ((place[1] // 2) % 2)
    y, core = place[1] // 4, place[1] % 2
    member = (jnp.where(core == 0, y, x) // 2) * 8 + z
    whole = jnp.concatenate([row_filter[...].astype(F32)] * (CHUNK // 4), axis=0)
    slots = lax.broadcasted_iota(jnp.int32, (CHUNK, WIDTH), 0) // 4
    filters[...] = jnp.where(slots == member, whole, 0.0)


def prepare(place, near_count, near_list, coords, row_filter):
    vm = pl.BlockSpec(memory_space=VMEM)
    sm = pl.BlockSpec(memory_space=pltpu.SMEM)
    return pl.pallas_call(
        prepare_kernel,
        out_shape=(
            jax.ShapeDtypeStruct((CX * CY, 9), F32),
            jax.ShapeDtypeStruct((CX * CY, 3, ATOMS, ATOMS), F32),
            jax.ShapeDtypeStruct((CHUNK, WIDTH), F32),
        ),
        in_specs=[sm, sm, vm, vm, vm],
        out_specs=(vm, vm, vm),
        compiler_params=pltpu.CompilerParams(vmem_limit_bytes=6 * 1024 * 1024),
        cost_estimate=pl.CostEstimate(flops=500_000_000, bytes_accessed=100_000, transcendentals=0),
        name="radial_prepare",
    )(place, near_count, near_list, coords, row_filter)


def radial_kernel(near_cells, fresh, rates, live, filters, mine, *rest):
    acc, scaled = rest[-2:]
    start = rest[-3]
    done = set()
    for i, ((na, nb), (source, at)) in enumerate(near_cells):
        cell_block = rest[source].at[at]
        values = cell_block[0:ATOMS, :]
        for k in range(8):
            scaled[i % 2, k * ATOMS : (k + 1) * ATOMS, :] = values * filters[k : k + 1, :]
        near = cell_block[ATOMS:PACK, 0:ATOMS].astype(F32)
        for ia in range(max(0, na - 1), min(CX, na + 2)):
            for ib in range(max(0, nb - 1), min(CY, nb + 2)):
                u, v = na - ia, nb - ib
                cell = ia * CY + ib
                dx = (near[0:1] + float(u)) - mine[cell, 0]
                dy = (near[1:2] + float(v)) - mine[cell, 1]
                dz = near[2:3] - mine[cell, 2]
                dist = dx * dx + dy * dy + dz * dz
                kernel = jnp.concatenate(
                    [jnp.exp2(dist * (rates[k] * -LOG2E)).astype(BF16) for k in range(8)], axis=1
                )
                o = (u + 1) * 3 + v + 1
                part = jnp.dot(kernel, scaled[i % 2], preferred_element_type=F32) * live[cell : cell + 1, o : o + 1]
                if cell in done:
                    acc[cell] += part
                elif fresh:
                    acc[cell] = part
                else:
                    acc[cell] = start[cell] + part
                done.add(cell)
    for cell in range(CX * CY):
        if cell not in done:
            acc[cell] = jnp.zeros((ATOMS, WIDTH), F32) if fresh else start[cell]


def radial_piece(near_cells, gammas, live, filters, mine, blocks, acc):
    vm = pl.BlockSpec(memory_space=VMEM)
    sm = pl.BlockSpec(memory_space=pltpu.SMEM)
    fresh = acc is None
    arrays = (gammas, live, filters, mine) + blocks + (() if fresh else (acc,))
    return pl.pallas_call(
        functools.partial(radial_kernel, near_cells, fresh),
        out_shape=jax.ShapeDtypeStruct((CX * CY, ATOMS, WIDTH), F32),
        in_specs=[sm] + [vm] * (len(arrays) - 1),
        out_specs=vm,
        scratch_shapes=[VMEM((2, 8 * ATOMS, WIDTH), BF16)],
        input_output_aliases={} if fresh else {len(arrays) - 1: 0},
        compiler_params=pltpu.CompilerParams(vmem_limit_bytes=10 * 1024 * 1024),
        cost_estimate=pl.CostEstimate(flops=2_000_000_000, bytes_accessed=2_000_000, transcendentals=0),
        name="radial_piece",
    )(*arrays)


def recip_kernel(low, high, cos_ref, sin_ref, coef, start, acc):
    lanes = slice(low, high)
    for row in range(4):
        rows = slice(row * 256, row * 256 + 256)
        acc[rows] = (
            start[rows]
            + jnp.dot(cos_ref[rows, lanes], coef[lanes, 0:WIDTH], preferred_element_type=F32)
            + jnp.dot(sin_ref[rows, lanes], coef[lanes, WIDTH:], preferred_element_type=F32)
        )


def recip_piece(low, high, cos_table, sin_table, coef, acc):
    vm = pl.BlockSpec(memory_space=VMEM)
    return pl.pallas_call(
        functools.partial(recip_kernel, low, high),
        out_shape=jax.ShapeDtypeStruct((1024, WIDTH), F32),
        in_specs=[vm] * 4,
        out_specs=vm,
        input_output_aliases={3: 0},
        compiler_params=pltpu.CompilerParams(vmem_limit_bytes=10 * 1024 * 1024),
        cost_estimate=pl.CostEstimate(flops=1_000_000_000, bytes_accessed=2_000_000, transcendentals=0),
        name="recip_piece",
    )(cos_table, sin_table, coef, acc)


def final_kernel(cos_ref, sin_ref, coef, features, acc, gain, w_in, w_out, out, result, sems):
    copies = []
    for block in range(4):
        rows = pl.ds(block * 256, 256)
        recip = jnp.dot(cos_ref[rows, :], coef[:, 0:WIDTH], preferred_element_type=F32)
        recip += jnp.dot(sin_ref[rows, :], coef[:, WIDTH:], preferred_element_type=F32)
        mixed = features[rows, :].astype(F32) + acc[rows, :] + recip
        power = jnp.mean(mixed * mixed, axis=-1, keepdims=True)
        normed = (mixed * lax.rsqrt(power + epsilon) * gain[...]).astype(BF16)
        v = jnp.dot(normed, w_in[...], preferred_element_type=F32)
        hidden = (v / (1.0 + jnp.exp(-v))).astype(BF16)
        result[rows, :] = (mixed + jnp.dot(hidden, w_out[...], preferred_element_type=F32)).astype(BF16)
        copy = pltpu.make_async_copy(result.at[rows], out.at[rows], sems.at[block])
        copy.start()
        copies.append(copy)
    for copy in copies:
        copy.wait()


def final(cos_table, sin_table, coef, features, acc, gain, w_in, w_out):
    whole = pl.BlockSpec(memory_space=VMEM)
    return pl.pallas_call(
        final_kernel,
        out_shape=pltpu.MemorySpace.HBM((1024, WIDTH), BF16),
        in_specs=[whole] * 8,
        out_specs=pl.BlockSpec(memory_space=pl.ANY),
        scratch_shapes=[VMEM((1024, WIDTH), BF16), pltpu.SemaphoreType.DMA((4,))],
        compiler_params=pltpu.CompilerParams(vmem_limit_bytes=14 * 1024 * 1024),
        cost_estimate=pl.CostEstimate(flops=3_000_000_000, bytes_accessed=8_000_000, transcendentals=0),
        name="mix_and_network",
    )(cos_table, sin_table, coef, features, acc, gain, w_in, w_out)


def shifted(value, axis, by):
    count = lax.axis_size(axis)
    return lax.ppermute(value, axis, [(i, (i + by) % count) for i in range(count)])


def per_device(
    features,
    coords,
    nbr_cells,
    nbr_count,
    miller,
    gammas,
    radial_filter,
    reciprocal_filter,
    norm_gain,
    w_in,
    w_out,
):
    gx, gy = lax.axis_index("gx"), lax.axis_index("gy")
    place = jnp.stack([gx, gy]).astype(jnp.int32)
    own_rows = features.reshape(1024, WIDTH)
    turned = coords.transpose(0, 2, 1, 3)
    order = vector_order()
    barrier = lax.optimization_barrier

    cos_far, sin_far, send, across, upper, lower = waves(place, turned, miller, order[:, HALF:], own_rows, True)
    got = permute(send, HALVING[0])
    low = shifted(lower, "gx", 1)
    high = shifted(upper, "gx", -1)
    cos_near, sin_near, keep = waves(place, turned, miller, order[:, :HALF], across, False)

    acc = None

    def piece(near_cells, blocks, acc):
        return radial_piece(near_cells, gammas, live, radial_filter, mine, blocks, acc)

    for step, height in ((1, 256), (2, 128), (3, 64)):
        send = (keep[height:].astype(F32) + got[height:].astype(F32)).astype(BF16)
        if step == 2:
            send, low, high, live, mine, filters = barrier((send, low, high, live, mine, filters))
        elif step == 3:
            send, acc = barrier((send, acc))
        fresh = permute(send, HALVING[step])
        if step == 2:
            left = shifted(jnp.concatenate([low[3:4], upper[3:4], lower[3:4], high[3:4]], axis=0), "gy", 1)
            right = shifted(jnp.concatenate([low[0:1], upper[0:1], lower[0:1], high[0:1]], axis=0), "gy", -1)
        if step == 1:
            place, send = barrier((place, send))
            live, mine, filters = prepare(
                place, nbr_count.reshape(8), nbr_cells.reshape(8, 9), turned, reciprocal_filter
            )
        else:
            jbs = (0, 1) if step == 2 else (2, 3)
            acc = piece(tuple(((ja, jb), (ja, jb)) for jb in jbs for ja in range(CX)), (upper, lower), acc)
        keep = keep[:height] + got[:height].astype(F32)
        got = fresh
    total = jnp.concatenate([keep + got.astype(F32), filters], axis=1)
    for step in range(4):
        total, acc = barrier((total, acc))
        if step == 1:
            total, left, right = barrier((total, left, right))
        fresh = permute(total.astype(BF16), DOUBLING[step])
        if step == 0:
            acc = piece(tuple(((-1, jb), (0, jb)) for jb in range(CY)), (low,), acc)
        elif step == 1:
            acc = piece(tuple(((CX, jb), (0, jb)) for jb in range(CY)), (high,), acc)
        elif step == 2:
            acc = piece(tuple(((ja - 1, -1), (0, ja)) for ja in range(CX + 2)), (left,), acc)
        else:
            acc = piece(tuple(((ja - 1, CY), (0, ja)) for ja in range(CX + 2)), (right,), acc)
        total = total + fresh.astype(F32)
    scale = total[:, 2 * WIDTH :]
    chunk = jnp.concatenate([total[:, :WIDTH] * scale, total[:, WIDTH : 2 * WIDTH] * scale], axis=1).astype(BF16)
    acc = acc.reshape(1024, WIDTH)
    for step, low_at, high_at in ((3, 0, 0), (2, 0, 128), (1, 128, 256), (0, 256, 512)):
        chunk, acc = barrier((chunk, acc))
        fresh = permute(chunk, HALVING[step])
        if high_at:
            acc = recip_piece(low_at, high_at, cos_near, sin_near, chunk, acc)
        if step:
            chunk = jnp.concatenate([chunk, fresh], axis=0)

    out = final(
        cos_far, sin_far, fresh, own_rows, acc, norm_gain.reshape(1, WIDTH), w_in, w_out
    )
    return out.reshape(CX, CY, ATOMS, WIDTH)


def solution(mesh):
    in_specs = (
        P("gx", "gy", None, None),
        P("gx", "gy", None, None),
        P("gx", "gy", None),
        P("gx", "gy"),
        P(),
        P(),
        P(),
        P(("gx", "gy"), None),
        P(),
        P(),
        P(),
    )
    out_specs = P("gx", "gy", None, None)
    return jax.shard_map(
        per_device, mesh=mesh, in_specs=in_specs, out_specs=out_specs, check_vma=False
    )
```

```python
import functools

import jax
import jax.numpy as jnp
from jax import lax
from jax.experimental import pallas as pl
from jax.experimental.pallas import tpu as pltpu
from jax.sharding import PartitionSpec as P

slab_depth = 2.0
epsilon = 1e-06
LOG2E = 1.4426950408889634
AXES = ("gx", "gy")
F32 = jnp.float32
BF16 = jnp.bfloat16
CX, CY, ATOMS, WIDTH = 2, 4, 128, 256
PACK = 144
VMEM = pltpu.VMEM

SIN_COEF = (3.14159027, -5.16740673, 2.54401052, -0.55946246)
COS_COEF = (0.99999325, -4.93393467, 4.0412481, -1.22203176)


def linear(x, y, z, core):
    return (x * 4 + z % 4) * 16 + y * 4 + (z // 4) * 2 + core


def partner_list(step):
    pairs = []
    for x in range(4):
        for y in range(4):
            for z in range(8):
                for core in range(2):
                    pairs.append((linear(x, y, z, core), linear(*step(x, y, z, core))))
    return pairs


def flip_core(x, y, z, core):
    return x, y, z, 1 - core


def flip_plane(first, second):
    def step(x, y, z, core):
        if core == 0:
            return x ^ first, y ^ second, z, core
        return x ^ second, y ^ first, z, core

    return step


def flip_z(which):
    table = ((1, 0, 3, 2, 5, 4, 7, 6), (7, 2, 1, 4, 3, 6, 5, 0), (3, 6, 5, 0, 7, 2, 1, 4))[which]

    def step(x, y, z, core):
        return x, y, table[z] if core == 0 else (table[(z - 1) % 8] + 1) % 8, core

    return step


HALVING = (flip_core, flip_plane(1, 0), flip_plane(3, 0), flip_plane(0, 1))
DOUBLING = (flip_plane(0, 3), flip_z(0), flip_z(1), flip_z(2))
CHUNK = 64


def permute(value, step):
    return lax.ppermute(value, AXES, partner_list(step))


def my_place():
    gx, gy = lax.axis_index("gx"), lax.axis_index("gy")
    return gx // 4, gy // 4, (gx % 4) + 4 * ((gy // 2) % 2), gy % 2


def vector_order():
    x, y, z, core = my_place()
    pos = lax.broadcasted_iota(jnp.int32, (1, 1024), 1)
    rest = pos % 4
    mz = (pos // 4) % 8
    mb = (pos // 32) % 2
    b3 = (pos // 64) % 2
    b2 = (pos // 128) % 2
    b1 = (pos // 256) % 2
    owner = core ^ (pos // 512)
    main = jnp.where(owner == 0, x, y) ^ b1 ^ (3 * b2)
    other = jnp.where(owner == 0, y, x)
    coset = (other ^ (other >> 1)) & 1
    side = (coset ^ b3) ^ (3 * mb)
    ox = jnp.where(owner == 0, main, side)
    oy = jnp.where(owner == 0, side, main)
    return linear(ox, oy, mz, owner) * 4 + rest


HALF = 512


def wave_kernel(first, place, coords, miller, order, source, cos_out, sin_out, sums, *rest):
    cos_ref, sin_ref, sems = rest[-3:]
    if first:
        turned, packed, features = rest[0], rest[1:3], rest[3]
        coords_in, miller_in = coords, miller
        coords, miller = rest[4:6]
        fetch = [
            pltpu.make_async_copy(coords_in, coords, sems.at[2, 1]),
            pltpu.make_async_copy(miller_in, miller, sems.at[2, 2]),
        ]
        load = pltpu.make_async_copy(source, features, sems.at[2, 0])
        for copy in fetch + [load]:
            copy.start()
        for copy in fetch:
            copy.wait()
    else:
        turned = source
    number = miller[...].astype(F32)
    five = jnp.concatenate([number, number[0:2], jnp.zeros((3, 1024), F32)], axis=0).astype(BF16)
    size = order.shape[1]
    natural = lax.broadcasted_iota(jnp.int32, (1024, size), 0)
    pick = jnp.where(natural == order[...], 1.0, 0.0).astype(BF16)
    placed = jnp.dot(five, pick, preferred_element_type=F32).astype(BF16)
    ones = jnp.ones((1, ATOMS), F32)
    copies = []

    for cell in range(CX * CY):
        ia, ib = cell // CY, cell % CY
        block = [coords[ia, d, ib : ib + 1, :].astype(F32) for d in range(3)]
        along = (place[0] * CX + ia).astype(F32) / 32.0
        across = (place[1] * CY + ib).astype(F32) / 64.0
        rows = jnp.concatenate(
            [
                block[0] / 32.0,
                block[1] / 64.0,
                block[2] / slab_depth,
                along * ones,
                across * ones,
                jnp.zeros((3, ATOMS), F32),
            ],
            axis=0,
        )
        columns = rows.T.astype(BF16)
        rows_at = pl.ds(cell * ATOMS, ATOMS)
        for j in range(size // 256):
            lanes = slice(j * 256, (j + 1) * 256)
            angle = jnp.dot(columns, placed[:, lanes], preferred_element_type=F32)
            r = angle - jnp.round(angle)
            s = r * r
            sine = SIN_COEF[3]
            cosine = COS_COEF[3]
            for a in (2, 1, 0):
                sine = sine * s + SIN_COEF[a]
                cosine = cosine * s + COS_COEF[a]
            sine = sine * r
            double = sine + sine
            cos_ref[rows_at, lanes] = (1.0 - double * sine).astype(BF16)
            sin_ref[rows_at, lanes] = (double * cosine).astype(BF16)
        for i, (source, target) in enumerate(((cos_ref, cos_out), (sin_ref, sin_out))):
            copy = pltpu.make_async_copy(source.at[rows_at], target.at[rows_at], sems.at[i, cell])
            copy.start()
            copies.append(copy)

    if first:
        load.wait()
        turned[...] = features[...].astype(F32).T.astype(BF16)
        for cell in range(CX * CY):
            ia, ib = cell // CY, cell % CY
            packed[ia][ib, 0:ATOMS, :] = features[cell * ATOMS : (cell + 1) * ATOMS, :]
            rows = [coords[ia, d, ib : ib + 1, :].astype(F32) for d in range(3)]
            rows = jnp.concatenate(rows + [jnp.zeros((PACK - ATOMS - 3, ATOMS), F32)], axis=0).astype(BF16)
            packed[ia][ib, ATOMS:PACK, :] = jnp.concatenate([rows, jnp.zeros_like(rows)], axis=1)
    for col, table in ((0, cos_ref), (1, sin_ref)):
        total = jnp.dot(turned[...], table[...], preferred_element_type=F32)
        sums[:, col * WIDTH : (col + 1) * WIDTH] = total.T.astype(sums.dtype)
    for copy in copies:
        copy.wait()


def waves(place, coords, miller, order, source, first):
    vm = pl.BlockSpec(memory_space=VMEM)
    hbm = pl.BlockSpec(memory_space=pl.ANY)
    place_of = hbm if first else vm
    size = order.shape[1]
    out_shape = [
        pltpu.MemorySpace.HBM((1024, size), BF16),
        pltpu.MemorySpace.HBM((1024, size), BF16),
        jax.ShapeDtypeStruct((size, 2 * WIDTH), BF16 if first else F32),
    ]
    scratch = [VMEM((1024, size), BF16), VMEM((1024, size), BF16), pltpu.SemaphoreType.DMA((3, CX * CY))]
    if first:
        source, coords, miller = (
            pltpu.with_memory_space_constraint(value, pltpu.MemorySpace.HBM) for value in (source, coords, miller)
        )
        out_shape.append(jax.ShapeDtypeStruct((WIDTH, 1024), BF16))
        out_shape += [jax.ShapeDtypeStruct((CY, PACK, WIDTH), BF16)] * CX
        scratch = [VMEM((1024, WIDTH), BF16), VMEM(coords.shape, BF16), VMEM(miller.shape, jnp.int32)] + scratch
    return pl.pallas_call(
        functools.partial(wave_kernel, first),
        out_shape=out_shape,
        in_specs=[pl.BlockSpec(memory_space=pltpu.SMEM), place_of, place_of, vm, place_of],
        out_specs=[hbm, hbm] + [vm] * (len(out_shape) - 2),
        scratch_shapes=scratch,
        compiler_params=pltpu.CompilerParams(vmem_limit_bytes=14 * 1024 * 1024),
        cost_estimate=pl.CostEstimate(flops=size * 4_000_000, bytes_accessed=3_000_000, transcendentals=0),
        name="wave_tables",
    )(place, coords, miller, order, source)


def prepare_kernel(place, near_count, near_list, coords, row_filter, live, mine, filters):
    shape = (CX * CY, 9)
    cell = lax.broadcasted_iota(jnp.int32, shape, 0)
    slot = lax.broadcasted_iota(jnp.int32, shape, 1)
    entry = near_list[...]
    step_x = ((entry >> 6) - (place[0] * CX + cell // CY) + 1) & 31
    step_y = ((entry & 63) - (place[1] * CY + cell % CY) + 1) & 63
    count = jnp.zeros(shape, jnp.int32)
    for c in range(CX * CY):
        count = jnp.where(cell == c, near_count[c], count)
    code = jnp.where(slot < count, step_x * 3 + step_y, -1)
    for o in range(9):
        live[:, o : o + 1] = jnp.max(jnp.where(code == o, 1.0, 0.0), axis=1, keepdims=True)
    for c in range(CX * CY):
        ia, ib = c // CY, c % CY
        rows = [coords[ia, d, ib : ib + 1, :].astype(F32) for d in range(3)]
        columns = jnp.concatenate(rows + [jnp.zeros((5, ATOMS), F32)], axis=0).T
        for d in range(3):
            mine[c, d] = jnp.broadcast_to(columns[:, d : d + 1], (ATOMS, ATOMS))
    x, z = place[0] // 4, place[0] % 4 + 4 * ((place[1] // 2) % 2)
    y, core = place[1] // 4, place[1] % 2
    member = (jnp.where(core == 0, y, x) // 2) * 8 + z
    whole = jnp.concatenate([row_filter[...].astype(F32)] * (CHUNK // 4), axis=0)
    slots = lax.broadcasted_iota(jnp.int32, (CHUNK, WIDTH), 0) // 4
    filters[...] = jnp.where(slots == member, whole, 0.0)


def prepare(place, near_count, near_list, coords, row_filter):
    vm = pl.BlockSpec(memory_space=VMEM)
    sm = pl.BlockSpec(memory_space=pltpu.SMEM)
    return pl.pallas_call(
        prepare_kernel,
        out_shape=(
            jax.ShapeDtypeStruct((CX * CY, 9), F32),
            jax.ShapeDtypeStruct((CX * CY, 3, ATOMS, ATOMS), F32),
            jax.ShapeDtypeStruct((CHUNK, WIDTH), F32),
        ),
        in_specs=[sm, sm, vm, vm, vm],
        out_specs=(vm, vm, vm),
        compiler_params=pltpu.CompilerParams(vmem_limit_bytes=6 * 1024 * 1024),
        cost_estimate=pl.CostEstimate(flops=500_000_000, bytes_accessed=100_000, transcendentals=0),
        name="radial_prepare",
    )(place, near_count, near_list, coords, row_filter)


def radial_kernel(near_cells, fresh, rates, live, filters, mine, *rest):
    acc, scaled = rest[-2:]
    start = rest[-3]
    done = set()
    for i, ((na, nb), (source, at)) in enumerate(near_cells):
        cell_block = rest[source].at[at]
        values = cell_block[0:ATOMS, :]
        for k in range(8):
            scaled[i % 2, k * ATOMS : (k + 1) * ATOMS, :] = values * filters[k : k + 1, :]
        near = cell_block[ATOMS:PACK, 0:ATOMS].astype(F32)
        for ia in range(max(0, na - 1), min(CX, na + 2)):
            for ib in range(max(0, nb - 1), min(CY, nb + 2)):
                u, v = na - ia, nb - ib
                cell = ia * CY + ib
                dx = (near[0:1] + float(u)) - mine[cell, 0]
                dy = (near[1:2] + float(v)) - mine[cell, 1]
                dz = near[2:3] - mine[cell, 2]
                dist = dx * dx + dy * dy + dz * dz
                kernel = jnp.concatenate(
                    [jnp.exp2(dist * (rates[k] * -LOG2E)).astype(BF16) for k in range(8)], axis=1
                )
                o = (u + 1) * 3 + v + 1
                part = jnp.dot(kernel, scaled[i % 2], preferred_element_type=F32) * live[cell : cell + 1, o : o + 1]
                if cell in done:
                    acc[cell] += part
                elif fresh:
                    acc[cell] = part
                else:
                    acc[cell] = start[cell] + part
                done.add(cell)
    for cell in range(CX * CY):
        if cell not in done:
            acc[cell] = jnp.zeros((ATOMS, WIDTH), F32) if fresh else start[cell]


def radial_piece(near_cells, gammas, live, filters, mine, blocks, acc):
    vm = pl.BlockSpec(memory_space=VMEM)
    sm = pl.BlockSpec(memory_space=pltpu.SMEM)
    fresh = acc is None
    arrays = (gammas, live, filters, mine) + blocks + (() if fresh else (acc,))
    return pl.pallas_call(
        functools.partial(radial_kernel, near_cells, fresh),
        out_shape=jax.ShapeDtypeStruct((CX * CY, ATOMS, WIDTH), F32),
        in_specs=[sm] + [vm] * (len(arrays) - 1),
        out_specs=vm,
        scratch_shapes=[VMEM((2, 8 * ATOMS, WIDTH), BF16)],
        input_output_aliases={} if fresh else {len(arrays) - 1: 0},
        compiler_params=pltpu.CompilerParams(vmem_limit_bytes=10 * 1024 * 1024),
        cost_estimate=pl.CostEstimate(flops=2_000_000_000, bytes_accessed=2_000_000, transcendentals=0),
        name="radial_piece",
    )(*arrays)


def recip_kernel(low, high, cos_ref, sin_ref, coef, start, acc):
    at = slice(low, high)
    lanes = slice(low % 256, (high - 1) % 256 + 1)
    for row in range(4):
        rows = slice(row * 256, row * 256 + 256)
        acc[rows] = (
            start[rows]
            + jnp.dot(cos_ref[rows, lanes], coef[at, 0:WIDTH], preferred_element_type=F32)
            + jnp.dot(sin_ref[rows, lanes], coef[at, WIDTH:], preferred_element_type=F32)
        )


def recip_piece(low, high, cos_table, sin_table, coef, acc):
    vm = pl.BlockSpec(memory_space=VMEM)
    return pl.pallas_call(
        functools.partial(recip_kernel, low, high),
        out_shape=jax.ShapeDtypeStruct((1024, WIDTH), F32),
        in_specs=[vm] * 4,
        out_specs=vm,
        input_output_aliases={3: 0},
        compiler_params=pltpu.CompilerParams(vmem_limit_bytes=10 * 1024 * 1024),
        cost_estimate=pl.CostEstimate(flops=1_000_000_000, bytes_accessed=2_000_000, transcendentals=0),
        name="recip_piece",
    )(cos_table, sin_table, coef, acc)


def final_kernel(cos_ref, sin_ref, coef, features, acc, gain, w_in, w_out, out, result, sems):
    copies = []
    for block in range(4):
        rows = pl.ds(block * 256, 256)
        recip = jnp.dot(cos_ref[rows, :], coef[:, 0:WIDTH], preferred_element_type=F32)
        recip += jnp.dot(sin_ref[rows, :], coef[:, WIDTH:], preferred_element_type=F32)
        mixed = features[rows, :].astype(F32) + acc[rows, :] + recip
        power = jnp.mean(mixed * mixed, axis=-1, keepdims=True)
        normed = (mixed * lax.rsqrt(power + epsilon) * gain[...]).astype(BF16)
        v = jnp.dot(normed, w_in[...], preferred_element_type=F32)
        hidden = (v / (1.0 + jnp.exp(-v))).astype(BF16)
        result[rows, :] = (mixed + jnp.dot(hidden, w_out[...], preferred_element_type=F32)).astype(BF16)
        copy = pltpu.make_async_copy(result.at[rows], out.at[rows], sems.at[block])
        copy.start()
        copies.append(copy)
    for copy in copies:
        copy.wait()


def final(cos_table, sin_table, coef, features, acc, gain, w_in, w_out):
    whole = pl.BlockSpec(memory_space=VMEM)
    return pl.pallas_call(
        final_kernel,
        out_shape=pltpu.MemorySpace.HBM((1024, WIDTH), BF16),
        in_specs=[whole] * 8,
        out_specs=pl.BlockSpec(memory_space=pl.ANY),
        scratch_shapes=[VMEM((1024, WIDTH), BF16), pltpu.SemaphoreType.DMA((4,))],
        compiler_params=pltpu.CompilerParams(vmem_limit_bytes=14 * 1024 * 1024),
        cost_estimate=pl.CostEstimate(flops=3_000_000_000, bytes_accessed=8_000_000, transcendentals=0),
        name="mix_and_network",
    )(cos_table, sin_table, coef, features, acc, gain, w_in, w_out)


def shifted(value, axis, by):
    count = lax.axis_size(axis)
    return lax.ppermute(value, axis, [(i, (i + by) % count) for i in range(count)])


def per_device(
    features,
    coords,
    nbr_cells,
    nbr_count,
    miller,
    gammas,
    radial_filter,
    reciprocal_filter,
    norm_gain,
    w_in,
    w_out,
):
    gx, gy = lax.axis_index("gx"), lax.axis_index("gy")
    place = jnp.stack([gx, gy]).astype(jnp.int32)
    own_rows = features.reshape(1024, WIDTH)
    turned = coords.transpose(0, 2, 1, 3)
    order = vector_order()
    barrier = lax.optimization_barrier

    cos_far, sin_far, send, across, upper, lower = waves(place, turned, miller, order[:, HALF:], own_rows, True)
    got = permute(send, HALVING[0])
    low = shifted(lower, "gx", 1)
    high = shifted(upper, "gx", -1)
    cos_next, sin_next, keep_next = waves(place, turned, miller, order[:, 256:HALF], across, False)

    acc = None

    def piece(near_cells, blocks, acc):
        return radial_piece(near_cells, gammas, live, radial_filter, mine, blocks, acc)

    for step, height in ((1, 256), (2, 128), (3, 64)):
        send = ((keep_next if step == 1 else keep[height:]) + got[height:].astype(F32)).astype(BF16)
        if step == 2:
            send, live, mine, filters = barrier((send, live, mine, filters))
        elif step == 3:
            send, acc, low, high = barrier((send, acc, low, high))
        fresh = permute(send, HALVING[step])
        if step == 3:
            left = shifted(jnp.concatenate([low[3:4], upper[3:4], lower[3:4], high[3:4]], axis=0), "gy", 1)
            right = shifted(jnp.concatenate([low[0:1], upper[0:1], lower[0:1], high[0:1]], axis=0), "gy", -1)
        if step == 1:
            across, place, send = barrier((across, place, send))
            cos_near, sin_near, keep = waves(place, turned, miller, order[:, :256], across, False)
            live, mine, filters = prepare(
                place, nbr_count.reshape(8), nbr_cells.reshape(8, 9), turned, reciprocal_filter
            )
        else:
            jbs = (0, 1) if step == 2 else (2, 3)
            acc = piece(tuple(((ja, jb), (ja, jb)) for jb in jbs for ja in range(CX)), (upper, lower), acc)
        keep = keep[:height] + got[:height].astype(F32)
        got = fresh
    total = jnp.concatenate([keep + got.astype(F32), filters], axis=1)
    for step in range(4):
        total, acc = barrier((total, acc))
        if step == 2:
            total, left, right = barrier((total, left, right))
        fresh = permute(total.astype(BF16), DOUBLING[step])
        if step == 0:
            acc = piece(tuple(((-1, jb), (0, jb)) for jb in range(CY)), (low,), acc)
        elif step == 1:
            acc = piece(tuple(((CX, jb), (0, jb)) for jb in range(CY)), (high,), acc)
        elif step == 2:
            acc = piece(tuple(((ja - 1, -1), (0, ja)) for ja in range(CX + 2)), (left,), acc)
        else:
            acc = piece(tuple(((ja - 1, CY), (0, ja)) for ja in range(CX + 2)), (right,), acc)
        total = total + fresh.astype(F32)
    scale = total[:, 2 * WIDTH :]
    chunk = jnp.concatenate([total[:, :WIDTH] * scale, total[:, WIDTH : 2 * WIDTH] * scale], axis=1).astype(BF16)
    acc = acc.reshape(1024, WIDTH)
    for step, low_at, high_at in ((3, 0, 0), (2, 0, 128), (1, 128, 256), (0, 256, 512)):
        chunk, acc = barrier((chunk, acc))
        fresh = permute(chunk, HALVING[step])
        if high_at:
            tables = (cos_near, sin_near) if high_at <= 256 else (cos_next, sin_next)
            acc = recip_piece(low_at, high_at, *tables, chunk, acc)
        if step:
            chunk = jnp.concatenate([chunk, fresh], axis=0)

    out = final(
        cos_far, sin_far, fresh, own_rows, acc, norm_gain.reshape(1, WIDTH), w_in, w_out
    )
    return out.reshape(CX, CY, ATOMS, WIDTH)


def solution(mesh):
    in_specs = (
        P("gx", "gy", None, None),
        P("gx", "gy", None, None),
        P("gx", "gy", None),
        P("gx", "gy"),
        P(),
        P(),
        P(),
        P(("gx", "gy"), None),
        P(),
        P(),
        P(),
    )
    out_specs = P("gx", "gy", None, None)
    return jax.shard_map(
        per_device, mesh=mesh, in_specs=in_specs, out_specs=out_specs, check_vma=False
    )
```

```python
import functools

import jax
import jax.numpy as jnp
from jax import lax
from jax.experimental import pallas as pl
from jax.experimental.pallas import tpu as pltpu
from jax.sharding import PartitionSpec as P

slab_depth = 2.0
epsilon = 1e-06
LOG2E = 1.4426950408889634
AXES = ("gx", "gy")
F32 = jnp.float32
BF16 = jnp.bfloat16
CX, CY, ATOMS, WIDTH = 2, 4, 128, 256
PACK = 144
VMEM = pltpu.VMEM

SIN_COEF = (3.14159027, -5.16740673, 2.54401052, -0.55946246)
COS_COEF = (0.99999325, -4.93393467, 4.0412481, -1.22203176)


def linear(x, y, z, core):
    return (x * 4 + z % 4) * 16 + y * 4 + (z // 4) * 2 + core


def partner_list(step):
    pairs = []
    for x in range(4):
        for y in range(4):
            for z in range(8):
                for core in range(2):
                    pairs.append((linear(x, y, z, core), linear(*step(x, y, z, core))))
    return pairs


def flip_core(x, y, z, core):
    return x, y, z, 1 - core


def flip_plane(first, second):
    def step(x, y, z, core):
        if core == 0:
            return x ^ first, y ^ second, z, core
        return x ^ second, y ^ first, z, core

    return step


def flip_z(which):
    table = ((1, 0, 3, 2, 5, 4, 7, 6), (7, 2, 1, 4, 3, 6, 5, 0), (3, 6, 5, 0, 7, 2, 1, 4))[which]

    def step(x, y, z, core):
        return x, y, table[z] if core == 0 else (table[(z - 1) % 8] + 1) % 8, core

    return step


HALVING = (flip_core, flip_plane(1, 0), flip_plane(3, 0), flip_plane(0, 1))
DOUBLING = (flip_plane(0, 3), flip_z(0), flip_z(1), flip_z(2))
CHUNK = 64


def permute(value, step):
    return lax.ppermute(value, AXES, partner_list(step))


def my_place():
    gx, gy = lax.axis_index("gx"), lax.axis_index("gy")
    return gx // 4, gy // 4, (gx % 4) + 4 * ((gy // 2) % 2), gy % 2


def vector_order():
    x, y, z, core = my_place()
    pos = lax.broadcasted_iota(jnp.int32, (1, 1024), 1)
    rest = pos % 4
    mz = (pos // 4) % 8
    mb = (pos // 32) % 2
    b3 = (pos // 64) % 2
    b2 = (pos // 128) % 2
    b1 = (pos // 256) % 2
    owner = core ^ (pos // 512)
    main = jnp.where(owner == 0, x, y) ^ b1 ^ (3 * b2)
    other = jnp.where(owner == 0, y, x)
    coset = (other ^ (other >> 1)) & 1
    side = (coset ^ b3) ^ (3 * mb)
    ox = jnp.where(owner == 0, main, side)
    oy = jnp.where(owner == 0, side, main)
    return linear(ox, oy, mz, owner) * 4 + rest


HALF = 512


def wave_kernel(first, place, coords, miller, order, source, cos_out, sin_out, sums, *rest):
    cos_ref, sin_ref, sems = rest[-3:]
    if first:
        turned, packed, features = rest[0], rest[1:3], rest[3]
        coords_in, miller_in = coords, miller
        coords, miller = rest[4:6]
        fetch = [
            pltpu.make_async_copy(coords_in, coords, sems.at[2, 1]),
            pltpu.make_async_copy(miller_in, miller, sems.at[2, 2]),
        ]
        load = pltpu.make_async_copy(source, features, sems.at[2, 0])
        for copy in fetch + [load]:
            copy.start()
        for copy in fetch:
            copy.wait()
    else:
        turned = source
    number = miller[...].astype(F32)
    five = jnp.concatenate([number, number[0:2], jnp.zeros((3, 1024), F32)], axis=0).astype(BF16)
    size = order.shape[1]
    natural = lax.broadcasted_iota(jnp.int32, (1024, size), 0)
    pick = jnp.where(natural == order[...], 1.0, 0.0).astype(BF16)
    placed = jnp.dot(five, pick, preferred_element_type=F32).astype(BF16)
    ones = jnp.ones((1, ATOMS), F32)
    copies = []

    for cell in range(CX * CY):
        ia, ib = cell // CY, cell % CY
        block = [coords[ia, d, ib : ib + 1, :].astype(F32) for d in range(3)]
        along = (place[0] * CX + ia).astype(F32) / 32.0
        across = (place[1] * CY + ib).astype(F32) / 64.0
        rows = jnp.concatenate(
            [
                block[0] / 32.0,
                block[1] / 64.0,
                block[2] / slab_depth,
                along * ones,
                across * ones,
                jnp.zeros((3, ATOMS), F32),
            ],
            axis=0,
        )
        columns = rows.T.astype(BF16)
        rows_at = pl.ds(cell * ATOMS, ATOMS)
        for j in range(size // 256):
            lanes = slice(j * 256, (j + 1) * 256)
            angle = jnp.dot(columns, placed[:, lanes], preferred_element_type=F32)
            r = angle - jnp.round(angle)
            s = r * r
            sine = SIN_COEF[3]
            cosine = COS_COEF[3]
            for a in (2, 1, 0):
                sine = sine * s + SIN_COEF[a]
                cosine = cosine * s + COS_COEF[a]
            sine = sine * r
            double = sine + sine
            cos_ref[rows_at, lanes] = (1.0 - double * sine).astype(BF16)
            sin_ref[rows_at, lanes] = (double * cosine).astype(BF16)
        for i, (source, target) in enumerate(((cos_ref, cos_out), (sin_ref, sin_out))):
            copy = pltpu.make_async_copy(source.at[rows_at], target.at[rows_at], sems.at[i, cell])
            copy.start()
            copies.append(copy)

    if first:
        load.wait()
        turned[...] = features[...].astype(F32).T.astype(BF16)
        for cell in range(CX * CY):
            ia, ib = cell // CY, cell % CY
            packed[ia][ib, 0:ATOMS, :] = features[cell * ATOMS : (cell + 1) * ATOMS, :]
            rows = [coords[ia, d, ib : ib + 1, :].astype(F32) for d in range(3)]
            rows = jnp.concatenate(rows + [jnp.zeros((PACK - ATOMS - 3, ATOMS), F32)], axis=0).astype(BF16)
            packed[ia][ib, ATOMS:PACK, :] = jnp.concatenate([rows, jnp.zeros_like(rows)], axis=1)
    for col, table in ((0, cos_ref), (1, sin_ref)):
        total = jnp.dot(turned[...], table[...], preferred_element_type=F32)
        sums[:, col * WIDTH : (col + 1) * WIDTH] = total.T.astype(sums.dtype)
    for copy in copies:
        copy.wait()


def waves(place, coords, miller, order, source, first):
    vm = pl.BlockSpec(memory_space=VMEM)
    hbm = pl.BlockSpec(memory_space=pl.ANY)
    place_of = hbm if first else vm
    size = order.shape[1]
    out_shape = [
        pltpu.MemorySpace.HBM((1024, size), BF16),
        pltpu.MemorySpace.HBM((1024, size), BF16),
        jax.ShapeDtypeStruct((size, 2 * WIDTH), BF16 if first else F32),
    ]
    scratch = [VMEM((1024, size), BF16), VMEM((1024, size), BF16), pltpu.SemaphoreType.DMA((3, CX * CY))]
    if first:
        source, coords, miller = (
            pltpu.with_memory_space_constraint(value, pltpu.MemorySpace.HBM) for value in (source, coords, miller)
        )
        out_shape.append(jax.ShapeDtypeStruct((WIDTH, 1024), BF16))
        out_shape += [jax.ShapeDtypeStruct((CY, PACK, WIDTH), BF16)] * CX
        scratch = [VMEM((1024, WIDTH), BF16), VMEM(coords.shape, BF16), VMEM(miller.shape, jnp.int32)] + scratch
    return pl.pallas_call(
        functools.partial(wave_kernel, first),
        out_shape=out_shape,
        in_specs=[pl.BlockSpec(memory_space=pltpu.SMEM), place_of, place_of, vm, place_of],
        out_specs=[hbm, hbm] + [vm] * (len(out_shape) - 2),
        scratch_shapes=scratch,
        compiler_params=pltpu.CompilerParams(vmem_limit_bytes=14 * 1024 * 1024),
        cost_estimate=pl.CostEstimate(flops=size * 4_000_000, bytes_accessed=3_000_000, transcendentals=0),
        name="wave_tables",
    )(place, coords, miller, order, source)


def prepare_kernel(place, near_count, near_list, coords, row_filter, live, mine, filters):
    shape = (CX * CY, 9)
    cell = lax.broadcasted_iota(jnp.int32, shape, 0)
    slot = lax.broadcasted_iota(jnp.int32, shape, 1)
    entry = near_list[...]
    step_x = ((entry >> 6) - (place[0] * CX + cell // CY) + 1) & 31
    step_y = ((entry & 63) - (place[1] * CY + cell % CY) + 1) & 63
    count = jnp.zeros(shape, jnp.int32)
    for c in range(CX * CY):
        count = jnp.where(cell == c, near_count[c], count)
    code = jnp.where(slot < count, step_x * 3 + step_y, -1)
    for o in range(9):
        live[:, o : o + 1] = jnp.max(jnp.where(code == o, 1.0, 0.0), axis=1, keepdims=True)
    for c in range(CX * CY):
        ia, ib = c // CY, c % CY
        rows = [coords[ia, d, ib : ib + 1, :].astype(F32) for d in range(3)]
        columns = jnp.concatenate(rows + [jnp.zeros((5, ATOMS), F32)], axis=0).T
        for d in range(3):
            mine[c, d] = jnp.broadcast_to(columns[:, d : d + 1], (ATOMS, ATOMS))
    x, z = place[0] // 4, place[0] % 4 + 4 * ((place[1] // 2) % 2)
    y, core = place[1] // 4, place[1] % 2
    member = (jnp.where(core == 0, y, x) // 2) * 8 + z
    whole = jnp.concatenate([row_filter[...].astype(F32)] * (CHUNK // 4), axis=0)
    slots = lax.broadcasted_iota(jnp.int32, (CHUNK, WIDTH), 0) // 4
    filters[...] = jnp.where(slots == member, whole, 0.0)


def prepare(place, near_count, near_list, coords, row_filter):
    vm = pl.BlockSpec(memory_space=VMEM)
    sm = pl.BlockSpec(memory_space=pltpu.SMEM)
    return pl.pallas_call(
        prepare_kernel,
        out_shape=(
            jax.ShapeDtypeStruct((CX * CY, 9), F32),
            jax.ShapeDtypeStruct((CX * CY, 3, ATOMS, ATOMS), F32),
            jax.ShapeDtypeStruct((CHUNK, WIDTH), F32),
        ),
        in_specs=[sm, sm, vm, vm, vm],
        out_specs=(vm, vm, vm),
        compiler_params=pltpu.CompilerParams(vmem_limit_bytes=6 * 1024 * 1024),
        cost_estimate=pl.CostEstimate(flops=500_000_000, bytes_accessed=100_000, transcendentals=0),
        name="radial_prepare",
    )(place, near_count, near_list, coords, row_filter)


def radial_kernel(near_cells, fresh, rates, live, filters, mine, *rest):
    acc, scaled = rest[-2:]
    start = rest[-3]
    done = set()
    for i, ((na, nb), (source, at)) in enumerate(near_cells):
        cell_block = rest[source].at[at]
        values = cell_block[0:ATOMS, :]
        for k in range(8):
            scaled[i % 2, k * ATOMS : (k + 1) * ATOMS, :] = values * filters[k : k + 1, :]
        near = cell_block[ATOMS:PACK, 0:ATOMS].astype(F32)
        for ia in range(max(0, na - 1), min(CX, na + 2)):
            for ib in range(max(0, nb - 1), min(CY, nb + 2)):
                u, v = na - ia, nb - ib
                cell = ia * CY + ib
                dx = (near[0:1] + float(u)) - mine[cell, 0]
                dy = (near[1:2] + float(v)) - mine[cell, 1]
                dz = near[2:3] - mine[cell, 2]
                dist = dx * dx + dy * dy + dz * dz
                kernel = jnp.concatenate(
                    [jnp.exp2(dist * (rates[k] * -LOG2E)).astype(BF16) for k in range(8)], axis=1
                )
                o = (u + 1) * 3 + v + 1
                part = jnp.dot(kernel, scaled[i % 2], preferred_element_type=F32) * live[cell : cell + 1, o : o + 1]
                if cell in done:
                    acc[cell] += part
                elif fresh:
                    acc[cell] = part
                else:
                    acc[cell] = start[cell] + part
                done.add(cell)
    for cell in range(CX * CY):
        if cell not in done:
            acc[cell] = jnp.zeros((ATOMS, WIDTH), F32) if fresh else start[cell]


def radial_piece(near_cells, gammas, live, filters, mine, blocks, acc):
    vm = pl.BlockSpec(memory_space=VMEM)
    sm = pl.BlockSpec(memory_space=pltpu.SMEM)
    fresh = acc is None
    arrays = (gammas, live, filters, mine) + blocks + (() if fresh else (acc,))
    return pl.pallas_call(
        functools.partial(radial_kernel, near_cells, fresh),
        out_shape=jax.ShapeDtypeStruct((CX * CY, ATOMS, WIDTH), F32),
        in_specs=[sm] + [vm] * (len(arrays) - 1),
        out_specs=vm,
        scratch_shapes=[VMEM((2, 8 * ATOMS, WIDTH), BF16)],
        input_output_aliases={} if fresh else {len(arrays) - 1: 0},
        compiler_params=pltpu.CompilerParams(vmem_limit_bytes=10 * 1024 * 1024),
        cost_estimate=pl.CostEstimate(flops=2_000_000_000, bytes_accessed=2_000_000, transcendentals=0),
        name="radial_piece",
    )(*arrays)


def edge_kernel(along_x, which, sides, rates, live, filters, mine, block, start, acc, scaled):
    low_side = sides[which] < 0
    step = jnp.where(low_side, -1.0, 1.0)
    across = CY if along_x else CX
    totals = [None] * across
    places = []
    for own in range(across):
        at = (own, (CX - 1) * CY + own) if along_x else (own * CY, own * CY + CY - 1)
        places.append((at, jnp.where(low_side, at[0], at[1])))
    for i in range(CY if along_x else CX + 2):
        line = i if along_x else i - 1
        values = block[i, 0:ATOMS, :]
        for k in range(8):
            scaled[i % 2, k * ATOMS : (k + 1) * ATOMS, :] = values * filters[k : k + 1, :]
        near = block[i, ATOMS:PACK, 0:ATOMS].astype(F32)
        for own in range(max(0, line - 1), min(across, line + 2)):
            shift = line - own
            (cell_low, cell_high), cell = places[own]
            u, v = (step, float(shift)) if along_x else (float(shift), step)
            dx = (near[0:1] + u) - mine[cell, 0]
            dy = (near[1:2] + v) - mine[cell, 1]
            dz = near[2:3] - mine[cell, 2]
            dist = dx * dx + dy * dy + dz * dz
            kernel = jnp.concatenate([jnp.exp2(dist * (rates[k] * -LOG2E)).astype(BF16) for k in range(8)], axis=1)
            o_low, o_high = (shift + 1, 7 + shift) if along_x else (3 * shift + 3, 3 * shift + 5)
            weight = jnp.where(
                low_side,
                live[cell_low : cell_low + 1, o_low : o_low + 1],
                live[cell_high : cell_high + 1, o_high : o_high + 1],
            )
            part = jnp.dot(kernel, scaled[i % 2], preferred_element_type=F32) * weight
            totals[own] = part if totals[own] is None else totals[own] + part
            if line == min(across - 1 + (0 if along_x else 1), own + 1):
                acc[cell] = start[cell] + totals[own]
    for cell in range(CX * CY):
        at_low = cell < CY if along_x else cell % CY == 0
        at_high = cell >= CY if along_x else cell % CY == CY - 1
        if along_x:
            keep_it = jnp.logical_not(low_side) if at_low else low_side
        elif at_low:
            keep_it = jnp.logical_not(low_side)
        elif at_high:
            keep_it = low_side
        else:
            keep_it = None

        def keep_cell(cell=cell):
            acc[cell] = start[cell]

        if keep_it is None:
            keep_cell()
        else:
            pl.when(keep_it)(keep_cell)


def edge_piece(along_x, which, sides, gammas, live, filters, mine, block, acc):
    vm = pl.BlockSpec(memory_space=VMEM)
    sm = pl.BlockSpec(memory_space=pltpu.SMEM)
    return pl.pallas_call(
        functools.partial(edge_kernel, along_x, which),
        out_shape=jax.ShapeDtypeStruct((CX * CY, ATOMS, WIDTH), F32),
        in_specs=[sm, sm] + [vm] * 5,
        out_specs=vm,
        scratch_shapes=[VMEM((2, 8 * ATOMS, WIDTH), BF16)],
        input_output_aliases={6: 0},
        compiler_params=pltpu.CompilerParams(vmem_limit_bytes=10 * 1024 * 1024),
        cost_estimate=pl.CostEstimate(flops=2_000_000_000, bytes_accessed=2_000_000, transcendentals=0),
        name="radial_edge",
    )(sides, gammas, live, filters, mine, block, acc)


def recip_kernel(low, high, cos_ref, sin_ref, coef, start, acc):
    at = slice(low, high)
    lanes = slice(low % 256, (high - 1) % 256 + 1)
    for row in range(4):
        rows = slice(row * 256, row * 256 + 256)
        acc[rows] = (
            start[rows]
            + jnp.dot(cos_ref[rows, lanes], coef[at, 0:WIDTH], preferred_element_type=F32)
            + jnp.dot(sin_ref[rows, lanes], coef[at, WIDTH:], preferred_element_type=F32)
        )


def recip_piece(low, high, cos_table, sin_table, coef, acc):
    vm = pl.BlockSpec(memory_space=VMEM)
    return pl.pallas_call(
        functools.partial(recip_kernel, low, high),
        out_shape=jax.ShapeDtypeStruct((1024, WIDTH), F32),
        in_specs=[vm] * 4,
        out_specs=vm,
        input_output_aliases={3: 0},
        compiler_params=pltpu.CompilerParams(vmem_limit_bytes=10 * 1024 * 1024),
        cost_estimate=pl.CostEstimate(flops=1_000_000_000, bytes_accessed=2_000_000, transcendentals=0),
        name="recip_piece",
    )(cos_table, sin_table, coef, acc)


def final_kernel(cos_ref, sin_ref, coef, features, acc, gain, w_in, w_out, out, result, sems):
    copies = []
    for block in range(4):
        rows = pl.ds(block * 256, 256)
        recip = jnp.dot(cos_ref[rows, :], coef[:, 0:WIDTH], preferred_element_type=F32)
        recip += jnp.dot(sin_ref[rows, :], coef[:, WIDTH:], preferred_element_type=F32)
        mixed = features[rows, :].astype(F32) + acc[rows, :] + recip
        power = jnp.mean(mixed * mixed, axis=-1, keepdims=True)
        normed = (mixed * lax.rsqrt(power + epsilon) * gain[...]).astype(BF16)
        v = jnp.dot(normed, w_in[...], preferred_element_type=F32)
        hidden = (v / (1.0 + jnp.exp(-v))).astype(BF16)
        result[rows, :] = (mixed + jnp.dot(hidden, w_out[...], preferred_element_type=F32)).astype(BF16)
        copy = pltpu.make_async_copy(result.at[rows], out.at[rows], sems.at[block])
        copy.start()
        copies.append(copy)
    for copy in copies:
        copy.wait()


def final(cos_table, sin_table, coef, features, acc, gain, w_in, w_out):
    whole = pl.BlockSpec(memory_space=VMEM)
    return pl.pallas_call(
        final_kernel,
        out_shape=pltpu.MemorySpace.HBM((1024, WIDTH), BF16),
        in_specs=[whole] * 8,
        out_specs=pl.BlockSpec(memory_space=pl.ANY),
        scratch_shapes=[VMEM((1024, WIDTH), BF16), pltpu.SemaphoreType.DMA((4,))],
        compiler_params=pltpu.CompilerParams(vmem_limit_bytes=14 * 1024 * 1024),
        cost_estimate=pl.CostEstimate(flops=3_000_000_000, bytes_accessed=8_000_000, transcendentals=0),
        name="mix_and_network",
    )(cos_table, sin_table, coef, features, acc, gain, w_in, w_out)


def row_pairs(first):
    def other(gx):
        return (gx + 1) % 16 if (gx % 2 == 0) == first else (gx - 1) % 16

    return [(i, other(i)) for i in range(16)]


def column_pairs(first):
    return row_pairs(first)


def per_device(
    features,
    coords,
    nbr_cells,
    nbr_count,
    miller,
    gammas,
    radial_filter,
    reciprocal_filter,
    norm_gain,
    w_in,
    w_out,
):
    gx, gy = lax.axis_index("gx"), lax.axis_index("gy")
    place = jnp.stack([gx, gy]).astype(jnp.int32)
    own_rows = features.reshape(1024, WIDTH)
    turned = coords.transpose(0, 2, 1, 3)
    order = vector_order()
    barrier = lax.optimization_barrier

    cos_far, sin_far, send, across, upper, lower = waves(place, turned, miller, order[:, HALF:], own_rows, True)
    got = permute(send, HALVING[0])
    even_x, even_y = gx % 2 == 0, gy % 2 == 0
    sides = jnp.stack(
        [jnp.where(even_x, 1, -1), jnp.where(even_x, -1, 1), jnp.where(even_y, 1, -1), jnp.where(even_y, -1, 1)]
    ).astype(jnp.int32)
    row_a = lax.ppermute(jnp.where(even_x, lower, upper), "gx", row_pairs(True))
    row_b = lax.ppermute(jnp.where(even_x, upper, lower), "gx", row_pairs(False))
    cos_next, sin_next, keep_next = waves(place, turned, miller, order[:, 256:HALF], across, False)

    acc = None

    def own_piece(jb, acc):
        near_cells = tuple(((ja, jb), (ja, jb)) for ja in range(CX))
        return radial_piece(near_cells, gammas, live, radial_filter, mine, (upper, lower), acc)

    def beyond(along_x, which, block, acc):
        return edge_piece(along_x, which, sides, gammas, live, radial_filter, mine, block, acc)

    for step, height in ((1, 256), (2, 128), (3, 64)):
        send = ((keep_next if step == 1 else keep[height:]) + got[height:].astype(F32)).astype(BF16)
        if step == 2:
            send, live, mine, filters = barrier((send, live, mine, filters))
        elif step == 3:
            send, acc = barrier((send, acc))
        fresh = permute(send, HALVING[step])
        if step == 1:
            across, place, send = barrier((across, place, send))
            cos_near, sin_near, keep = waves(place, turned, miller, order[:, :256], across, False)
            live, mine, filters = prepare(
                place, nbr_count.reshape(8), nbr_cells.reshape(8, 9), turned, reciprocal_filter
            )
        else:
            acc = own_piece(step - 2, acc)
        keep = keep[:height] + got[:height].astype(F32)
        got = fresh
    total = jnp.concatenate([keep + got.astype(F32), filters], axis=1)
    for step in range(4):
        total, acc = barrier((total, acc))
        fresh = permute(total.astype(BF16), DOUBLING[step])
        if step < 2:
            acc = own_piece(step + 2, acc)
        else:
            acc = beyond(True, step - 2, row_a if step == 2 else row_b, acc)
        total = total + fresh.astype(F32)
    scale = total[:, 2 * WIDTH :]
    chunk = jnp.concatenate([total[:, :WIDTH] * scale, total[:, WIDTH : 2 * WIDTH] * scale], axis=1).astype(BF16)
    chunk, row_a, row_b = barrier((chunk, row_a, row_b))
    for step, low_at, high_at in ((3, 0, 0), (2, 0, 128), (1, 128, 256), (0, 256, 512)):
        chunk, acc = barrier((chunk, acc))
        fresh = permute(chunk, HALVING[step])
        if step == 3:
            ends = [
                (jnp.where(even_x, row_b[b : b + 1], row_a[b : b + 1]), jnp.where(even_x, row_a[b : b + 1], row_b[b : b + 1]))
                for b in (0, CY - 1)
            ]
            left, right = (
                jnp.concatenate([low, upper[b : b + 1], lower[b : b + 1], high], axis=0)
                for b, (low, high) in zip((0, CY - 1), ends)
            )
            column_b = lax.ppermute(jnp.where(even_y, left, right), "gy", column_pairs(False))
            near_send = jnp.where(even_y, right, left)
        elif step == 2:
            near_send, chunk = barrier((near_send, chunk))
            column_a = lax.ppermute(near_send, "gy", column_pairs(True))
        elif step == 1:
            acc = beyond(False, 2, column_a, acc)
        elif step == 0:
            acc = beyond(False, 3, column_b, acc)
        if high_at:
            tables = (cos_near, sin_near) if high_at <= 256 else (cos_next, sin_next)
            acc = recip_piece(low_at, high_at, *tables, chunk, acc.reshape(1024, WIDTH)).reshape(CX * CY, ATOMS, WIDTH)
        if step:
            chunk = jnp.concatenate([chunk, fresh], axis=0)
    acc = acc.reshape(1024, WIDTH)

    out = final(
        cos_far, sin_far, fresh, own_rows, acc, norm_gain.reshape(1, WIDTH), w_in, w_out
    )
    return out.reshape(CX, CY, ATOMS, WIDTH)


def solution(mesh):
    in_specs = (
        P("gx", "gy", None, None),
        P("gx", "gy", None, None),
        P("gx", "gy", None),
        P("gx", "gy"),
        P(),
        P(),
        P(),
        P(("gx", "gy"), None),
        P(),
        P(),
        P(),
    )
    out_specs = P("gx", "gy", None, None)
    return jax.shard_map(
        per_device, mesh=mesh, in_specs=in_specs, out_specs=out_specs, check_vma=False
    )
```

```python
import functools

import jax
import jax.numpy as jnp
from jax import lax
from jax.experimental import pallas as pl
from jax.experimental.pallas import tpu as pltpu
from jax.sharding import PartitionSpec as P

slab_depth = 2.0
epsilon = 1e-06
LOG2E = 1.4426950408889634
AXES = ("gx", "gy")
F32 = jnp.float32
BF16 = jnp.bfloat16
CX, CY, ATOMS, WIDTH = 2, 4, 128, 256
PACK = 144
VMEM = pltpu.VMEM

SIN_COEF = (3.14159027, -5.16740673, 2.54401052, -0.55946246)
COS_COEF = (0.99999325, -4.93393467, 4.0412481, -1.22203176)


def linear(x, y, z, core):
    return (x * 4 + z % 4) * 16 + y * 4 + (z // 4) * 2 + core


def partner_list(step):
    pairs = []
    for x in range(4):
        for y in range(4):
            for z in range(8):
                for core in range(2):
                    pairs.append((linear(x, y, z, core), linear(*step(x, y, z, core))))
    return pairs


def flip_core(x, y, z, core):
    return x, y, z, 1 - core


def flip_x(first, second):
    def step(x, y, z, core):
        return x ^ (second if core else first), y, z, core

    return step


def flip_y(first, second):
    def step(x, y, z, core):
        return x, y ^ (second if core else first), z, core

    return step


def flip_z(which):
    table = ((1, 0, 3, 2, 5, 4, 7, 6), (7, 2, 1, 4, 3, 6, 5, 0), (3, 6, 5, 0, 7, 2, 1, 4))[which]

    def step(x, y, z, core):
        return x, y, table[z] if core == 0 else (table[(z - 1) % 8] + 1) % 8, core

    return step


HALVING = (flip_core, flip_y(1, 3), flip_y(3, 1), flip_x(1, 3))
DOUBLING = (flip_x(3, 1), flip_z(0), flip_z(1), flip_z(2))
CHUNK = 64


def permute(value, step):
    return lax.ppermute(value, AXES, partner_list(step))


def my_place():
    gx, gy = lax.axis_index("gx"), lax.axis_index("gy")
    return gx // 4, gy // 4, (gx % 4) + 4 * ((gy // 2) % 2), gy % 2


def vector_order():
    x, y, z, core = my_place()
    pos = lax.broadcasted_iota(jnp.int32, (1, 1024), 1)
    rest = pos % 4
    mz = (pos // 4) % 8
    mb = (pos // 32) % 2
    b3 = (pos // 64) % 2
    b2 = (pos // 128) % 2
    b1 = (pos // 256) % 2
    owner = core ^ (pos // 512)
    oy = y ^ jnp.where(owner == 0, b1 ^ (3 * b2), (3 * b1) ^ b2)
    coset = jnp.where(owner == 0, (x ^ (x >> 1)) & 1, x >> 1) ^ b3
    ox = jnp.where(owner == 0, coset ^ (3 * mb), 2 * coset + mb)
    return linear(ox, oy, mz, owner) * 4 + rest


HALF = 512


def wave_kernel(first, place, coords, miller, order, source, cos_out, sin_out, sums, *rest):
    cos_ref, sin_ref, sems = rest[-3:]
    if first:
        turned, packed, features = rest[0], rest[1:3], rest[3]
        coords_in, miller_in = coords, miller
        coords, miller = rest[4:6]
        fetch = [
            pltpu.make_async_copy(coords_in, coords, sems.at[2, 1]),
            pltpu.make_async_copy(miller_in, miller, sems.at[2, 2]),
        ]
        load = pltpu.make_async_copy(source, features, sems.at[2, 0])
        for copy in fetch + [load]:
            copy.start()
        for copy in fetch:
            copy.wait()
    else:
        turned = source
    number = miller[...].astype(F32)
    five = jnp.concatenate([number, number[0:2], jnp.zeros((3, 1024), F32)], axis=0).astype(BF16)
    size = order.shape[1]
    natural = lax.broadcasted_iota(jnp.int32, (1024, size), 0)
    pick = jnp.where(natural == order[...], 1.0, 0.0).astype(BF16)
    placed = jnp.dot(five, pick, preferred_element_type=F32).astype(BF16)
    ones = jnp.ones((1, ATOMS), F32)
    copies = []

    for cell in range(CX * CY):
        ia, ib = cell // CY, cell % CY
        block = [coords[ia, d, ib : ib + 1, :].astype(F32) for d in range(3)]
        along = (place[0] * CX + ia).astype(F32) / 32.0
        across = (place[1] * CY + ib).astype(F32) / 64.0
        rows = jnp.concatenate(
            [
                block[0] / 32.0,
                block[1] / 64.0,
                block[2] / slab_depth,
                along * ones,
                across * ones,
                jnp.zeros((3, ATOMS), F32),
            ],
            axis=0,
        )
        columns = rows.T.astype(BF16)
        rows_at = pl.ds(cell * ATOMS, ATOMS)
        for j in range(size // 256):
            lanes = slice(j * 256, (j + 1) * 256)
            angle = jnp.dot(columns, placed[:, lanes], preferred_element_type=F32)
            r = angle - jnp.round(angle)
            s = r * r
            sine = SIN_COEF[3]
            cosine = COS_COEF[3]
            for a in (2, 1, 0):
                sine = sine * s + SIN_COEF[a]
                cosine = cosine * s + COS_COEF[a]
            sine = sine * r
            double = sine + sine
            cos_ref[rows_at, lanes] = (1.0 - double * sine).astype(BF16)
            sin_ref[rows_at, lanes] = (double * cosine).astype(BF16)
        for i, (source, target) in enumerate(((cos_ref, cos_out), (sin_ref, sin_out))):
            copy = pltpu.make_async_copy(source.at[rows_at], target.at[rows_at], sems.at[i, cell])
            copy.start()
            copies.append(copy)

    if first:
        load.wait()
        turned[...] = features[...].astype(F32).T.astype(BF16)
        for cell in range(CX * CY):
            ia, ib = cell // CY, cell % CY
            packed[ia][ib, 0:ATOMS, :] = features[cell * ATOMS : (cell + 1) * ATOMS, :]
            rows = [coords[ia, d, ib : ib + 1, :].astype(F32) for d in range(3)]
            rows = jnp.concatenate(rows + [jnp.zeros((PACK - ATOMS - 3, ATOMS), F32)], axis=0).astype(BF16)
            packed[ia][ib, ATOMS:PACK, :] = jnp.concatenate([rows, jnp.zeros_like(rows)], axis=1)
    for col, table in ((0, cos_ref), (1, sin_ref)):
        total = jnp.dot(turned[...], table[...], preferred_element_type=F32)
        sums[:, col * WIDTH : (col + 1) * WIDTH] = total.T.astype(sums.dtype)
    for copy in copies:
        copy.wait()


def waves(place, coords, miller, order, source, first):
    vm = pl.BlockSpec(memory_space=VMEM)
    hbm = pl.BlockSpec(memory_space=pl.ANY)
    place_of = hbm if first else vm
    size = order.shape[1]
    out_shape = [
        pltpu.MemorySpace.HBM((1024, size), BF16),
        pltpu.MemorySpace.HBM((1024, size), BF16),
        jax.ShapeDtypeStruct((size, 2 * WIDTH), BF16 if first else F32),
    ]
    scratch = [VMEM((1024, size), BF16), VMEM((1024, size), BF16), pltpu.SemaphoreType.DMA((3, CX * CY))]
    if first:
        source, coords, miller = (
            pltpu.with_memory_space_constraint(value, pltpu.MemorySpace.HBM) for value in (source, coords, miller)
        )
        out_shape.append(jax.ShapeDtypeStruct((WIDTH, 1024), BF16))
        out_shape += [jax.ShapeDtypeStruct((CY, PACK, WIDTH), BF16)] * CX
        scratch = [VMEM((1024, WIDTH), BF16), VMEM(coords.shape, BF16), VMEM(miller.shape, jnp.int32)] + scratch
    return pl.pallas_call(
        functools.partial(wave_kernel, first),
        out_shape=out_shape,
        in_specs=[pl.BlockSpec(memory_space=pltpu.SMEM), place_of, place_of, vm, place_of],
        out_specs=[hbm, hbm] + [vm] * (len(out_shape) - 2),
        scratch_shapes=scratch,
        compiler_params=pltpu.CompilerParams(vmem_limit_bytes=14 * 1024 * 1024),
        cost_estimate=pl.CostEstimate(flops=size * 4_000_000, bytes_accessed=3_000_000, transcendentals=0),
        name="wave_tables",
    )(place, coords, miller, order, source)


def prepare_kernel(place, near_count, near_list, coords, row_filter, live, mine, filters):
    shape = (CX * CY, 9)
    cell = lax.broadcasted_iota(jnp.int32, shape, 0)
    slot = lax.broadcasted_iota(jnp.int32, shape, 1)
    entry = near_list[...]
    step_x = ((entry >> 6) - (place[0] * CX + cell // CY) + 1) & 31
    step_y = ((entry & 63) - (place[1] * CY + cell % CY) + 1) & 63
    count = jnp.zeros(shape, jnp.int32)
    for c in range(CX * CY):
        count = jnp.where(cell == c, near_count[c], count)
    code = jnp.where(slot < count, step_x * 3 + step_y, -1)
    for o in range(9):
        live[:, o : o + 1] = jnp.max(jnp.where(code == o, 1.0, 0.0), axis=1, keepdims=True)
    for c in range(CX * CY):
        ia, ib = c // CY, c % CY
        rows = [coords[ia, d, ib : ib + 1, :].astype(F32) for d in range(3)]
        columns = jnp.concatenate(rows + [jnp.zeros((5, ATOMS), F32)], axis=0).T
        for d in range(3):
            mine[c, d] = jnp.broadcast_to(columns[:, d : d + 1], (ATOMS, ATOMS))
    x, z = place[0] // 4, place[0] % 4 + 4 * ((place[1] // 2) % 2)
    member = jnp.where(place[1] % 2 == 0, x // 2, x % 2) * 8 + z
    whole = jnp.concatenate([row_filter[...].astype(F32)] * (CHUNK // 4), axis=0)
    slots = lax.broadcasted_iota(jnp.int32, (CHUNK, WIDTH), 0) // 4
    filters[...] = jnp.where(slots == member, whole, 0.0)


def prepare(place, near_count, near_list, coords, row_filter):
    vm = pl.BlockSpec(memory_space=VMEM)
    sm = pl.BlockSpec(memory_space=pltpu.SMEM)
    return pl.pallas_call(
        prepare_kernel,
        out_shape=(
            jax.ShapeDtypeStruct((CX * CY, 9), F32),
            jax.ShapeDtypeStruct((CX * CY, 3, ATOMS, ATOMS), F32),
            jax.ShapeDtypeStruct((CHUNK, WIDTH), F32),
        ),
        in_specs=[sm, sm, vm, vm, vm],
        out_specs=(vm, vm, vm),
        compiler_params=pltpu.CompilerParams(vmem_limit_bytes=6 * 1024 * 1024),
        cost_estimate=pl.CostEstimate(flops=500_000_000, bytes_accessed=100_000, transcendentals=0),
        name="radial_prepare",
    )(place, near_count, near_list, coords, row_filter)


def radial_kernel(near_cells, fresh, rates, live, filters, mine, *rest):
    acc, scaled = rest[-2:]
    start = rest[-3]
    done = set()
    for i, ((na, nb), (source, at)) in enumerate(near_cells):
        cell_block = rest[source].at[at]
        values = cell_block[0:ATOMS, :]
        for k in range(8):
            scaled[i % 2, k * ATOMS : (k + 1) * ATOMS, :] = values * filters[k : k + 1, :]
        near = cell_block[ATOMS:PACK, 0:ATOMS].astype(F32)
        for ia in range(max(0, na - 1), min(CX, na + 2)):
            for ib in range(max(0, nb - 1), min(CY, nb + 2)):
                u, v = na - ia, nb - ib
                cell = ia * CY + ib
                dx = (near[0:1] + float(u)) - mine[cell, 0]
                dy = (near[1:2] + float(v)) - mine[cell, 1]
                dz = near[2:3] - mine[cell, 2]
                dist = dx * dx + dy * dy + dz * dz
                kernel = jnp.concatenate(
                    [jnp.exp2(dist * (rates[k] * -LOG2E)).astype(BF16) for k in range(8)], axis=1
                )
                o = (u + 1) * 3 + v + 1
                part = jnp.dot(kernel, scaled[i % 2], preferred_element_type=F32) * live[cell : cell + 1, o : o + 1]
                if cell in done:
                    acc[cell] += part
                elif fresh:
                    acc[cell] = part
                else:
                    acc[cell] = start[cell] + part
                done.add(cell)
    for cell in range(CX * CY):
        if cell not in done:
            acc[cell] = jnp.zeros((ATOMS, WIDTH), F32) if fresh else start[cell]


def radial_piece(near_cells, gammas, live, filters, mine, blocks, acc):
    vm = pl.BlockSpec(memory_space=VMEM)
    sm = pl.BlockSpec(memory_space=pltpu.SMEM)
    fresh = acc is None
    arrays = (gammas, live, filters, mine) + blocks + (() if fresh else (acc,))
    return pl.pallas_call(
        functools.partial(radial_kernel, near_cells, fresh),
        out_shape=jax.ShapeDtypeStruct((CX * CY, ATOMS, WIDTH), F32),
        in_specs=[sm] + [vm] * (len(arrays) - 1),
        out_specs=vm,
        scratch_shapes=[VMEM((2, 8 * ATOMS, WIDTH), BF16)],
        input_output_aliases={} if fresh else {len(arrays) - 1: 0},
        compiler_params=pltpu.CompilerParams(vmem_limit_bytes=10 * 1024 * 1024),
        cost_estimate=pl.CostEstimate(flops=2_000_000_000, bytes_accessed=2_000_000, transcendentals=0),
        name="radial_piece",
    )(*arrays)


def edge_kernel(along_x, which, sides, rates, live, filters, mine, block, start, acc, scaled):
    low_side = sides[which] < 0
    step = jnp.where(low_side, -1.0, 1.0)
    across = CY if along_x else CX
    totals = [None] * across
    places = []
    for own in range(across):
        at = (own, (CX - 1) * CY + own) if along_x else (own * CY, own * CY + CY - 1)
        places.append((at, jnp.where(low_side, at[0], at[1])))
    for i in range(CY if along_x else CX + 2):
        line = i if along_x else i - 1
        values = block[i, 0:ATOMS, :]
        for k in range(8):
            scaled[i % 2, k * ATOMS : (k + 1) * ATOMS, :] = values * filters[k : k + 1, :]
        near = block[i, ATOMS:PACK, 0:ATOMS].astype(F32)
        for own in range(max(0, line - 1), min(across, line + 2)):
            shift = line - own
            (cell_low, cell_high), cell = places[own]
            u, v = (step, float(shift)) if along_x else (float(shift), step)
            dx = (near[0:1] + u) - mine[cell, 0]
            dy = (near[1:2] + v) - mine[cell, 1]
            dz = near[2:3] - mine[cell, 2]
            dist = dx * dx + dy * dy + dz * dz
            kernel = jnp.concatenate([jnp.exp2(dist * (rates[k] * -LOG2E)).astype(BF16) for k in range(8)], axis=1)
            o_low, o_high = (shift + 1, 7 + shift) if along_x else (3 * shift + 3, 3 * shift + 5)
            weight = jnp.where(
                low_side,
                live[cell_low : cell_low + 1, o_low : o_low + 1],
                live[cell_high : cell_high + 1, o_high : o_high + 1],
            )
            part = jnp.dot(kernel, scaled[i % 2], preferred_element_type=F32) * weight
            totals[own] = part if totals[own] is None else totals[own] + part
            if line == min(across - 1 + (0 if along_x else 1), own + 1):
                acc[cell] = start[cell] + totals[own]
    for cell in range(CX * CY):
        at_low = cell < CY if along_x else cell % CY == 0
        at_high = cell >= CY if along_x else cell % CY == CY - 1
        if along_x:
            keep_it = jnp.logical_not(low_side) if at_low else low_side
        elif at_low:
            keep_it = jnp.logical_not(low_side)
        elif at_high:
            keep_it = low_side
        else:
            keep_it = None

        def keep_cell(cell=cell):
            acc[cell] = start[cell]

        if keep_it is None:
            keep_cell()
        else:
            pl.when(keep_it)(keep_cell)


def edge_piece(along_x, which, sides, gammas, live, filters, mine, block, acc):
    vm = pl.BlockSpec(memory_space=VMEM)
    sm = pl.BlockSpec(memory_space=pltpu.SMEM)
    return pl.pallas_call(
        functools.partial(edge_kernel, along_x, which),
        out_shape=jax.ShapeDtypeStruct((CX * CY, ATOMS, WIDTH), F32),
        in_specs=[sm, sm] + [vm] * 5,
        out_specs=vm,
        scratch_shapes=[VMEM((2, 8 * ATOMS, WIDTH), BF16)],
        input_output_aliases={6: 0},
        compiler_params=pltpu.CompilerParams(vmem_limit_bytes=10 * 1024 * 1024),
        cost_estimate=pl.CostEstimate(flops=2_000_000_000, bytes_accessed=2_000_000, transcendentals=0),
        name="radial_edge",
    )(sides, gammas, live, filters, mine, block, acc)


def recip_kernel(low, high, cos_ref, sin_ref, coef, start, acc):
    at = slice(low, high)
    lanes = slice(low % 256, (high - 1) % 256 + 1)
    for row in range(4):
        rows = slice(row * 256, row * 256 + 256)
        acc[rows] = (
            start[rows]
            + jnp.dot(cos_ref[rows, lanes], coef[at, 0:WIDTH], preferred_element_type=F32)
            + jnp.dot(sin_ref[rows, lanes], coef[at, WIDTH:], preferred_element_type=F32)
        )


def recip_piece(low, high, cos_table, sin_table, coef, acc):
    vm = pl.BlockSpec(memory_space=VMEM)
    return pl.pallas_call(
        functools.partial(recip_kernel, low, high),
        out_shape=jax.ShapeDtypeStruct((1024, WIDTH), F32),
        in_specs=[vm] * 4,
        out_specs=vm,
        input_output_aliases={3: 0},
        compiler_params=pltpu.CompilerParams(vmem_limit_bytes=10 * 1024 * 1024),
        cost_estimate=pl.CostEstimate(flops=1_000_000_000, bytes_accessed=2_000_000, transcendentals=0),
        name="recip_piece",
    )(cos_table, sin_table, coef, acc)


def final_kernel(cos_ref, sin_ref, coef, features, acc, gain, w_in, w_out, out, result, sems):
    copies = []
    for block in range(4):
        rows = pl.ds(block * 256, 256)
        recip = jnp.dot(cos_ref[rows, :], coef[:, 0:WIDTH], preferred_element_type=F32)
        recip += jnp.dot(sin_ref[rows, :], coef[:, WIDTH:], preferred_element_type=F32)
        mixed = features[rows, :].astype(F32) + acc[rows, :] + recip
        power = jnp.mean(mixed * mixed, axis=-1, keepdims=True)
        normed = (mixed * lax.rsqrt(power + epsilon) * gain[...]).astype(BF16)
        v = jnp.dot(normed, w_in[...], preferred_element_type=F32)
        hidden = (v / (1.0 + jnp.exp(-v))).astype(BF16)
        result[rows, :] = (mixed + jnp.dot(hidden, w_out[...], preferred_element_type=F32)).astype(BF16)
        copy = pltpu.make_async_copy(result.at[rows], out.at[rows], sems.at[block])
        copy.start()
        copies.append(copy)
    for copy in copies:
        copy.wait()


def final(cos_table, sin_table, coef, features, acc, gain, w_in, w_out):
    whole = pl.BlockSpec(memory_space=VMEM)
    return pl.pallas_call(
        final_kernel,
        out_shape=pltpu.MemorySpace.HBM((1024, WIDTH), BF16),
        in_specs=[whole] * 8,
        out_specs=pl.BlockSpec(memory_space=pl.ANY),
        scratch_shapes=[VMEM((1024, WIDTH), BF16), pltpu.SemaphoreType.DMA((4,))],
        compiler_params=pltpu.CompilerParams(vmem_limit_bytes=14 * 1024 * 1024),
        cost_estimate=pl.CostEstimate(flops=3_000_000_000, bytes_accessed=8_000_000, transcendentals=0),
        name="mix_and_network",
    )(cos_table, sin_table, coef, features, acc, gain, w_in, w_out)


def row_pairs(first):
    def other(gx):
        return (gx + 1) % 16 if (gx % 2 == 0) == first else (gx - 1) % 16

    return [(i, other(i)) for i in range(16)]


def column_pairs(first):
    return row_pairs(first)


def per_device(
    features,
    coords,
    nbr_cells,
    nbr_count,
    miller,
    gammas,
    radial_filter,
    reciprocal_filter,
    norm_gain,
    w_in,
    w_out,
):
    gx, gy = lax.axis_index("gx"), lax.axis_index("gy")
    place = jnp.stack([gx, gy]).astype(jnp.int32)
    own_rows = features.reshape(1024, WIDTH)
    turned = coords.transpose(0, 2, 1, 3)
    order = vector_order()
    barrier = lax.optimization_barrier

    cos_far, sin_far, send, across, upper, lower = waves(place, turned, miller, order[:, HALF:], own_rows, True)
    got = permute(send, HALVING[0])
    even_x, even_y = gx % 2 == 0, gy % 2 == 0
    sides = jnp.stack(
        [jnp.where(even_x, 1, -1), jnp.where(even_x, -1, 1), jnp.where(even_y, 1, -1), jnp.where(even_y, -1, 1)]
    ).astype(jnp.int32)
    row_a = lax.ppermute(jnp.where(even_x, lower, upper), "gx", row_pairs(True))
    row_b = lax.ppermute(jnp.where(even_x, upper, lower), "gx", row_pairs(False))
    cos_next, sin_next, keep_next = waves(place, turned, miller, order[:, 256:HALF], across, False)

    acc = None

    def own_piece(jb, acc):
        near_cells = tuple(((ja, jb), (ja, jb)) for ja in range(CX))
        return radial_piece(near_cells, gammas, live, radial_filter, mine, (upper, lower), acc)

    def beyond(along_x, which, block, acc):
        return edge_piece(along_x, which, sides, gammas, live, radial_filter, mine, block, acc)

    for step, height in ((1, 256), (2, 128), (3, 64)):
        send = ((keep_next if step == 1 else keep[height:]) + got[height:].astype(F32)).astype(BF16)
        if step == 2:
            send, live, mine, filters = barrier((send, live, mine, filters))
        elif step == 3:
            send, acc, row_a, row_b = barrier((send, acc, row_a, row_b))
        fresh = permute(send, HALVING[step])
        if step == 3:
            ends = [
                (jnp.where(even_x, row_b[b : b + 1], row_a[b : b + 1]), jnp.where(even_x, row_a[b : b + 1], row_b[b : b + 1]))
                for b in (0, CY - 1)
            ]
            left, right = (
                jnp.concatenate([low, upper[b : b + 1], lower[b : b + 1], high], axis=0)
                for b, (low, high) in zip((0, CY - 1), ends)
            )
            far_send, near_send = jnp.where(even_y, left, right), jnp.where(even_y, right, left)
            far_send, near_send, acc = barrier((far_send, near_send, acc))
            column_b = lax.ppermute(far_send, "gy", column_pairs(False))
            column_a = lax.ppermute(near_send, "gy", column_pairs(True))
        if step == 1:
            across, place, send = barrier((across, place, send))
            cos_near, sin_near, keep = waves(place, turned, miller, order[:, :256], across, False)
            live, mine, filters = prepare(
                place, nbr_count.reshape(8), nbr_cells.reshape(8, 9), turned, reciprocal_filter
            )
        else:
            acc = own_piece(step - 2, acc)
        keep = keep[:height] + got[:height].astype(F32)
        got = fresh
    total = jnp.concatenate([keep + got.astype(F32), filters], axis=1)
    for step in range(4):
        total, acc = barrier((total, acc))
        if step == 1:
            total, column_a, column_b = barrier((total, column_a, column_b))
        fresh = permute(total.astype(BF16), DOUBLING[step])
        if step < 2:
            acc = own_piece(step + 2, acc)
        else:
            acc = beyond(True, step - 2, row_a if step == 2 else row_b, acc)
        total = total + fresh.astype(F32)
    scale = total[:, 2 * WIDTH :]
    chunk = jnp.concatenate([total[:, :WIDTH] * scale, total[:, WIDTH : 2 * WIDTH] * scale], axis=1).astype(BF16)
    for step, low_at, high_at in ((3, 0, 0), (2, 0, 128), (1, 128, 256), (0, 256, 512)):
        chunk, acc = barrier((chunk, acc))
        fresh = permute(chunk, HALVING[step])
        if step == 1:
            acc = beyond(False, 2, column_a, acc)
        elif step == 0:
            acc = beyond(False, 3, column_b, acc)
        if high_at:
            tables = (cos_near, sin_near) if high_at <= 256 else (cos_next, sin_next)
            acc = recip_piece(low_at, high_at, *tables, chunk, acc.reshape(1024, WIDTH)).reshape(CX * CY, ATOMS, WIDTH)
        if step:
            chunk = jnp.concatenate([chunk, fresh], axis=0)
    acc = acc.reshape(1024, WIDTH)

    out = final(
        cos_far, sin_far, fresh, own_rows, acc, norm_gain.reshape(1, WIDTH), w_in, w_out
    )
    return out.reshape(CX, CY, ATOMS, WIDTH)


def solution(mesh):
    in_specs = (
        P("gx", "gy", None, None),
        P("gx", "gy", None, None),
        P("gx", "gy", None),
        P("gx", "gy"),
        P(),
        P(),
        P(),
        P(("gx", "gy"), None),
        P(),
        P(),
        P(),
    )
    out_specs = P("gx", "gy", None, None)
    return jax.shard_map(
        per_device, mesh=mesh, in_specs=in_specs, out_specs=out_specs, check_vma=False
    )
```

```python
import functools

import jax
import jax.numpy as jnp
from jax import lax
from jax.experimental import pallas as pl
from jax.experimental.pallas import tpu as pltpu
from jax.sharding import PartitionSpec as P

slab_depth = 2.0
epsilon = 1e-06
LOG2E = 1.4426950408889634
AXES = ("gx", "gy")
F32 = jnp.float32
BF16 = jnp.bfloat16
CX, CY, ATOMS, WIDTH = 2, 4, 128, 256
PACK = 144
VMEM = pltpu.VMEM

SIN_COEF = (3.14159027, -5.16740673, 2.54401052, -0.55946246)
COS_COEF = (0.99999325, -4.93393467, 4.0412481, -1.22203176)


def linear(x, y, z, core):
    return (x * 4 + z % 4) * 16 + y * 4 + (z // 4) * 2 + core


def partner_list(step):
    pairs = []
    for x in range(4):
        for y in range(4):
            for z in range(8):
                for core in range(2):
                    pairs.append((linear(x, y, z, core), linear(*step(x, y, z, core))))
    return pairs


def flip_core(x, y, z, core):
    return x, y, z, 1 - core


def flip_x(first, second):
    def step(x, y, z, core):
        return x ^ (second if core else first), y, z, core

    return step


def flip_y(first, second):
    def step(x, y, z, core):
        return x, y ^ (second if core else first), z, core

    return step


def flip_z(which):
    table = ((1, 0, 3, 2, 5, 4, 7, 6), (7, 2, 1, 4, 3, 6, 5, 0), (3, 6, 5, 0, 7, 2, 1, 4))[which]

    def step(x, y, z, core):
        return x, y, table[z] if core == 0 else (table[(z - 1) % 8] + 1) % 8, core

    return step


HALVING = (flip_core, flip_y(1, 3), flip_y(3, 1), flip_x(1, 3))
DOUBLING = (flip_x(3, 1), flip_z(0), flip_z(1), flip_z(2))
CHUNK = 64


def permute(value, step):
    return lax.ppermute(value, AXES, partner_list(step))


def my_place():
    gx, gy = lax.axis_index("gx"), lax.axis_index("gy")
    return gx // 4, gy // 4, (gx % 4) + 4 * ((gy // 2) % 2), gy % 2


def vector_order():
    x, y, z, core = my_place()
    pos = lax.broadcasted_iota(jnp.int32, (1, 1024), 1)
    rest = pos % 4
    mz = (pos // 4) % 8
    mb = (pos // 32) % 2
    b3 = (pos // 64) % 2
    b2 = (pos // 128) % 2
    b1 = (pos // 256) % 2
    owner = core ^ (pos // 512)
    oy = y ^ jnp.where(owner == 0, b1 ^ (3 * b2), (3 * b1) ^ b2)
    coset = jnp.where(owner == 0, (x ^ (x >> 1)) & 1, x >> 1) ^ b3
    ox = jnp.where(owner == 0, coset ^ (3 * mb), 2 * coset + mb)
    return linear(ox, oy, mz, owner) * 4 + rest


HALF = 512


def wave_kernel(first, place, coords, miller, order, source, cos_out, sin_out, sums, *rest):
    cos_ref, sin_ref, sems = rest[-3:]
    if first:
        turned, packed, features = rest[0], rest[1:3], rest[3]
        coords_in, miller_in = coords, miller
        coords, miller = rest[4:6]
        fetch = [
            pltpu.make_async_copy(coords_in, coords, sems.at[2, 1]),
            pltpu.make_async_copy(miller_in, miller, sems.at[2, 2]),
        ]
        load = pltpu.make_async_copy(source, features, sems.at[2, 0])
        for copy in fetch + [load]:
            copy.start()
        for copy in fetch:
            copy.wait()
    else:
        turned = source
    number = miller[...].astype(F32)
    five = jnp.concatenate([number, number[0:2], jnp.zeros((3, 1024), F32)], axis=0).astype(BF16)
    size = order.shape[1]
    natural = lax.broadcasted_iota(jnp.int32, (1024, size), 0)
    pick = jnp.where(natural == order[...], 1.0, 0.0).astype(BF16)
    placed = jnp.dot(five, pick, preferred_element_type=F32).astype(BF16)
    ones = jnp.ones((1, ATOMS), F32)
    copies = []

    for cell in range(CX * CY):
        ia, ib = cell // CY, cell % CY
        block = [coords[ia, d, ib : ib + 1, :].astype(F32) for d in range(3)]
        along = (place[0] * CX + ia).astype(F32) / 32.0
        across = (place[1] * CY + ib).astype(F32) / 64.0
        rows = jnp.concatenate(
            [
                block[0] / 32.0,
                block[1] / 64.0,
                block[2] / slab_depth,
                along * ones,
                across * ones,
                jnp.zeros((3, ATOMS), F32),
            ],
            axis=0,
        )
        columns = rows.T.astype(BF16)
        rows_at = pl.ds(cell * ATOMS, ATOMS)
        for j in range(size // 256):
            lanes = slice(j * 256, (j + 1) * 256)
            angle = jnp.dot(columns, placed[:, lanes], preferred_element_type=F32)
            r = angle - jnp.round(angle)
            s = r * r
            sine = SIN_COEF[3]
            cosine = COS_COEF[3]
            for a in (2, 1, 0):
                sine = sine * s + SIN_COEF[a]
                cosine = cosine * s + COS_COEF[a]
            sine = sine * r
            double = sine + sine
            cos_ref[rows_at, lanes] = (1.0 - double * sine).astype(BF16)
            sin_ref[rows_at, lanes] = (double * cosine).astype(BF16)
        for i, (source, target) in enumerate(((cos_ref, cos_out), (sin_ref, sin_out))):
            copy = pltpu.make_async_copy(source.at[rows_at], target.at[rows_at], sems.at[i, cell])
            copy.start()
            copies.append(copy)

    if first:
        load.wait()
        turned[...] = features[...].astype(F32).T.astype(BF16)
        for cell in range(CX * CY):
            ia, ib = cell // CY, cell % CY
            packed[ia][ib, 0:ATOMS, :] = features[cell * ATOMS : (cell + 1) * ATOMS, :]
            rows = [coords[ia, d, ib : ib + 1, :].astype(F32) for d in range(3)]
            rows = jnp.concatenate(rows + [jnp.zeros((PACK - ATOMS - 3, ATOMS), F32)], axis=0).astype(BF16)
            packed[ia][ib, ATOMS:PACK, :] = jnp.concatenate([rows, jnp.zeros_like(rows)], axis=1)
    for col, table in ((0, cos_ref), (1, sin_ref)):
        total = jnp.dot(turned[...], table[...], preferred_element_type=F32)
        sums[:, col * WIDTH : (col + 1) * WIDTH] = total.T.astype(sums.dtype)
    for copy in copies:
        copy.wait()


def waves(place, coords, miller, order, source, first):
    vm = pl.BlockSpec(memory_space=VMEM)
    hbm = pl.BlockSpec(memory_space=pl.ANY)
    place_of = hbm if first else vm
    size = order.shape[1]
    out_shape = [
        pltpu.MemorySpace.HBM((1024, size), BF16),
        pltpu.MemorySpace.HBM((1024, size), BF16),
        jax.ShapeDtypeStruct((size, 2 * WIDTH), BF16 if first else F32),
    ]
    scratch = [VMEM((1024, size), BF16), VMEM((1024, size), BF16), pltpu.SemaphoreType.DMA((3, CX * CY))]
    if first:
        source, coords, miller = (
            pltpu.with_memory_space_constraint(value, pltpu.MemorySpace.HBM) for value in (source, coords, miller)
        )
        out_shape.append(jax.ShapeDtypeStruct((WIDTH, 1024), BF16))
        out_shape += [jax.ShapeDtypeStruct((CY, PACK, WIDTH), BF16)] * CX
        scratch = [VMEM((1024, WIDTH), BF16), VMEM(coords.shape, BF16), VMEM(miller.shape, jnp.int32)] + scratch
    return pl.pallas_call(
        functools.partial(wave_kernel, first),
        out_shape=out_shape,
        in_specs=[pl.BlockSpec(memory_space=pltpu.SMEM), place_of, place_of, vm, place_of],
        out_specs=[hbm, hbm] + [vm] * (len(out_shape) - 2),
        scratch_shapes=scratch,
        compiler_params=pltpu.CompilerParams(vmem_limit_bytes=14 * 1024 * 1024),
        cost_estimate=pl.CostEstimate(flops=size * 4_000_000, bytes_accessed=3_000_000, transcendentals=0),
        name="wave_tables",
    )(place, coords, miller, order, source)


def prepare_kernel(place, near_count, near_list, coords, row_filter, live, mine, filters):
    shape = (CX * CY, 9)
    cell = lax.broadcasted_iota(jnp.int32, shape, 0)
    slot = lax.broadcasted_iota(jnp.int32, shape, 1)
    entry = near_list[...]
    step_x = ((entry >> 6) - (place[0] * CX + cell // CY) + 1) & 31
    step_y = ((entry & 63) - (place[1] * CY + cell % CY) + 1) & 63
    count = jnp.zeros(shape, jnp.int32)
    for c in range(CX * CY):
        count = jnp.where(cell == c, near_count[c], count)
    code = jnp.where(slot < count, step_x * 3 + step_y, -1)
    for o in range(9):
        live[:, o : o + 1] = jnp.max(jnp.where(code == o, 1.0, 0.0), axis=1, keepdims=True)
    for c in range(CX * CY):
        ia, ib = c // CY, c % CY
        rows = [coords[ia, d, ib : ib + 1, :].astype(F32) for d in range(3)]
        columns = jnp.concatenate(rows + [jnp.zeros((5, ATOMS), F32)], axis=0).T
        for d in range(3):
            mine[c, d] = jnp.broadcast_to(columns[:, d : d + 1], (ATOMS, ATOMS))
    x, z = place[0] // 4, place[0] % 4 + 4 * ((place[1] // 2) % 2)
    member = jnp.where(place[1] % 2 == 0, x // 2, x % 2) * 8 + z
    whole = jnp.concatenate([row_filter[...].astype(F32)] * (CHUNK // 4), axis=0)
    slots = lax.broadcasted_iota(jnp.int32, (CHUNK, WIDTH), 0) // 4
    filters[...] = jnp.where(slots == member, whole, 0.0)


def prepare(place, near_count, near_list, coords, row_filter):
    vm = pl.BlockSpec(memory_space=VMEM)
    sm = pl.BlockSpec(memory_space=pltpu.SMEM)
    return pl.pallas_call(
        prepare_kernel,
        out_shape=(
            jax.ShapeDtypeStruct((CX * CY, 9), F32),
            jax.ShapeDtypeStruct((CX * CY, 3, ATOMS, ATOMS), F32),
            jax.ShapeDtypeStruct((CHUNK, WIDTH), F32),
        ),
        in_specs=[sm, sm, vm, vm, vm],
        out_specs=(vm, vm, vm),
        compiler_params=pltpu.CompilerParams(vmem_limit_bytes=6 * 1024 * 1024),
        cost_estimate=pl.CostEstimate(flops=500_000_000, bytes_accessed=100_000, transcendentals=0),
        name="radial_prepare",
    )(place, near_count, near_list, coords, row_filter)


def radial_kernel(near_cells, fresh, rates, live, filters, mine, *rest):
    acc, scaled = rest[-2:]
    start = rest[-3]
    done = set()
    for i, ((na, nb), (source, at)) in enumerate(near_cells):
        cell_block = rest[source].at[at]
        values = cell_block[0:ATOMS, :]
        for k in range(8):
            scaled[i % 2, k * ATOMS : (k + 1) * ATOMS, :] = values * filters[k : k + 1, :]
        near = cell_block[ATOMS:PACK, 0:ATOMS].astype(F32)
        for ia in range(max(0, na - 1), min(CX, na + 2)):
            for ib in range(max(0, nb - 1), min(CY, nb + 2)):
                u, v = na - ia, nb - ib
                cell = ia * CY + ib
                dx = (near[0:1] + float(u)) - mine[cell, 0]
                dy = (near[1:2] + float(v)) - mine[cell, 1]
                dz = near[2:3] - mine[cell, 2]
                dist = dx * dx + dy * dy + dz * dz
                kernel = jnp.concatenate(
                    [jnp.exp2(dist * (rates[k] * -LOG2E)).astype(BF16) for k in range(8)], axis=1
                )
                o = (u + 1) * 3 + v + 1
                part = jnp.dot(kernel, scaled[i % 2], preferred_element_type=F32) * live[cell : cell + 1, o : o + 1]
                if cell in done:
                    acc[cell] += part
                elif fresh:
                    acc[cell] = part
                else:
                    acc[cell] = start[cell] + part
                done.add(cell)
    for cell in range(CX * CY):
        if cell not in done:
            acc[cell] = jnp.zeros((ATOMS, WIDTH), F32) if fresh else start[cell]


def radial_piece(near_cells, gammas, live, filters, mine, blocks, acc):
    vm = pl.BlockSpec(memory_space=VMEM)
    sm = pl.BlockSpec(memory_space=pltpu.SMEM)
    fresh = acc is None
    arrays = (gammas, live, filters, mine) + blocks + (() if fresh else (acc,))
    return pl.pallas_call(
        functools.partial(radial_kernel, near_cells, fresh),
        out_shape=jax.ShapeDtypeStruct((CX * CY, ATOMS, WIDTH), F32),
        in_specs=[sm] + [vm] * (len(arrays) - 1),
        out_specs=vm,
        scratch_shapes=[VMEM((2, 8 * ATOMS, WIDTH), BF16)],
        input_output_aliases={} if fresh else {len(arrays) - 1: 0},
        compiler_params=pltpu.CompilerParams(vmem_limit_bytes=10 * 1024 * 1024),
        cost_estimate=pl.CostEstimate(flops=2_000_000_000, bytes_accessed=2_000_000, transcendentals=0),
        name="radial_piece",
    )(*arrays)


def edge_kernel(along_x, which, sides, rates, live, filters, mine, block, start, acc, scaled):
    low_side = sides[which] < 0
    step = jnp.where(low_side, -1.0, 1.0)
    across = CY if along_x else CX
    totals = [None] * across
    places = []
    for own in range(across):
        at = (own, (CX - 1) * CY + own) if along_x else (own * CY, own * CY + CY - 1)
        places.append((at, jnp.where(low_side, at[0], at[1])))
    for i in range(CY if along_x else CX + 2):
        line = i if along_x else i - 1
        values = block[i, 0:ATOMS, :]
        for k in range(8):
            scaled[i % 2, k * ATOMS : (k + 1) * ATOMS, :] = values * filters[k : k + 1, :]
        near = block[i, ATOMS:PACK, 0:ATOMS].astype(F32)
        for own in range(max(0, line - 1), min(across, line + 2)):
            shift = line - own
            (cell_low, cell_high), cell = places[own]
            u, v = (step, float(shift)) if along_x else (float(shift), step)
            dx = (near[0:1] + u) - mine[cell, 0]
            dy = (near[1:2] + v) - mine[cell, 1]
            dz = near[2:3] - mine[cell, 2]
            dist = dx * dx + dy * dy + dz * dz
            kernel = jnp.concatenate([jnp.exp2(dist * (rates[k] * -LOG2E)).astype(BF16) for k in range(8)], axis=1)
            o_low, o_high = (shift + 1, 7 + shift) if along_x else (3 * shift + 3, 3 * shift + 5)
            weight = jnp.where(
                low_side,
                live[cell_low : cell_low + 1, o_low : o_low + 1],
                live[cell_high : cell_high + 1, o_high : o_high + 1],
            )
            part = jnp.dot(kernel, scaled[i % 2], preferred_element_type=F32) * weight
            totals[own] = part if totals[own] is None else totals[own] + part
            if line == min(across - 1 + (0 if along_x else 1), own + 1):
                acc[cell] = start[cell] + totals[own]
    for cell in range(CX * CY):
        at_low = cell < CY if along_x else cell % CY == 0
        at_high = cell >= CY if along_x else cell % CY == CY - 1
        if along_x:
            keep_it = jnp.logical_not(low_side) if at_low else low_side
        elif at_low:
            keep_it = jnp.logical_not(low_side)
        elif at_high:
            keep_it = low_side
        else:
            keep_it = None

        def keep_cell(cell=cell):
            acc[cell] = start[cell]

        if keep_it is None:
            keep_cell()
        else:
            pl.when(keep_it)(keep_cell)


def edge_piece(along_x, which, sides, gammas, live, filters, mine, block, acc):
    vm = pl.BlockSpec(memory_space=VMEM)
    sm = pl.BlockSpec(memory_space=pltpu.SMEM)
    return pl.pallas_call(
        functools.partial(edge_kernel, along_x, which),
        out_shape=jax.ShapeDtypeStruct((CX * CY, ATOMS, WIDTH), F32),
        in_specs=[sm, sm] + [vm] * 5,
        out_specs=vm,
        scratch_shapes=[VMEM((2, 8 * ATOMS, WIDTH), BF16)],
        input_output_aliases={6: 0},
        compiler_params=pltpu.CompilerParams(vmem_limit_bytes=10 * 1024 * 1024),
        cost_estimate=pl.CostEstimate(flops=20_000_000_000, bytes_accessed=2_000_000, transcendentals=0),
        name="radial_edge",
    )(sides, gammas, live, filters, mine, block, acc)


def recip_kernel(low, high, cos_ref, sin_ref, coef, start, acc):
    at = slice(low, high)
    lanes = slice(low % 256, (high - 1) % 256 + 1)
    for row in range(4):
        rows = slice(row * 256, row * 256 + 256)
        acc[rows] = (
            start[rows]
            + jnp.dot(cos_ref[rows, lanes], coef[at, 0:WIDTH], preferred_element_type=F32)
            + jnp.dot(sin_ref[rows, lanes], coef[at, WIDTH:], preferred_element_type=F32)
        )


def recip_piece(low, high, cos_table, sin_table, coef, acc):
    vm = pl.BlockSpec(memory_space=VMEM)
    return pl.pallas_call(
        functools.partial(recip_kernel, low, high),
        out_shape=jax.ShapeDtypeStruct((1024, WIDTH), F32),
        in_specs=[vm] * 4,
        out_specs=vm,
        input_output_aliases={3: 0},
        compiler_params=pltpu.CompilerParams(vmem_limit_bytes=10 * 1024 * 1024),
        cost_estimate=pl.CostEstimate(flops=10_000_000_000, bytes_accessed=2_000_000, transcendentals=0),
        name="recip_piece",
    )(cos_table, sin_table, coef, acc)


def final_kernel(cos_ref, sin_ref, coef, features, acc, gain, w_in, w_out, out, result, sems):
    copies = []
    for block in range(4):
        rows = pl.ds(block * 256, 256)
        recip = jnp.dot(cos_ref[rows, :], coef[:, 0:WIDTH], preferred_element_type=F32)
        recip += jnp.dot(sin_ref[rows, :], coef[:, WIDTH:], preferred_element_type=F32)
        mixed = features[rows, :].astype(F32) + acc[rows, :] + recip
        power = jnp.mean(mixed * mixed, axis=-1, keepdims=True)
        normed = (mixed * lax.rsqrt(power + epsilon) * gain[...]).astype(BF16)
        v = jnp.dot(normed, w_in[...], preferred_element_type=F32)
        hidden = (v / (1.0 + jnp.exp(-v))).astype(BF16)
        result[rows, :] = (mixed + jnp.dot(hidden, w_out[...], preferred_element_type=F32)).astype(BF16)
        copy = pltpu.make_async_copy(result.at[rows], out.at[rows], sems.at[block])
        copy.start()
        copies.append(copy)
    for copy in copies:
        copy.wait()


def final(cos_table, sin_table, coef, features, acc, gain, w_in, w_out):
    whole = pl.BlockSpec(memory_space=VMEM)
    return pl.pallas_call(
        final_kernel,
        out_shape=pltpu.MemorySpace.HBM((1024, WIDTH), BF16),
        in_specs=[whole] * 8,
        out_specs=pl.BlockSpec(memory_space=pl.ANY),
        scratch_shapes=[VMEM((1024, WIDTH), BF16), pltpu.SemaphoreType.DMA((4,))],
        compiler_params=pltpu.CompilerParams(vmem_limit_bytes=14 * 1024 * 1024),
        cost_estimate=pl.CostEstimate(flops=3_000_000_000, bytes_accessed=8_000_000, transcendentals=0),
        name="mix_and_network",
    )(cos_table, sin_table, coef, features, acc, gain, w_in, w_out)


def row_pairs(first):
    def other(gx):
        return (gx + 1) % 16 if (gx % 2 == 0) == first else (gx - 1) % 16

    return [(i, other(i)) for i in range(16)]


def column_pairs(first):
    return row_pairs(first)


def per_device(
    features,
    coords,
    nbr_cells,
    nbr_count,
    miller,
    gammas,
    radial_filter,
    reciprocal_filter,
    norm_gain,
    w_in,
    w_out,
):
    gx, gy = lax.axis_index("gx"), lax.axis_index("gy")
    place = jnp.stack([gx, gy]).astype(jnp.int32)
    own_rows = features.reshape(1024, WIDTH)
    turned = coords.transpose(0, 2, 1, 3)
    order = vector_order()
    barrier = lax.optimization_barrier

    cos_far, sin_far, send, across, upper, lower = waves(place, turned, miller, order[:, HALF:], own_rows, True)
    got = permute(send, HALVING[0])
    even_x, even_y = gx % 2 == 0, gy % 2 == 0
    sides = jnp.stack(
        [jnp.where(even_x, 1, -1), jnp.where(even_x, -1, 1), jnp.where(even_y, 1, -1), jnp.where(even_y, -1, 1)]
    ).astype(jnp.int32)
    row_a = lax.ppermute(jnp.where(even_x, lower, upper), "gx", row_pairs(True))
    row_b = lax.ppermute(jnp.where(even_x, upper, lower), "gx", row_pairs(False))
    cos_next, sin_next, keep_next = waves(place, turned, miller, order[:, 256:HALF], across, False)

    acc = None

    def own_piece(jb, acc):
        near_cells = tuple(((ja, jb), (ja, jb)) for ja in range(CX))
        return radial_piece(near_cells, gammas, live, radial_filter, mine, (upper, lower), acc)

    def beyond(along_x, which, block, acc):
        return edge_piece(along_x, which, sides, gammas, live, radial_filter, mine, block, acc)

    for step, height in ((1, 256), (2, 128), (3, 64)):
        send = ((keep_next if step == 1 else keep[height:]) + got[height:].astype(F32)).astype(BF16)
        if step == 2:
            send, live, mine, filters = barrier((send, live, mine, filters))
        elif step == 3:
            send, acc = barrier((send, acc))
        fresh = permute(send, HALVING[step])
        if step == 1:
            across, place, send = barrier((across, place, send))
            cos_near, sin_near, keep = waves(place, turned, miller, order[:, :256], across, False)
            live, mine, filters = prepare(
                place, nbr_count.reshape(8), nbr_cells.reshape(8, 9), turned, reciprocal_filter
            )
        else:
            acc = own_piece(step - 2, acc)
        keep = keep[:height] + got[:height].astype(F32)
        got = fresh
    total = jnp.concatenate([keep + got.astype(F32), filters], axis=1)
    for step in range(4):
        total, acc = barrier((total, acc))
        fresh = permute(total.astype(BF16), DOUBLING[step])
        if step < 2:
            acc = own_piece(step + 2, acc)
        else:
            acc = beyond(True, step - 2, row_a if step == 2 else row_b, acc)
        total = total + fresh.astype(F32)
    scale = total[:, 2 * WIDTH :]
    chunk = jnp.concatenate([total[:, :WIDTH] * scale, total[:, WIDTH : 2 * WIDTH] * scale], axis=1).astype(BF16)
    chunk, row_a, row_b = barrier((chunk, row_a, row_b))
    for step, low_at, high_at in ((3, 0, 0), (2, 0, 128), (1, 128, 256), (0, 256, 512)):
        chunk, acc = barrier((chunk, acc))
        fresh = permute(chunk, HALVING[step])
        if step == 3:
            ends = [
                (jnp.where(even_x, row_b[b : b + 1], row_a[b : b + 1]), jnp.where(even_x, row_a[b : b + 1], row_b[b : b + 1]))
                for b in (0, CY - 1)
            ]
            left, right = (
                jnp.concatenate([low, upper[b : b + 1], lower[b : b + 1], high], axis=0)
                for b, (low, high) in zip((0, CY - 1), ends)
            )
            far_send, near_send = jnp.where(even_y, left, right), jnp.where(even_y, right, left)
            column_b = lax.ppermute(far_send, "gy", column_pairs(False))
        elif step == 2:
            near_send, chunk = barrier((near_send, chunk))
            column_a = lax.ppermute(near_send, "gy", column_pairs(True))
        elif step == 1:
            acc = beyond(False, 2, column_a, acc)
        elif step == 0:
            acc = beyond(False, 3, column_b, acc)
        if high_at:
            tables = (cos_near, sin_near) if high_at <= 256 else (cos_next, sin_next)
            acc = recip_piece(low_at, high_at, *tables, chunk, acc.reshape(1024, WIDTH)).reshape(CX * CY, ATOMS, WIDTH)
        if step:
            chunk = jnp.concatenate([chunk, fresh], axis=0)
    acc = acc.reshape(1024, WIDTH)

    out = final(
        cos_far, sin_far, fresh, own_rows, acc, norm_gain.reshape(1, WIDTH), w_in, w_out
    )
    return out.reshape(CX, CY, ATOMS, WIDTH)


def solution(mesh):
    in_specs = (
        P("gx", "gy", None, None),
        P("gx", "gy", None, None),
        P("gx", "gy", None),
        P("gx", "gy"),
        P(),
        P(),
        P(),
        P(("gx", "gy"), None),
        P(),
        P(),
        P(),
    )
    out_specs = P("gx", "gy", None, None)
    return jax.shard_map(
        per_device, mesh=mesh, in_specs=in_specs, out_specs=out_specs, check_vma=False
    )
```

```python
import functools

import jax
import jax.numpy as jnp
from jax import lax
from jax.experimental import pallas as pl
from jax.experimental.pallas import tpu as pltpu
from jax.sharding import PartitionSpec as P

slab_depth = 2.0
epsilon = 1e-06
LOG2E = 1.4426950408889634
AXES = ("gx", "gy")
F32 = jnp.float32
BF16 = jnp.bfloat16
CX, CY, ATOMS, WIDTH = 2, 4, 128, 256
PACK = 144
VMEM = pltpu.VMEM

SIN_COEF = (3.14159027, -5.16740673, 2.54401052, -0.55946246)
COS_COEF = (0.99999325, -4.93393467, 4.0412481, -1.22203176)


def linear(x, y, z, core):
    return (x * 4 + z % 4) * 16 + y * 4 + (z // 4) * 2 + core


def partner_list(step):
    pairs = []
    for x in range(4):
        for y in range(4):
            for z in range(8):
                for core in range(2):
                    pairs.append((linear(x, y, z, core), linear(*step(x, y, z, core))))
    return pairs


def flip_core(x, y, z, core):
    return x, y, z, 1 - core


def flip_x(first, second):
    def step(x, y, z, core):
        return x ^ (second if core else first), y, z, core

    return step


def flip_y(first, second):
    def step(x, y, z, core):
        return x, y ^ (second if core else first), z, core

    return step


def flip_z(which):
    table = ((1, 0, 3, 2, 5, 4, 7, 6), (7, 2, 1, 4, 3, 6, 5, 0), (3, 6, 5, 0, 7, 2, 1, 4))[which]

    def step(x, y, z, core):
        return x, y, table[z] if core == 0 else (table[(z - 1) % 8] + 1) % 8, core

    return step


HALVING = (flip_core, flip_y(1, 3), flip_y(3, 1), flip_x(1, 3))
DOUBLING = (flip_x(3, 1), flip_z(0), flip_z(1), flip_z(2))
CHUNK = 64


def permute(value, step):
    return lax.ppermute(value, AXES, partner_list(step))


def my_place():
    gx, gy = lax.axis_index("gx"), lax.axis_index("gy")
    return gx // 4, gy // 4, (gx % 4) + 4 * ((gy // 2) % 2), gy % 2


def vector_order():
    x, y, z, core = my_place()
    pos = lax.broadcasted_iota(jnp.int32, (1, 1024), 1)
    rest = pos % 4
    mz = (pos // 4) % 8
    mb = (pos // 32) % 2
    b2 = (pos // 64) % 2
    b3 = (pos // 128) % 2
    b1 = (pos // 256) % 2
    owner = core ^ (pos // 512)
    oy = y ^ jnp.where(owner == 0, b1 ^ (3 * b2), (3 * b1) ^ b2)
    coset = jnp.where(owner == 0, (x ^ (x >> 1)) & 1, x >> 1) ^ b3
    ox = jnp.where(owner == 0, coset ^ (3 * mb), 2 * coset + mb)
    return linear(ox, oy, mz, owner) * 4 + rest


HALF = 512


def wave_kernel(first, place, coords, miller, order, source, cos_out, sin_out, sums, *rest):
    cos_ref, sin_ref, copies = cos_out, sin_out, []
    if first:
        turned, packed, features = rest[0], rest[1:3], rest[3]
        coords_in, miller_in = coords, miller
        coords, miller, cos_ref, sin_ref, sems, table_sems = rest[4:]
        fetch = [
            pltpu.make_async_copy(coords_in, coords, sems.at[1]),
            pltpu.make_async_copy(miller_in, miller, sems.at[2]),
        ]
        load = pltpu.make_async_copy(source, features, sems.at[0])
        for copy in fetch + [load]:
            copy.start()
        for copy in fetch:
            copy.wait()
    else:
        turned = source
    number = miller[...].astype(F32)
    five = jnp.concatenate([number, number[0:2], jnp.zeros((3, 1024), F32)], axis=0).astype(BF16)
    size = order.shape[1]
    natural = lax.broadcasted_iota(jnp.int32, (1024, size), 0)
    pick = jnp.where(natural == order[...], 1.0, 0.0).astype(BF16)
    placed = jnp.dot(five, pick, preferred_element_type=F32).astype(BF16)
    ones = jnp.ones((1, ATOMS), F32)

    for cell in range(CX * CY):
        rows_at = pl.ds(cell * ATOMS, ATOMS)
        ia, ib = cell // CY, cell % CY
        block = [coords[ia, d, ib : ib + 1, :].astype(F32) for d in range(3)]
        along = (place[0] * CX + ia).astype(F32) / 32.0
        across = (place[1] * CY + ib).astype(F32) / 64.0
        rows = jnp.concatenate(
            [
                block[0] / 32.0,
                block[1] / 64.0,
                block[2] / slab_depth,
                along * ones,
                across * ones,
                jnp.zeros((3, ATOMS), F32),
            ],
            axis=0,
        )
        at = rows.T.astype(BF16)
        for j in range(size // 256):
            lanes = slice(j * 256, (j + 1) * 256)
            angle = jnp.dot(at, placed[:, lanes], preferred_element_type=F32)
            r = angle - jnp.round(angle)
            s = r * r
            sine = SIN_COEF[3]
            cosine = COS_COEF[3]
            for a in (2, 1, 0):
                sine = sine * s + SIN_COEF[a]
                cosine = cosine * s + COS_COEF[a]
            sine = sine * r
            double = sine + sine
            cos_ref[rows_at, lanes] = (1.0 - double * sine).astype(BF16)
            sin_ref[rows_at, lanes] = (double * cosine).astype(BF16)

        if first:
            for i, (table, target) in enumerate(((cos_ref, cos_out), (sin_ref, sin_out))):
                copy = pltpu.make_async_copy(table.at[rows_at], target.at[rows_at], table_sems.at[i, cell])
                copy.start()
                copies.append(copy)

    if first:
        load.wait()
        turned[...] = features[...].astype(F32).T.astype(BF16)
        for cell in range(CX * CY):
            ia, ib = cell // CY, cell % CY
            packed[ia][ib, 0:ATOMS, :] = features[cell * ATOMS : (cell + 1) * ATOMS, :]
            rows = [coords[ia, d, ib : ib + 1, :].astype(F32) for d in range(3)]
            rows = jnp.concatenate(rows + [jnp.zeros((PACK - ATOMS - 3, ATOMS), F32)], axis=0).astype(BF16)
            packed[ia][ib, ATOMS:PACK, :] = jnp.concatenate([rows, jnp.zeros_like(rows)], axis=1)
    for col, table in ((0, cos_ref), (1, sin_ref)):
        total = jnp.dot(turned[...], table[...], preferred_element_type=F32)
        sums[:, col * WIDTH : (col + 1) * WIDTH] = total.T.astype(sums.dtype)
    for copy in copies:
        copy.wait()


def waves(place, coords, miller, order, source, first):
    vm = pl.BlockSpec(memory_space=VMEM)
    hbm = pl.BlockSpec(memory_space=pl.ANY)
    place_of = hbm if first else vm
    size = order.shape[1]
    out_shape = [
        (pltpu.MemorySpace.HBM if first else pltpu.MemorySpace.VMEM)((1024, size), BF16),
        (pltpu.MemorySpace.HBM if first else pltpu.MemorySpace.VMEM)((1024, size), BF16),
        jax.ShapeDtypeStruct((size, 2 * WIDTH), BF16 if first else F32),
    ]
    scratch = []
    if first:
        source, coords, miller = (
            pltpu.with_memory_space_constraint(value, pltpu.MemorySpace.HBM) for value in (source, coords, miller)
        )
        out_shape.append(jax.ShapeDtypeStruct((WIDTH, 1024), BF16))
        out_shape += [jax.ShapeDtypeStruct((CY, PACK, WIDTH), BF16)] * CX
        scratch = [VMEM((1024, WIDTH), BF16), VMEM(coords.shape, BF16), VMEM(miller.shape, jnp.int32)]
        scratch += [VMEM((1024, size), BF16)] * 2 + [pltpu.SemaphoreType.DMA((3,)), pltpu.SemaphoreType.DMA((2, CX * CY))]
    return pl.pallas_call(
        functools.partial(wave_kernel, first),
        out_shape=out_shape,
        in_specs=[pl.BlockSpec(memory_space=pltpu.SMEM), place_of, place_of, vm, place_of],
        out_specs=[place_of, place_of] + [vm] * (len(out_shape) - 2),
        scratch_shapes=scratch,
        compiler_params=pltpu.CompilerParams(vmem_limit_bytes=14 * 1024 * 1024),
        cost_estimate=pl.CostEstimate(flops=size * 4_000_000, bytes_accessed=3_000_000, transcendentals=0),
        name="wave_tables",
    )(place, coords, miller, order, source)


def prepare_kernel(place, near_count, near_list, coords, row_filter, live, mine, filters):
    shape = (CX * CY, 9)
    cell = lax.broadcasted_iota(jnp.int32, shape, 0)
    slot = lax.broadcasted_iota(jnp.int32, shape, 1)
    entry = near_list[...]
    step_x = ((entry >> 6) - (place[0] * CX + cell // CY) + 1) & 31
    step_y = ((entry & 63) - (place[1] * CY + cell % CY) + 1) & 63
    count = jnp.zeros(shape, jnp.int32)
    for c in range(CX * CY):
        count = jnp.where(cell == c, near_count[c], count)
    code = jnp.where(slot < count, step_x * 3 + step_y, -1)
    for o in range(9):
        live[:, o : o + 1] = jnp.max(jnp.where(code == o, 1.0, 0.0), axis=1, keepdims=True)
    for c in range(CX * CY):
        ia, ib = c // CY, c % CY
        rows = [coords[ia, d, ib : ib + 1, :].astype(F32) for d in range(3)]
        columns = jnp.concatenate(rows + [jnp.zeros((5, ATOMS), F32)], axis=0).T
        for d in range(3):
            mine[c, d] = jnp.broadcast_to(columns[:, d : d + 1], (ATOMS, ATOMS))
    x, z = place[0] // 4, place[0] % 4 + 4 * ((place[1] // 2) % 2)
    member = jnp.where(place[1] % 2 == 0, x // 2, x % 2) * 8 + z
    whole = jnp.concatenate([row_filter[...].astype(F32)] * (CHUNK // 4), axis=0)
    slots = lax.broadcasted_iota(jnp.int32, (CHUNK, WIDTH), 0) // 4
    filters[...] = jnp.where(slots == member, whole, 0.0)


def prepare(place, near_count, near_list, coords, row_filter):
    vm = pl.BlockSpec(memory_space=VMEM)
    sm = pl.BlockSpec(memory_space=pltpu.SMEM)
    return pl.pallas_call(
        prepare_kernel,
        out_shape=(
            jax.ShapeDtypeStruct((CX * CY, 9), F32),
            jax.ShapeDtypeStruct((CX * CY, 3, ATOMS, ATOMS), F32),
            jax.ShapeDtypeStruct((CHUNK, WIDTH), F32),
        ),
        in_specs=[sm, sm, vm, vm, vm],
        out_specs=(vm, vm, vm),
        compiler_params=pltpu.CompilerParams(vmem_limit_bytes=6 * 1024 * 1024),
        cost_estimate=pl.CostEstimate(flops=500_000_000, bytes_accessed=100_000, transcendentals=0),
        name="radial_prepare",
    )(place, near_count, near_list, coords, row_filter)


def radial_kernel(near_cells, fresh, rates, live, filters, mine, *rest):
    acc, scaled = rest[-2:]
    start = rest[-3]
    done = set()
    for i, ((na, nb), (source, at)) in enumerate(near_cells):
        cell_block = rest[source].at[at]
        values = cell_block[0:ATOMS, :]
        for k in range(8):
            scaled[i % 2, k * ATOMS : (k + 1) * ATOMS, :] = values * filters[k : k + 1, :]
        near = cell_block[ATOMS:PACK, 0:ATOMS].astype(F32)
        for ia in range(max(0, na - 1), min(CX, na + 2)):
            for ib in range(max(0, nb - 1), min(CY, nb + 2)):
                u, v = na - ia, nb - ib
                cell = ia * CY + ib
                dx = (near[0:1] + float(u)) - mine[cell, 0]
                dy = (near[1:2] + float(v)) - mine[cell, 1]
                dz = near[2:3] - mine[cell, 2]
                dist = dx * dx + dy * dy + dz * dz
                kernel = jnp.concatenate(
                    [jnp.exp2(dist * (rates[k] * -LOG2E)).astype(BF16) for k in range(8)], axis=1
                )
                o = (u + 1) * 3 + v + 1
                part = jnp.dot(kernel, scaled[i % 2], preferred_element_type=F32) * live[cell : cell + 1, o : o + 1]
                if cell in done:
                    acc[cell] += part
                elif fresh:
                    acc[cell] = part
                else:
                    acc[cell] = start[cell] + part
                done.add(cell)
    for cell in range(CX * CY):
        if cell not in done:
            acc[cell] = jnp.zeros((ATOMS, WIDTH), F32) if fresh else start[cell]


def radial_piece(near_cells, gammas, live, filters, mine, blocks, acc):
    vm = pl.BlockSpec(memory_space=VMEM)
    sm = pl.BlockSpec(memory_space=pltpu.SMEM)
    fresh = acc is None
    arrays = (gammas, live, filters, mine) + blocks + (() if fresh else (acc,))
    return pl.pallas_call(
        functools.partial(radial_kernel, near_cells, fresh),
        out_shape=jax.ShapeDtypeStruct((CX * CY, ATOMS, WIDTH), F32),
        in_specs=[sm] + [vm] * (len(arrays) - 1),
        out_specs=vm,
        scratch_shapes=[VMEM((2, 8 * ATOMS, WIDTH), BF16)],
        input_output_aliases={} if fresh else {len(arrays) - 1: 0},
        compiler_params=pltpu.CompilerParams(vmem_limit_bytes=10 * 1024 * 1024),
        cost_estimate=pl.CostEstimate(flops=2_000_000_000, bytes_accessed=2_000_000, transcendentals=0),
        name="radial_piece",
    )(*arrays)


def edge_kernel(along_x, which, sides, rates, live, filters, mine, block, start, acc, scaled):
    low_side = sides[which] < 0
    step = jnp.where(low_side, -1.0, 1.0)
    across = CY if along_x else CX
    totals = [None] * across
    places = []
    for own in range(across):
        at = (own, (CX - 1) * CY + own) if along_x else (own * CY, own * CY + CY - 1)
        places.append((at, jnp.where(low_side, at[0], at[1])))
    for i in range(CY if along_x else CX + 2):
        line = i if along_x else i - 1
        values = block[i, 0:ATOMS, :]
        for k in range(8):
            scaled[i % 2, k * ATOMS : (k + 1) * ATOMS, :] = values * filters[k : k + 1, :]
        near = block[i, ATOMS:PACK, 0:ATOMS].astype(F32)
        for own in range(max(0, line - 1), min(across, line + 2)):
            shift = line - own
            (cell_low, cell_high), cell = places[own]
            u, v = (step, float(shift)) if along_x else (float(shift), step)
            dx = (near[0:1] + u) - mine[cell, 0]
            dy = (near[1:2] + v) - mine[cell, 1]
            dz = near[2:3] - mine[cell, 2]
            dist = dx * dx + dy * dy + dz * dz
            kernel = jnp.concatenate([jnp.exp2(dist * (rates[k] * -LOG2E)).astype(BF16) for k in range(8)], axis=1)
            o_low, o_high = (shift + 1, 7 + shift) if along_x else (3 * shift + 3, 3 * shift + 5)
            weight = jnp.where(
                low_side,
                live[cell_low : cell_low + 1, o_low : o_low + 1],
                live[cell_high : cell_high + 1, o_high : o_high + 1],
            )
            part = jnp.dot(kernel, scaled[i % 2], preferred_element_type=F32) * weight
            totals[own] = part if totals[own] is None else totals[own] + part
            if line == min(across - 1 + (0 if along_x else 1), own + 1):
                acc[cell] = start[cell] + totals[own]
    for cell in range(CX * CY):
        at_low = cell < CY if along_x else cell % CY == 0
        at_high = cell >= CY if along_x else cell % CY == CY - 1
        if along_x:
            keep_it = jnp.logical_not(low_side) if at_low else low_side
        elif at_low:
            keep_it = jnp.logical_not(low_side)
        elif at_high:
            keep_it = low_side
        else:
            keep_it = None

        def keep_cell(cell=cell):
            acc[cell] = start[cell]

        if keep_it is None:
            keep_cell()
        else:
            pl.when(keep_it)(keep_cell)


def edge_piece(along_x, which, sides, gammas, live, filters, mine, block, acc):
    flops = 20_000_000_000
    vm = pl.BlockSpec(memory_space=VMEM)
    sm = pl.BlockSpec(memory_space=pltpu.SMEM)
    return pl.pallas_call(
        functools.partial(edge_kernel, along_x, which),
        out_shape=jax.ShapeDtypeStruct((CX * CY, ATOMS, WIDTH), F32),
        in_specs=[sm, sm] + [vm] * 5,
        out_specs=vm,
        scratch_shapes=[VMEM((2, 8 * ATOMS, WIDTH), BF16)],
        input_output_aliases={6: 0},
        compiler_params=pltpu.CompilerParams(vmem_limit_bytes=10 * 1024 * 1024),
        cost_estimate=pl.CostEstimate(flops=flops, bytes_accessed=2_000_000, transcendentals=0),
        name="radial_edge",
    )(sides, gammas, live, filters, mine, block, acc)


def recip_kernel(spots, *refs):
    coef, start, acc = refs[-3:]
    for row in range(4):
        rows = slice(row * 256, row * 256 + 256)
        total = start[rows]
        for i, (column, at) in enumerate(spots):
            lanes, span = slice(column, column + 128), slice(at, at + 128)
            total += jnp.dot(refs[2 * i][rows, lanes], coef[span, 0:WIDTH], preferred_element_type=F32)
            total += jnp.dot(refs[2 * i + 1][rows, lanes], coef[span, WIDTH:], preferred_element_type=F32)
        acc[rows] = total


def recip_piece(parts, far, coef, acc):
    vm = pl.BlockSpec(memory_space=VMEM)
    tables = [table for part in parts for table in part[:2]] + list(far)
    return pl.pallas_call(
        functools.partial(recip_kernel, tuple(part[2:] for part in parts)),
        out_shape=jax.ShapeDtypeStruct((1024, WIDTH), F32),
        in_specs=[vm] * (len(tables) + 2),
        out_specs=vm,
        input_output_aliases={len(tables) + 1: 0},
        compiler_params=pltpu.CompilerParams(vmem_limit_bytes=10 * 1024 * 1024),
        cost_estimate=pl.CostEstimate(flops=10_000_000_000, bytes_accessed=2_000_000, transcendentals=0),
        name="recip_piece",
    )(*tables, coef, acc)


def final_kernel(cos_ref, sin_ref, coef_in, upper, lower, acc, gain, w_in, w_out, out, coef, result, sems):
    for block, source in enumerate((0, 2, 1, 3)):
        coef[block * 128 : block * 128 + 128, :] = coef_in[source * 128 : source * 128 + 128, :]
    copies = []
    for block in range(4):
        rows = pl.ds(block * 256, 256)
        recip = jnp.dot(cos_ref[rows, :], coef[:, 0:WIDTH], preferred_element_type=F32)
        recip += jnp.dot(sin_ref[rows, :], coef[:, WIDTH:], preferred_element_type=F32)
        cells = (upper, lower)[block // 2]
        features = jnp.concatenate([cells[block % 2 * 2 + i, 0:ATOMS, :] for i in range(2)], axis=0)
        mixed = features.astype(F32) + acc[rows, :] + recip
        power = jnp.mean(mixed * mixed, axis=-1, keepdims=True)
        normed = (mixed * lax.rsqrt(power + epsilon) * gain[...]).astype(BF16)
        v = jnp.dot(normed, w_in[...], preferred_element_type=F32)
        hidden = (v / (1.0 + jnp.exp(-v))).astype(BF16)
        result[rows, :] = (mixed + jnp.dot(hidden, w_out[...], preferred_element_type=F32)).astype(BF16)
        copy = pltpu.make_async_copy(result.at[rows], out.at[rows], sems.at[block])
        copy.start()
        copies.append(copy)
    for copy in copies:
        copy.wait()


def final(cos_table, sin_table, coef, upper, lower, acc, gain, w_in, w_out):
    whole = pl.BlockSpec(memory_space=VMEM)
    return pl.pallas_call(
        final_kernel,
        out_shape=pltpu.MemorySpace.HBM((1024, WIDTH), BF16),
        in_specs=[whole] * 9,
        out_specs=pl.BlockSpec(memory_space=pl.ANY),
        scratch_shapes=[VMEM((HALF, 2 * WIDTH), BF16), VMEM((1024, WIDTH), BF16), pltpu.SemaphoreType.DMA((4,))],
        compiler_params=pltpu.CompilerParams(vmem_limit_bytes=14 * 1024 * 1024),
        cost_estimate=pl.CostEstimate(flops=3_000_000_000, bytes_accessed=8_000_000, transcendentals=0),
        name="mix_and_network",
    )(cos_table, sin_table, coef, upper, lower, acc, gain, w_in, w_out)


def row_pairs(first):
    def other(gx):
        return (gx + 1) % 16 if (gx % 2 == 0) == first else (gx - 1) % 16

    return [(i, other(i)) for i in range(16)]


def column_pairs(first):
    return row_pairs(first)


def first_blocks(rows):
    return jnp.concatenate([rows[0:64], rows[128:192]], axis=0)


def second_blocks(rows):
    return jnp.concatenate([rows[64:128], rows[192:256]], axis=0)


def per_device(
    features,
    coords,
    nbr_cells,
    nbr_count,
    miller,
    gammas,
    radial_filter,
    reciprocal_filter,
    norm_gain,
    w_in,
    w_out,
):
    gx, gy = lax.axis_index("gx"), lax.axis_index("gy")
    place = jnp.stack([gx, gy]).astype(jnp.int32)
    own_rows = features.reshape(1024, WIDTH)
    turned = coords.transpose(0, 2, 1, 3)
    order = vector_order()
    barrier = lax.optimization_barrier

    cos_far, sin_far, send, across, upper, lower = waves(place, turned, miller, order[:, HALF:], own_rows, True)
    got = permute(send, HALVING[0])
    even_x, even_y = gx % 2 == 0, gy % 2 == 0
    sides = jnp.stack(
        [jnp.where(even_x, 1, -1), jnp.where(even_x, -1, 1), jnp.where(even_y, 1, -1), jnp.where(even_y, -1, 1)]
    ).astype(jnp.int32)
    row_a = lax.ppermute(jnp.where(even_x, lower, upper), "gx", row_pairs(True))
    row_b = lax.ppermute(jnp.where(even_x, upper, lower), "gx", row_pairs(False))
    cos_next, sin_next, keep_next = waves(place, turned, miller, order[:, 256:HALF], across, False)

    acc = None

    def own_piece(jb, acc):
        near_cells = tuple(((ja, jb), (ja, jb)) for ja in range(CX))
        return radial_piece(near_cells, gammas, live, radial_filter, mine, (upper, lower), acc)

    def beyond(along_x, which, block, acc):
        return edge_piece(along_x, which, sides, gammas, live, radial_filter, mine, block, acc)

    for step, height in ((1, 256), (2, 128), (3, 64)):
        if step == 2:
            send = (second_blocks(keep) + second_blocks(got).astype(F32)).astype(BF16)
        else:
            send = ((keep_next if step == 1 else keep[height:]) + got[height:].astype(F32)).astype(BF16)
        if step == 2:
            send, live, mine, filters = barrier((send, live, mine, filters))
        elif step == 3:
            send, acc = barrier((send, acc))
        fresh = permute(send, HALVING[step])
        if step == 1:
            across, place, send = barrier((across, place, send))
            cos_near, sin_near, keep = waves(place, turned, miller, order[:, :256], across, False)
            live, mine, filters = prepare(
                place, nbr_count.reshape(8), nbr_cells.reshape(8, 9), turned, reciprocal_filter
            )
        else:
            acc = own_piece(step - 2, acc)
        if step == 2:
            keep = first_blocks(keep) + first_blocks(got).astype(F32)
        else:
            keep = keep[:height] + got[:height].astype(F32)
        got = fresh
    total = jnp.concatenate([keep + got.astype(F32), filters], axis=1)
    for step in range(4):
        total, acc = barrier((total, acc))
        fresh = permute(total.astype(BF16), DOUBLING[step])
        if step < 2:
            acc = own_piece(step + 2, acc)
        else:
            acc = beyond(True, step - 2, row_a if step == 2 else row_b, acc)
        total = total + fresh.astype(F32)
    scale = total[:, 2 * WIDTH :]
    chunk = jnp.concatenate([total[:, :WIDTH] * scale, total[:, WIDTH : 2 * WIDTH] * scale], axis=1).astype(BF16)
    chunk, row_a, row_b = barrier((chunk, row_a, row_b))
    for turn, step in enumerate((2, 1, 3, 0)):
        chunk, acc = barrier((chunk, acc))
        fresh = permute(chunk, HALVING[step])
        if turn == 0:
            ends = [
                (jnp.where(even_x, row_b[b : b + 1], row_a[b : b + 1]), jnp.where(even_x, row_a[b : b + 1], row_b[b : b + 1]))
                for b in (0, CY - 1)
            ]
            left, right = (
                jnp.concatenate([low, upper[b : b + 1], lower[b : b + 1], high], axis=0)
                for b, (low, high) in zip((0, CY - 1), ends)
            )
            far_send, near_send = jnp.where(even_y, left, right), jnp.where(even_y, right, left)
            column_b = lax.ppermute(far_send, "gy", column_pairs(False))
        elif turn == 1:
            near_send, chunk = barrier((near_send, chunk))
            column_a = lax.ppermute(near_send, "gy", column_pairs(True))
        elif turn == 2:
            acc = beyond(False, 2, column_a, acc)
        elif turn == 3:
            acc = beyond(False, 3, column_b, acc)
        parts = (
            (),
            ((cos_near, sin_near, 0, 0),),
            ((cos_next, sin_next, 0, 128),),
            ((cos_near, sin_near, 128, 256), (cos_next, sin_next, 128, 384)),
        )[turn]
        if parts:
            far = (cos_far, sin_far, w_in, w_out) if turn > 1 else ()
            acc = recip_piece(parts, far, chunk, acc.reshape(1024, WIDTH)).reshape(CX * CY, ATOMS, WIDTH)
        if step:
            chunk = jnp.concatenate([chunk, fresh], axis=0)
    acc = acc.reshape(1024, WIDTH)

    out = final(
        cos_far, sin_far, fresh, upper, lower, acc, norm_gain.reshape(1, WIDTH), w_in, w_out
    )
    return out.reshape(CX, CY, ATOMS, WIDTH)


def solution(mesh):
    in_specs = (
        P("gx", "gy", None, None),
        P("gx", "gy", None, None),
        P("gx", "gy", None),
        P("gx", "gy"),
        P(),
        P(),
        P(),
        P(("gx", "gy"), None),
        P(),
        P(),
        P(),
    )
    out_specs = P("gx", "gy", None, None)
    return jax.shard_map(
        per_device, mesh=mesh, in_specs=in_specs, out_specs=out_specs, check_vma=False
    )
```

```python
import functools

import jax
import jax.numpy as jnp
from jax import lax
from jax.experimental import pallas as pl
from jax.experimental.pallas import tpu as pltpu
from jax.sharding import PartitionSpec as P

slab_depth = 2.0
epsilon = 1e-06
LOG2E = 1.4426950408889634
AXES = ("gx", "gy")
F32 = jnp.float32
BF16 = jnp.bfloat16
CX, CY, ATOMS, WIDTH = 2, 4, 128, 256
PACK = 144
VMEM = pltpu.VMEM

SIN_COEF = (3.14159027, -5.16740673, 2.54401052, -0.55946246)
COS_COEF = (0.99999325, -4.93393467, 4.0412481, -1.22203176)


def linear(x, y, z, core):
    return (x * 4 + z % 4) * 16 + y * 4 + (z // 4) * 2 + core


def partner_list(step):
    pairs = []
    for x in range(4):
        for y in range(4):
            for z in range(8):
                for core in range(2):
                    pairs.append((linear(x, y, z, core), linear(*step(x, y, z, core))))
    return pairs


def flip_core(x, y, z, core):
    return x, y, z, 1 - core


def flip_x(first, second):
    def step(x, y, z, core):
        return x ^ (second if core else first), y, z, core

    return step


def flip_y(first, second):
    def step(x, y, z, core):
        return x, y ^ (second if core else first), z, core

    return step


def flip_z(which):
    table = ((1, 0, 3, 2, 5, 4, 7, 6), (7, 2, 1, 4, 3, 6, 5, 0), (3, 6, 5, 0, 7, 2, 1, 4))[which]

    def step(x, y, z, core):
        return x, y, table[z] if core == 0 else (table[(z - 1) % 8] + 1) % 8, core

    return step


HALVING = (flip_core, flip_y(1, 3), flip_y(3, 1), flip_x(1, 3))
DOUBLING = (flip_x(3, 1), flip_z(0), flip_z(1), flip_z(2))
CHUNK = 64


def permute(value, step):
    return lax.ppermute(value, AXES, partner_list(step))


def my_place():
    gx, gy = lax.axis_index("gx"), lax.axis_index("gy")
    return gx // 4, gy // 4, (gx % 4) + 4 * ((gy // 2) % 2), gy % 2


def vector_order():
    x, y, z, core = my_place()
    pos = lax.broadcasted_iota(jnp.int32, (1, 1024), 1)
    rest = pos % 4
    mz = (pos // 4) % 8
    mb = (pos // 32) % 2
    b2 = (pos // 64) % 2
    b3 = (pos // 128) % 2
    b1 = (pos // 256) % 2
    owner = core ^ (pos // 512)
    oy = y ^ jnp.where(owner == 0, b1 ^ (3 * b2), (3 * b1) ^ b2)
    coset = jnp.where(owner == 0, (x ^ (x >> 1)) & 1, x >> 1) ^ b3
    ox = jnp.where(owner == 0, coset ^ (3 * mb), 2 * coset + mb)
    return linear(ox, oy, mz, owner) * 4 + rest


def z_sources():
    table = []
    for core in range(2):
        for own in range(8):
            for b in range(8):
                z = own
                for which in (2, 1, 0):
                    if b >> which & 1:
                        z = flip_z(which)(0, 0, z, core)[2]
                table.append(z)
    return jnp.asarray(table, jnp.int32)


HALF = 512


def wave_kernel(first, place, coords, miller, order, source, cos_out, sin_out, sums, *rest):
    cos_ref, sin_ref, copies = cos_out, sin_out, []
    if first:
        turned, packed, features = rest[0], rest[1:3], rest[3]
        coords_in, miller_in = coords, miller
        coords, miller, cos_ref, sin_ref, sems, table_sems = rest[4:]
        fetch = [
            pltpu.make_async_copy(coords_in, coords, sems.at[1]),
            pltpu.make_async_copy(miller_in, miller, sems.at[2]),
        ]
        load = pltpu.make_async_copy(source, features, sems.at[0])
        for copy in fetch + [load]:
            copy.start()
    else:
        turned, fetch = source, ()
    size = order.shape[1]
    natural = lax.broadcasted_iota(jnp.int32, (1024, size), 0)
    pick = jnp.where(natural == order[...], 1.0, 0.0).astype(BF16)
    for copy in fetch:
        copy.wait()
    number = miller[...].astype(F32)
    five = jnp.concatenate([number, number[0:2], jnp.zeros((3, 1024), F32)], axis=0).astype(BF16)
    placed = jnp.dot(five, pick, preferred_element_type=F32).astype(BF16)
    ones = jnp.ones((1, ATOMS), F32)

    for cell in range(CX * CY):
        rows_at = pl.ds(cell * ATOMS, ATOMS)
        ia, ib = cell // CY, cell % CY
        block = [coords[ia, d, ib : ib + 1, :].astype(F32) for d in range(3)]
        along = (place[0] * CX + ia).astype(F32) / 32.0
        across = (place[1] * CY + ib).astype(F32) / 64.0
        rows = jnp.concatenate(
            [
                block[0] / 32.0,
                block[1] / 64.0,
                block[2] / slab_depth,
                along * ones,
                across * ones,
                jnp.zeros((3, ATOMS), F32),
            ],
            axis=0,
        )
        at = rows.T.astype(BF16)
        for j in range(size // 256):
            lanes = slice(j * 256, (j + 1) * 256)
            angle = jnp.dot(at, placed[:, lanes], preferred_element_type=F32)
            r = angle - jnp.round(angle)
            s = r * r
            sine = SIN_COEF[3]
            cosine = COS_COEF[3]
            for a in (2, 1, 0):
                sine = sine * s + SIN_COEF[a]
                cosine = cosine * s + COS_COEF[a]
            sine = sine * r
            double = sine + sine
            cos_ref[rows_at, lanes] = (1.0 - double * sine).astype(BF16)
            sin_ref[rows_at, lanes] = (double * cosine).astype(BF16)

        if first:
            for i, (table, target) in enumerate(((cos_ref, cos_out), (sin_ref, sin_out))):
                copy = pltpu.make_async_copy(table.at[rows_at], target.at[rows_at], table_sems.at[i, cell])
                copy.start()
                copies.append(copy)

    if first:
        load.wait()
        turned[...] = features[...].astype(F32).T.astype(BF16)
        for cell in range(CX * CY):
            ia, ib = cell // CY, cell % CY
            packed[ia][ib, 0:ATOMS, :] = features[cell * ATOMS : (cell + 1) * ATOMS, :]
            rows = [coords[ia, d, ib : ib + 1, :].astype(F32) for d in range(3)]
            rows = jnp.concatenate(rows + [jnp.zeros((PACK - ATOMS - 3, ATOMS), F32)], axis=0).astype(BF16)
            packed[ia][ib, ATOMS:PACK, :] = jnp.concatenate([rows, jnp.zeros_like(rows)], axis=1)
    for col, table in ((0, cos_ref), (1, sin_ref)):
        total = jnp.dot(turned[...], table[...], preferred_element_type=F32)
        sums[:, col * WIDTH : (col + 1) * WIDTH] = total.T.astype(sums.dtype)
    for copy in copies:
        copy.wait()


def waves(place, coords, miller, order, source, first):
    vm = pl.BlockSpec(memory_space=VMEM)
    hbm = pl.BlockSpec(memory_space=pl.ANY)
    place_of = hbm if first else vm
    size = order.shape[1]
    out_shape = [
        (pltpu.MemorySpace.HBM if first else pltpu.MemorySpace.VMEM)((1024, size), BF16),
        (pltpu.MemorySpace.HBM if first else pltpu.MemorySpace.VMEM)((1024, size), BF16),
        jax.ShapeDtypeStruct((size, 2 * WIDTH), BF16 if first else F32),
    ]
    scratch = []
    if first:
        source, coords, miller = (
            pltpu.with_memory_space_constraint(value, pltpu.MemorySpace.HBM) for value in (source, coords, miller)
        )
        out_shape.append(jax.ShapeDtypeStruct((WIDTH, 1024), BF16))
        out_shape += [jax.ShapeDtypeStruct((CY, PACK, WIDTH), BF16)] * CX
        scratch = [VMEM((1024, WIDTH), BF16), VMEM(coords.shape, BF16), VMEM(miller.shape, jnp.int32)]
        scratch += [VMEM((1024, size), BF16)] * 2 + [pltpu.SemaphoreType.DMA((3,)), pltpu.SemaphoreType.DMA((2, CX * CY))]
    return pl.pallas_call(
        functools.partial(wave_kernel, first),
        out_shape=out_shape,
        in_specs=[pl.BlockSpec(memory_space=pltpu.SMEM), place_of, place_of, vm, place_of],
        out_specs=[place_of, place_of] + [vm] * (len(out_shape) - 2),
        scratch_shapes=scratch,
        compiler_params=pltpu.CompilerParams(vmem_limit_bytes=14 * 1024 * 1024),
        cost_estimate=pl.CostEstimate(flops=size * 4_000_000, bytes_accessed=3_000_000, transcendentals=0),
        name="wave_tables",
    )(place, coords, miller, order, source)


def prepare_kernel(place, near_count, sources, near_list, coords, live, mine, placement):
    row = lax.broadcasted_iota(jnp.int32, (CHUNK, 32), 0)
    at = lax.broadcasted_iota(jnp.int32, (CHUNK, 32), 1)
    core, x, z = place[1] % 2, place[0] // 4, place[0] % 4 + 4 * ((place[1] // 2) % 2)
    from_z = jnp.zeros((CHUNK, 32), jnp.int32)
    for b in range(8):
        from_z = jnp.where(at // 4 == b, sources[(core * 8 + z) * 8 + b], from_z)
    half = jnp.where(core == 0, x // 2, x % 2)
    member = (half ^ (at // 2 % 2)) * 8 + from_z
    placement[...] = jnp.where((row // 4 == member) & (row % 4 // 2 == at % 2), 1.0, 0.0)

    shape = (CX * CY, 9)
    cell = lax.broadcasted_iota(jnp.int32, shape, 0)
    slot = lax.broadcasted_iota(jnp.int32, shape, 1)
    entry = near_list[...]
    step_x = ((entry >> 6) - (place[0] * CX + cell // CY) + 1) & 31
    step_y = ((entry & 63) - (place[1] * CY + cell % CY) + 1) & 63
    count = jnp.zeros(shape, jnp.int32)
    for c in range(CX * CY):
        count = jnp.where(cell == c, near_count[c], count)
    code = jnp.where(slot < count, step_x * 3 + step_y, -1)
    for o in range(9):
        live[:, o : o + 1] = jnp.max(jnp.where(code == o, 1.0, 0.0), axis=1, keepdims=True)
    for c in range(CX * CY):
        ia, ib = c // CY, c % CY
        rows = [coords[ia, d, ib : ib + 1, :].astype(F32) for d in range(3)]
        columns = jnp.concatenate(rows + [jnp.zeros((5, ATOMS), F32)], axis=0).T
        for d in range(3):
            mine[c, d] = jnp.broadcast_to(columns[:, d : d + 1], (ATOMS, ATOMS))


def prepare(place, near_count, near_list, coords):
    sources = z_sources()
    vm = pl.BlockSpec(memory_space=VMEM)
    sm = pl.BlockSpec(memory_space=pltpu.SMEM)
    return pl.pallas_call(
        prepare_kernel,
        out_shape=(
            jax.ShapeDtypeStruct((CX * CY, 9), F32),
            jax.ShapeDtypeStruct((CX * CY, 3, ATOMS, ATOMS), F32),
            jax.ShapeDtypeStruct((CHUNK, 32), F32),
        ),
        in_specs=[sm, sm, sm, vm, vm],
        out_specs=(vm, vm, vm),
        compiler_params=pltpu.CompilerParams(vmem_limit_bytes=6 * 1024 * 1024),
        cost_estimate=pl.CostEstimate(flops=500_000_000, bytes_accessed=100_000, transcendentals=0),
        name="radial_prepare",
    )(place, near_count, sources, near_list, coords)


def radial_kernel(near_cells, fresh, rates, live, filters, mine, *rest):
    acc, scaled = rest[-2:]
    start = rest[-3]
    done = set()
    for i, ((na, nb), (source, at)) in enumerate(near_cells):
        cell_block = rest[source].at[at]
        values = cell_block[0:ATOMS, :]
        for k in range(8):
            scaled[i % 2, k * ATOMS : (k + 1) * ATOMS, :] = values * filters[k : k + 1, :]
        near = cell_block[ATOMS:PACK, 0:ATOMS].astype(F32)
        for ia in range(max(0, na - 1), min(CX, na + 2)):
            for ib in range(max(0, nb - 1), min(CY, nb + 2)):
                u, v = na - ia, nb - ib
                cell = ia * CY + ib
                dx = (near[0:1] + float(u)) - mine[cell, 0]
                dy = (near[1:2] + float(v)) - mine[cell, 1]
                dz = near[2:3] - mine[cell, 2]
                dist = dx * dx + dy * dy + dz * dz
                kernel = jnp.concatenate(
                    [jnp.exp2(dist * (rates[k] * -LOG2E)).astype(BF16) for k in range(8)], axis=1
                )
                o = (u + 1) * 3 + v + 1
                part = jnp.dot(kernel, scaled[i % 2], preferred_element_type=F32) * live[cell : cell + 1, o : o + 1]
                if cell in done:
                    acc[cell] += part
                elif fresh:
                    acc[cell] = part
                else:
                    acc[cell] = start[cell] + part
                done.add(cell)
    for cell in range(CX * CY):
        if cell not in done:
            acc[cell] = jnp.zeros((ATOMS, WIDTH), F32) if fresh else start[cell]


def radial_piece(near_cells, gammas, live, filters, mine, blocks, acc):
    vm = pl.BlockSpec(memory_space=VMEM)
    sm = pl.BlockSpec(memory_space=pltpu.SMEM)
    fresh = acc is None
    arrays = (gammas, live, filters, mine) + blocks + (() if fresh else (acc,))
    return pl.pallas_call(
        functools.partial(radial_kernel, near_cells, fresh),
        out_shape=jax.ShapeDtypeStruct((CX * CY, ATOMS, WIDTH), F32),
        in_specs=[sm] + [vm] * (len(arrays) - 1),
        out_specs=vm,
        scratch_shapes=[VMEM((2, 8 * ATOMS, WIDTH), BF16)],
        input_output_aliases={} if fresh else {len(arrays) - 1: 0},
        compiler_params=pltpu.CompilerParams(vmem_limit_bytes=10 * 1024 * 1024),
        cost_estimate=pl.CostEstimate(flops=2_000_000_000, bytes_accessed=2_000_000, transcendentals=0),
        name="radial_piece",
    )(*arrays)


def edge_kernel(along_x, which, sides, rates, live, filters, mine, block, start, acc, scaled):
    low_side = sides[which] < 0
    step = jnp.where(low_side, -1.0, 1.0)
    across = CY if along_x else CX
    totals = [None] * across
    places = []
    for own in range(across):
        at = (own, (CX - 1) * CY + own) if along_x else (own * CY, own * CY + CY - 1)
        places.append((at, jnp.where(low_side, at[0], at[1])))
    for i in range(CY if along_x else CX + 2):
        line = i if along_x else i - 1
        values = block[i, 0:ATOMS, :]
        for k in range(8):
            scaled[i % 2, k * ATOMS : (k + 1) * ATOMS, :] = values * filters[k : k + 1, :]
        near = block[i, ATOMS:PACK, 0:ATOMS].astype(F32)
        for own in range(max(0, line - 1), min(across, line + 2)):
            shift = line - own
            (cell_low, cell_high), cell = places[own]
            u, v = (step, float(shift)) if along_x else (float(shift), step)
            dx = (near[0:1] + u) - mine[cell, 0]
            dy = (near[1:2] + v) - mine[cell, 1]
            dz = near[2:3] - mine[cell, 2]
            dist = dx * dx + dy * dy + dz * dz
            kernel = jnp.concatenate([jnp.exp2(dist * (rates[k] * -LOG2E)).astype(BF16) for k in range(8)], axis=1)
            o_low, o_high = (shift + 1, 7 + shift) if along_x else (3 * shift + 3, 3 * shift + 5)
            weight = jnp.where(
                low_side,
                live[cell_low : cell_low + 1, o_low : o_low + 1],
                live[cell_high : cell_high + 1, o_high : o_high + 1],
            )
            part = jnp.dot(kernel, scaled[i % 2], preferred_element_type=F32) * weight
            totals[own] = part if totals[own] is None else totals[own] + part
            if line == min(across - 1 + (0 if along_x else 1), own + 1):
                acc[cell] = start[cell] + totals[own]
    for cell in range(CX * CY):
        at_low = cell < CY if along_x else cell % CY == 0
        at_high = cell >= CY if along_x else cell % CY == CY - 1
        if along_x:
            keep_it = jnp.logical_not(low_side) if at_low else low_side
        elif at_low:
            keep_it = jnp.logical_not(low_side)
        elif at_high:
            keep_it = low_side
        else:
            keep_it = None

        def keep_cell(cell=cell):
            acc[cell] = start[cell]

        if keep_it is None:
            keep_cell()
        else:
            pl.when(keep_it)(keep_cell)


def edge_piece(along_x, which, sides, gammas, live, filters, mine, block, acc):
    flops = 20_000_000_000
    vm = pl.BlockSpec(memory_space=VMEM)
    sm = pl.BlockSpec(memory_space=pltpu.SMEM)
    return pl.pallas_call(
        functools.partial(edge_kernel, along_x, which),
        out_shape=jax.ShapeDtypeStruct((CX * CY, ATOMS, WIDTH), F32),
        in_specs=[sm, sm] + [vm] * 5,
        out_specs=vm,
        scratch_shapes=[VMEM((2, 8 * ATOMS, WIDTH), BF16)],
        input_output_aliases={6: 0},
        compiler_params=pltpu.CompilerParams(vmem_limit_bytes=10 * 1024 * 1024),
        cost_estimate=pl.CostEstimate(flops=flops, bytes_accessed=2_000_000, transcendentals=0),
        name="radial_edge",
    )(sides, gammas, live, filters, mine, block, acc)


def coefficient_kernel(total, rows, fresh, placement, out):
    gathered = jnp.concatenate([rows[...], fresh[CHUNK:, :]], axis=0)
    placed = jnp.dot(placement[...].astype(BF16), gathered, preferred_element_type=F32)
    odd = lax.broadcasted_iota(jnp.int32, (CHUNK, WIDTH), 0) % 2 == 1
    scale = jnp.where(odd, placed[:, WIDTH:], placed[:, :WIDTH])
    sums = total[...] + fresh[0:CHUNK, :].astype(F32)
    out[:, :WIDTH] = (sums[:, :WIDTH] * scale).astype(BF16)
    out[:, WIDTH:] = (sums[:, WIDTH:] * scale).astype(BF16)


def coefficients(total, rows, fresh, placement):
    vm = pl.BlockSpec(memory_space=VMEM)
    return pl.pallas_call(
        coefficient_kernel,
        out_shape=jax.ShapeDtypeStruct((CHUNK, 2 * WIDTH), BF16),
        in_specs=[vm] * 4,
        out_specs=vm,
        compiler_params=pltpu.CompilerParams(vmem_limit_bytes=4 * 1024 * 1024),
        cost_estimate=pl.CostEstimate(flops=100_000_000, bytes_accessed=200_000, transcendentals=0),
        name="coefficients",
    )(total, rows, fresh, placement)


def recip_kernel(spots, *refs):
    coef, start, acc = refs[-3:]
    for row in range(4):
        rows = slice(row * 256, row * 256 + 256)
        total = start[rows]
        for i, (column, at) in enumerate(spots):
            lanes, span = slice(column, column + 128), slice(at, at + 128)
            total += jnp.dot(refs[2 * i][rows, lanes], coef[span, 0:WIDTH], preferred_element_type=F32)
            total += jnp.dot(refs[2 * i + 1][rows, lanes], coef[span, WIDTH:], preferred_element_type=F32)
        acc[rows] = total


def recip_piece(parts, far, coef, acc):
    vm = pl.BlockSpec(memory_space=VMEM)
    tables = [table for part in parts for table in part[:2]] + list(far)
    return pl.pallas_call(
        functools.partial(recip_kernel, tuple(part[2:] for part in parts)),
        out_shape=jax.ShapeDtypeStruct((1024, WIDTH), F32),
        in_specs=[vm] * (len(tables) + 2),
        out_specs=vm,
        input_output_aliases={len(tables) + 1: 0},
        compiler_params=pltpu.CompilerParams(vmem_limit_bytes=10 * 1024 * 1024),
        cost_estimate=pl.CostEstimate(flops=10_000_000_000, bytes_accessed=2_000_000, transcendentals=0),
        name="recip_piece",
    )(*tables, coef, acc)


def final_kernel(cos_ref, sin_ref, coef_in, upper, lower, acc, gain, w_in, w_out, out, coef, result, sems):
    for block, source in enumerate((0, 2, 1, 3)):
        coef[block * 128 : block * 128 + 128, :] = coef_in[source * 128 : source * 128 + 128, :]
    copies = []
    for block in range(4):
        rows = pl.ds(block * 256, 256)
        recip = jnp.dot(cos_ref[rows, :], coef[:, 0:WIDTH], preferred_element_type=F32)
        recip += jnp.dot(sin_ref[rows, :], coef[:, WIDTH:], preferred_element_type=F32)
        cells = (upper, lower)[block // 2]
        features = jnp.concatenate([cells[block % 2 * 2 + i, 0:ATOMS, :] for i in range(2)], axis=0)
        mixed = features.astype(F32) + acc[rows, :] + recip
        power = jnp.mean(mixed * mixed, axis=-1, keepdims=True)
        normed = (mixed * lax.rsqrt(power + epsilon) * gain[...]).astype(BF16)
        v = jnp.dot(normed, w_in[...], preferred_element_type=F32)
        hidden = (v / (1.0 + jnp.exp(-v))).astype(BF16)
        result[rows, :] = (mixed + jnp.dot(hidden, w_out[...], preferred_element_type=F32)).astype(BF16)
        copy = pltpu.make_async_copy(result.at[rows], out.at[rows], sems.at[block])
        copy.start()
        copies.append(copy)
    for copy in copies:
        copy.wait()


def final(cos_table, sin_table, coef, upper, lower, acc, gain, w_in, w_out):
    whole = pl.BlockSpec(memory_space=VMEM)
    return pl.pallas_call(
        final_kernel,
        out_shape=pltpu.MemorySpace.HBM((1024, WIDTH), BF16),
        in_specs=[whole] * 9,
        out_specs=pl.BlockSpec(memory_space=pl.ANY),
        scratch_shapes=[VMEM((HALF, 2 * WIDTH), BF16), VMEM((1024, WIDTH), BF16), pltpu.SemaphoreType.DMA((4,))],
        compiler_params=pltpu.CompilerParams(vmem_limit_bytes=14 * 1024 * 1024),
        cost_estimate=pl.CostEstimate(flops=3_000_000_000, bytes_accessed=8_000_000, transcendentals=0),
        name="mix_and_network",
    )(cos_table, sin_table, coef, upper, lower, acc, gain, w_in, w_out)


def row_pairs(first):
    def other(gx):
        return (gx + 1) % 16 if (gx % 2 == 0) == first else (gx - 1) % 16

    return [(i, other(i)) for i in range(16)]


def column_pairs(first):
    return row_pairs(first)


def first_blocks(rows):
    return jnp.concatenate([rows[0:64], rows[128:192]], axis=0)


def second_blocks(rows):
    return jnp.concatenate([rows[64:128], rows[192:256]], axis=0)


def per_device(
    features,
    coords,
    nbr_cells,
    nbr_count,
    miller,
    gammas,
    radial_filter,
    reciprocal_filter,
    norm_gain,
    w_in,
    w_out,
):
    gx, gy = lax.axis_index("gx"), lax.axis_index("gy")
    place = jnp.stack([gx, gy]).astype(jnp.int32)
    own_rows = features.reshape(1024, WIDTH)
    turned = coords.transpose(0, 2, 1, 3)
    order = vector_order()
    barrier = lax.optimization_barrier

    cos_far, sin_far, send, across, upper, lower = waves(place, turned, miller, order[:, HALF:], own_rows, True)
    got = permute(send, HALVING[0])
    even_x, even_y = gx % 2 == 0, gy % 2 == 0
    sides = jnp.stack(
        [jnp.where(even_x, 1, -1), jnp.where(even_x, -1, 1), jnp.where(even_y, 1, -1), jnp.where(even_y, -1, 1)]
    ).astype(jnp.int32)
    row_a = lax.ppermute(jnp.where(even_x, lower, upper), "gx", row_pairs(True))
    row_b = lax.ppermute(jnp.where(even_x, upper, lower), "gx", row_pairs(False))
    cos_next, sin_next, keep_next = waves(place, turned, miller, order[:, 256:HALF], across, False)

    acc = None

    def own_piece(jb, acc):
        near_cells = tuple(((ja, jb), (ja, jb)) for ja in range(CX))
        return radial_piece(near_cells, gammas, live, radial_filter, mine, (upper, lower), acc)

    def beyond(along_x, which, block, acc):
        return edge_piece(along_x, which, sides, gammas, live, radial_filter, mine, block, acc)

    for step, height in ((1, 256), (2, 128), (3, 64)):
        if step == 2:
            send = (second_blocks(keep) + second_blocks(got).astype(F32)).astype(BF16)
        else:
            send = ((keep_next if step == 1 else keep[height:]) + got[height:].astype(F32)).astype(BF16)
        if step == 2:
            send, live, mine, placement = barrier((send, live, mine, placement))
        elif step == 3:
            send, acc = barrier((send, acc))
        fresh = permute(send, HALVING[step])
        if step == 1:
            across, place, send = barrier((across, place, send))
            cos_near, sin_near, keep = waves(place, turned, miller, order[:, :256], across, False)
            live, mine, placement = prepare(place, nbr_count.reshape(8), nbr_cells.reshape(8, 9), turned)
        else:
            acc = own_piece(step - 2, acc)
        if step == 2:
            keep = first_blocks(keep) + first_blocks(got).astype(F32)
        else:
            keep = keep[:height] + got[:height].astype(F32)
        got = fresh
    total = keep + got.astype(F32)
    rows = reciprocal_filter.reshape(2, 2 * WIDTH)
    for step in range(4):
        total, acc = barrier((total, acc))
        fresh = permute(jnp.concatenate([total.astype(BF16), rows], axis=0), DOUBLING[step])
        if step < 2:
            acc = own_piece(step + 2, acc)
        else:
            acc = beyond(True, step - 2, row_a if step == 2 else row_b, acc)
        if step < 3:
            total = total + fresh[:CHUNK].astype(F32)
            rows = jnp.concatenate([rows, fresh[CHUNK:]], axis=0)
    chunk = coefficients(total, rows, fresh, placement)
    chunk, row_a, row_b = barrier((chunk, row_a, row_b))
    for turn, step in enumerate((2, 1, 3, 0)):
        chunk, acc = barrier((chunk, acc))
        fresh = permute(chunk, HALVING[step])
        if turn == 0:
            ends = [
                (jnp.where(even_x, row_b[b : b + 1], row_a[b : b + 1]), jnp.where(even_x, row_a[b : b + 1], row_b[b : b + 1]))
                for b in (0, CY - 1)
            ]
            left, right = (
                jnp.concatenate([low, upper[b : b + 1], lower[b : b + 1], high], axis=0)
                for b, (low, high) in zip((0, CY - 1), ends)
            )
            far_send, near_send = jnp.where(even_y, left, right), jnp.where(even_y, right, left)
            column_b = lax.ppermute(far_send, "gy", column_pairs(False))
        elif turn == 1:
            near_send, chunk = barrier((near_send, chunk))
            column_a = lax.ppermute(near_send, "gy", column_pairs(True))
        elif turn == 2:
            acc = beyond(False, 2, column_a, acc)
        elif turn == 3:
            acc = beyond(False, 3, column_b, acc)
        parts = (
            (),
            ((cos_near, sin_near, 0, 0),),
            ((cos_next, sin_next, 0, 128),),
            ((cos_near, sin_near, 128, 256), (cos_next, sin_next, 128, 384)),
        )[turn]
        if parts:
            far = (cos_far, sin_far, w_in, w_out) if turn > 1 else ()
            acc = recip_piece(parts, far, chunk, acc.reshape(1024, WIDTH)).reshape(CX * CY, ATOMS, WIDTH)
        if step:
            chunk = jnp.concatenate([chunk, fresh], axis=0)
    acc = acc.reshape(1024, WIDTH)

    out = final(
        cos_far, sin_far, fresh, upper, lower, acc, norm_gain.reshape(1, WIDTH), w_in, w_out
    )
    return out.reshape(CX, CY, ATOMS, WIDTH)


def solution(mesh):
    in_specs = (
        P("gx", "gy", None, None),
        P("gx", "gy", None, None),
        P("gx", "gy", None),
        P("gx", "gy"),
        P(),
        P(),
        P(),
        P(("gx", "gy"), None),
        P(),
        P(),
        P(),
    )
    out_specs = P("gx", "gy", None, None)
    return jax.shard_map(
        per_device, mesh=mesh, in_specs=in_specs, out_specs=out_specs, check_vma=False
    )
```

```python
import functools

import jax
import jax.numpy as jnp
from jax import lax
from jax.experimental import pallas as pl
from jax.experimental.pallas import tpu as pltpu
from jax.sharding import PartitionSpec as P

slab_depth = 2.0
epsilon = 1e-06
LOG2E = 1.4426950408889634
AXES = ("gx", "gy")
F32 = jnp.float32
BF16 = jnp.bfloat16
CX, CY, ATOMS, WIDTH = 2, 4, 128, 256
PACK = 144
VMEM = pltpu.VMEM

SIN_COEF = (3.14159027, -5.16740673, 2.54401052, -0.55946246)
COS_COEF = (0.99999325, -4.93393467, 4.0412481, -1.22203176)


def linear(x, y, z, core):
    return (x * 4 + z % 4) * 16 + y * 4 + (z // 4) * 2 + core


def partner_list(step):
    pairs = []
    for x in range(4):
        for y in range(4):
            for z in range(8):
                for core in range(2):
                    pairs.append((linear(x, y, z, core), linear(*step(x, y, z, core))))
    return pairs


def flip_core(x, y, z, core):
    return x, y, z, 1 - core


def flip_x(first, second):
    def step(x, y, z, core):
        return x ^ (second if core else first), y, z, core

    return step


def flip_y(first, second):
    def step(x, y, z, core):
        return x, y ^ (second if core else first), z, core

    return step


def flip_z(which):
    table = ((1, 0, 3, 2, 5, 4, 7, 6), (7, 2, 1, 4, 3, 6, 5, 0), (3, 6, 5, 0, 7, 2, 1, 4))[which]

    def step(x, y, z, core):
        return x, y, table[z] if core == 0 else (table[(z - 1) % 8] + 1) % 8, core

    return step


HALVING = (flip_core, flip_y(1, 3), flip_y(3, 1), flip_x(1, 3))
DOUBLING = (flip_x(3, 1), flip_z(0), flip_z(1), flip_z(2))
CHUNK = 64


def permute(value, step):
    return lax.ppermute(value, AXES, partner_list(step))


def my_place():
    gx, gy = lax.axis_index("gx"), lax.axis_index("gy")
    return gx // 4, gy // 4, (gx % 4) + 4 * ((gy // 2) % 2), gy % 2


def vector_order():
    x, y, z, core = my_place()
    pos = lax.broadcasted_iota(jnp.int32, (1, 1024), 1)
    rest = pos % 4
    mz = (pos // 4) % 8
    mb = (pos // 32) % 2
    b2 = (pos // 64) % 2
    b3 = (pos // 128) % 2
    b1 = (pos // 256) % 2
    owner = core ^ (pos // 512)
    oy = y ^ jnp.where(owner == 0, b1 ^ (3 * b2), (3 * b1) ^ b2)
    coset = jnp.where(owner == 0, (x ^ (x >> 1)) & 1, x >> 1) ^ b3
    ox = jnp.where(owner == 0, coset ^ (3 * mb), 2 * coset + mb)
    return linear(ox, oy, mz, owner) * 4 + rest


HALF = 512


def wave_kernel(first, place, coords, miller, order, source, cos_out, sin_out, sums, *rest):
    cos_ref, sin_ref, copies = cos_out, sin_out, []
    if first:
        turned, packed, features = rest[0], rest[1:3], rest[3]
        coords_in, miller_in = coords, miller
        coords, miller, cos_ref, sin_ref, sems, table_sems = rest[4:]
        fetch = [
            pltpu.make_async_copy(coords_in, coords, sems.at[1]),
            pltpu.make_async_copy(miller_in, miller, sems.at[2]),
        ]
        load = pltpu.make_async_copy(source, features, sems.at[0])
        for copy in fetch + [load]:
            copy.start()
    else:
        turned, fetch = source, ()
    size = order.shape[1]
    natural = lax.broadcasted_iota(jnp.int32, (1024, size), 0)
    pick = jnp.where(natural == order[...], 1.0, 0.0).astype(BF16)
    for copy in fetch:
        copy.wait()
    number = miller[...].astype(F32)
    five = jnp.concatenate([number, number[0:2], jnp.zeros((3, 1024), F32)], axis=0).astype(BF16)
    placed = jnp.dot(five, pick, preferred_element_type=F32).astype(BF16)
    ones = jnp.ones((1, ATOMS), F32)

    for cell in range(CX * CY):
        rows_at = pl.ds(cell * ATOMS, ATOMS)
        ia, ib = cell // CY, cell % CY
        block = [coords[ia, d, ib : ib + 1, :].astype(F32) for d in range(3)]
        along = (place[0] * CX + ia).astype(F32) / 32.0
        across = (place[1] * CY + ib).astype(F32) / 64.0
        rows = jnp.concatenate(
            [
                block[0] / 32.0,
                block[1] / 64.0,
                block[2] / slab_depth,
                along * ones,
                across * ones,
                jnp.zeros((3, ATOMS), F32),
            ],
            axis=0,
        )
        at = rows.T.astype(BF16)
        for j in range(size // 256):
            lanes = slice(j * 256, (j + 1) * 256)
            angle = jnp.dot(at, placed[:, lanes], preferred_element_type=F32)
            r = angle - jnp.round(angle)
            s = r * r
            sine = SIN_COEF[3]
            cosine = COS_COEF[3]
            for a in (2, 1, 0):
                sine = sine * s + SIN_COEF[a]
                cosine = cosine * s + COS_COEF[a]
            sine = sine * r
            double = sine + sine
            cos_ref[rows_at, lanes] = (1.0 - double * sine).astype(BF16)
            sin_ref[rows_at, lanes] = (double * cosine).astype(BF16)

        if first:
            for i, (table, target) in enumerate(((cos_ref, cos_out), (sin_ref, sin_out))):
                copy = pltpu.make_async_copy(table.at[rows_at], target.at[rows_at], table_sems.at[i, cell])
                copy.start()
                copies.append(copy)

    if first:
        load.wait()
        turned[...] = features[...].astype(F32).T.astype(BF16)
        for cell in range(CX * CY):
            ia, ib = cell // CY, cell % CY
            packed[ia][ib, 0:ATOMS, :] = features[cell * ATOMS : (cell + 1) * ATOMS, :]
            rows = [coords[ia, d, ib : ib + 1, :].astype(F32) for d in range(3)]
            rows = jnp.concatenate(rows + [jnp.zeros((PACK - ATOMS - 3, ATOMS), F32)], axis=0).astype(BF16)
            packed[ia][ib, ATOMS:PACK, :] = jnp.concatenate([rows, jnp.zeros_like(rows)], axis=1)
    for col, table in ((0, cos_ref), (1, sin_ref)):
        total = jnp.dot(turned[...], table[...], preferred_element_type=F32)
        sums[:, col * WIDTH : (col + 1) * WIDTH] = total.T.astype(sums.dtype)
    for copy in copies:
        copy.wait()


def waves(place, coords, miller, order, source, first):
    vm = pl.BlockSpec(memory_space=VMEM)
    hbm = pl.BlockSpec(memory_space=pl.ANY)
    place_of = hbm if first else vm
    size = order.shape[1]
    out_shape = [
        (pltpu.MemorySpace.HBM if first else pltpu.MemorySpace.VMEM)((1024, size), BF16),
        (pltpu.MemorySpace.HBM if first else pltpu.MemorySpace.VMEM)((1024, size), BF16),
        jax.ShapeDtypeStruct((size, 2 * WIDTH), BF16 if first else F32),
    ]
    scratch = []
    if first:
        source, coords, miller = (
            pltpu.with_memory_space_constraint(value, pltpu.MemorySpace.HBM) for value in (source, coords, miller)
        )
        out_shape.append(jax.ShapeDtypeStruct((WIDTH, 1024), BF16))
        out_shape += [jax.ShapeDtypeStruct((CY, PACK, WIDTH), BF16)] * CX
        scratch = [VMEM((1024, WIDTH), BF16), VMEM(coords.shape, BF16), VMEM(miller.shape, jnp.int32)]
        scratch += [VMEM((1024, size), BF16)] * 2 + [pltpu.SemaphoreType.DMA((3,)), pltpu.SemaphoreType.DMA((2, CX * CY))]
    return pl.pallas_call(
        functools.partial(wave_kernel, first),
        out_shape=out_shape,
        in_specs=[pl.BlockSpec(memory_space=pltpu.SMEM), place_of, place_of, vm, place_of],
        out_specs=[place_of, place_of] + [vm] * (len(out_shape) - 2),
        scratch_shapes=scratch,
        compiler_params=pltpu.CompilerParams(vmem_limit_bytes=14 * 1024 * 1024),
        cost_estimate=pl.CostEstimate(flops=size * 4_000_000, bytes_accessed=3_000_000, transcendentals=0),
        name="wave_tables",
    )(place, coords, miller, order, source)


def prepare_kernel(place, near_count, near_list, coords, row_filter, live, mine, filters):
    shape = (CX * CY, 9)
    cell = lax.broadcasted_iota(jnp.int32, shape, 0)
    slot = lax.broadcasted_iota(jnp.int32, shape, 1)
    entry = near_list[...]
    step_x = ((entry >> 6) - (place[0] * CX + cell // CY) + 1) & 31
    step_y = ((entry & 63) - (place[1] * CY + cell % CY) + 1) & 63
    count = jnp.zeros(shape, jnp.int32)
    for c in range(CX * CY):
        count = jnp.where(cell == c, near_count[c], count)
    code = jnp.where(slot < count, step_x * 3 + step_y, -1)
    for o in range(9):
        live[:, o : o + 1] = jnp.max(jnp.where(code == o, 1.0, 0.0), axis=1, keepdims=True)
    for c in range(CX * CY):
        ia, ib = c // CY, c % CY
        rows = [coords[ia, d, ib : ib + 1, :].astype(F32) for d in range(3)]
        columns = jnp.concatenate(rows + [jnp.zeros((5, ATOMS), F32)], axis=0).T
        for d in range(3):
            mine[c, d] = jnp.broadcast_to(columns[:, d : d + 1], (ATOMS, ATOMS))
    x, z = place[0] // 4, place[0] % 4 + 4 * ((place[1] // 2) % 2)
    member = jnp.where(place[1] % 2 == 0, x // 2, x % 2) * 8 + z
    whole = jnp.concatenate([row_filter[...].astype(F32)] * (CHUNK // 4), axis=0)
    slots = lax.broadcasted_iota(jnp.int32, (CHUNK, WIDTH), 0) // 4
    filters[...] = jnp.where(slots == member, whole, 0.0)


def prepare(place, near_count, near_list, coords, row_filter):
    vm = pl.BlockSpec(memory_space=VMEM)
    sm = pl.BlockSpec(memory_space=pltpu.SMEM)
    return pl.pallas_call(
        prepare_kernel,
        out_shape=(
            jax.ShapeDtypeStruct((CX * CY, 9), F32),
            jax.ShapeDtypeStruct((CX * CY, 3, ATOMS, ATOMS), F32),
            jax.ShapeDtypeStruct((CHUNK, WIDTH), F32),
        ),
        in_specs=[sm, sm, vm, vm, vm],
        out_specs=(vm, vm, vm),
        compiler_params=pltpu.CompilerParams(vmem_limit_bytes=6 * 1024 * 1024),
        cost_estimate=pl.CostEstimate(flops=500_000_000, bytes_accessed=100_000, transcendentals=0),
        name="radial_prepare",
    )(place, near_count, near_list, coords, row_filter)


def radial_kernel(near_cells, fresh, rates, live, filters, mine, *rest):
    acc, scaled = rest[-2:]
    start = rest[-3]
    done = set()
    for i, ((na, nb), (source, at)) in enumerate(near_cells):
        cell_block = rest[source].at[at]
        values = cell_block[0:ATOMS, :]
        for k in range(8):
            scaled[i % 2, k * ATOMS : (k + 1) * ATOMS, :] = values * filters[k : k + 1, :]
        near = cell_block[ATOMS:PACK, 0:ATOMS].astype(F32)
        for ia in range(max(0, na - 1), min(CX, na + 2)):
            for ib in range(max(0, nb - 1), min(CY, nb + 2)):
                u, v = na - ia, nb - ib
                cell = ia * CY + ib
                dx = (near[0:1] + float(u)) - mine[cell, 0]
                dy = (near[1:2] + float(v)) - mine[cell, 1]
                dz = near[2:3] - mine[cell, 2]
                dist = dx * dx + dy * dy + dz * dz
                kernel = jnp.concatenate(
                    [jnp.exp2(dist * (rates[k] * -LOG2E)).astype(BF16) for k in range(8)], axis=1
                )
                o = (u + 1) * 3 + v + 1
                part = jnp.dot(kernel, scaled[i % 2], preferred_element_type=F32) * live[cell : cell + 1, o : o + 1]
                if cell in done:
                    acc[cell] += part
                elif fresh:
                    acc[cell] = part
                else:
                    acc[cell] = start[cell] + part
                done.add(cell)
    for cell in range(CX * CY):
        if cell not in done:
            acc[cell] = jnp.zeros((ATOMS, WIDTH), F32) if fresh else start[cell]


def radial_piece(near_cells, gammas, live, filters, mine, blocks, acc):
    vm = pl.BlockSpec(memory_space=VMEM)
    sm = pl.BlockSpec(memory_space=pltpu.SMEM)
    fresh = acc is None
    arrays = (gammas, live, filters, mine) + blocks + (() if fresh else (acc,))
    return pl.pallas_call(
        functools.partial(radial_kernel, near_cells, fresh),
        out_shape=jax.ShapeDtypeStruct((CX * CY, ATOMS, WIDTH), F32),
        in_specs=[sm] + [vm] * (len(arrays) - 1),
        out_specs=vm,
        scratch_shapes=[VMEM((2, 8 * ATOMS, WIDTH), BF16)],
        input_output_aliases={} if fresh else {len(arrays) - 1: 0},
        compiler_params=pltpu.CompilerParams(vmem_limit_bytes=10 * 1024 * 1024),
        cost_estimate=pl.CostEstimate(flops=2_000_000_000, bytes_accessed=2_000_000, transcendentals=0),
        name="radial_piece",
    )(*arrays)


def edge_kernel(along_x, which, sides, rates, live, filters, mine, block, start, acc, scaled):
    low_side = sides[which] < 0
    step = jnp.where(low_side, -1.0, 1.0)
    across = CY if along_x else CX
    totals = [None] * across
    places = []
    for own in range(across):
        at = (own, (CX - 1) * CY + own) if along_x else (own * CY, own * CY + CY - 1)
        places.append((at, jnp.where(low_side, at[0], at[1])))
    for i in range(CY if along_x else CX + 2):
        line = i if along_x else i - 1
        values = block[i, 0:ATOMS, :]
        for k in range(8):
            scaled[i % 2, k * ATOMS : (k + 1) * ATOMS, :] = values * filters[k : k + 1, :]
        near = block[i, ATOMS:PACK, 0:ATOMS].astype(F32)
        for own in range(max(0, line - 1), min(across, line + 2)):
            shift = line - own
            (cell_low, cell_high), cell = places[own]
            u, v = (step, float(shift)) if along_x else (float(shift), step)
            dx = (near[0:1] + u) - mine[cell, 0]
            dy = (near[1:2] + v) - mine[cell, 1]
            dz = near[2:3] - mine[cell, 2]
            dist = dx * dx + dy * dy + dz * dz
            kernel = jnp.concatenate([jnp.exp2(dist * (rates[k] * -LOG2E)).astype(BF16) for k in range(8)], axis=1)
            o_low, o_high = (shift + 1, 7 + shift) if along_x else (3 * shift + 3, 3 * shift + 5)
            weight = jnp.where(
                low_side,
                live[cell_low : cell_low + 1, o_low : o_low + 1],
                live[cell_high : cell_high + 1, o_high : o_high + 1],
            )
            part = jnp.dot(kernel, scaled[i % 2], preferred_element_type=F32) * weight
            totals[own] = part if totals[own] is None else totals[own] + part
            if line == min(across - 1 + (0 if along_x else 1), own + 1):
                acc[cell] = start[cell] + totals[own]
    for cell in range(CX * CY):
        at_low = cell < CY if along_x else cell % CY == 0
        at_high = cell >= CY if along_x else cell % CY == CY - 1
        if along_x:
            keep_it = jnp.logical_not(low_side) if at_low else low_side
        elif at_low:
            keep_it = jnp.logical_not(low_side)
        elif at_high:
            keep_it = low_side
        else:
            keep_it = None

        def keep_cell(cell=cell):
            acc[cell] = start[cell]

        if keep_it is None:
            keep_cell()
        else:
            pl.when(keep_it)(keep_cell)


def edge_piece(along_x, which, sides, gammas, live, filters, mine, block, acc):
    flops = 20_000_000_000
    vm = pl.BlockSpec(memory_space=VMEM)
    sm = pl.BlockSpec(memory_space=pltpu.SMEM)
    return pl.pallas_call(
        functools.partial(edge_kernel, along_x, which),
        out_shape=jax.ShapeDtypeStruct((CX * CY, ATOMS, WIDTH), F32),
        in_specs=[sm, sm] + [vm] * 5,
        out_specs=vm,
        scratch_shapes=[VMEM((2, 8 * ATOMS, WIDTH), BF16)],
        input_output_aliases={6: 0},
        compiler_params=pltpu.CompilerParams(vmem_limit_bytes=10 * 1024 * 1024),
        cost_estimate=pl.CostEstimate(flops=flops, bytes_accessed=2_000_000, transcendentals=0),
        name="radial_edge",
    )(sides, gammas, live, filters, mine, block, acc)


def recip_kernel(spots, *refs):
    coef, start, acc = refs[-3:]
    for row in range(4):
        rows = slice(row * 256, row * 256 + 256)
        total = start[rows]
        for i, (column, at) in enumerate(spots):
            lanes, span = slice(column, column + 128), slice(at, at + 128)
            total += jnp.dot(refs[2 * i][rows, lanes], coef[span, 0:WIDTH], preferred_element_type=F32)
            total += jnp.dot(refs[2 * i + 1][rows, lanes], coef[span, WIDTH:], preferred_element_type=F32)
        acc[rows] = total


def recip_piece(parts, far, coef, acc):
    vm = pl.BlockSpec(memory_space=VMEM)
    tables = [table for part in parts for table in part[:2]] + list(far)
    return pl.pallas_call(
        functools.partial(recip_kernel, tuple(part[2:] for part in parts)),
        out_shape=jax.ShapeDtypeStruct((1024, WIDTH), F32),
        in_specs=[vm] * (len(tables) + 2),
        out_specs=vm,
        input_output_aliases={len(tables) + 1: 0},
        compiler_params=pltpu.CompilerParams(vmem_limit_bytes=10 * 1024 * 1024),
        cost_estimate=pl.CostEstimate(flops=10_000_000_000, bytes_accessed=2_000_000, transcendentals=0),
        name="recip_piece",
    )(*tables, coef, acc)


def final_kernel(cos_ref, sin_ref, coef_in, upper, lower, acc, gain, w_in, w_out, out, coef, result, sems):
    for block, source in enumerate((0, 2, 1, 3)):
        coef[block * 128 : block * 128 + 128, :] = coef_in[source * 128 : source * 128 + 128, :]
    copies = []
    for block in range(4):
        rows = pl.ds(block * 256, 256)
        recip = jnp.dot(cos_ref[rows, :], coef[:, 0:WIDTH], preferred_element_type=F32)
        recip += jnp.dot(sin_ref[rows, :], coef[:, WIDTH:], preferred_element_type=F32)
        cells = (upper, lower)[block // 2]
        features = jnp.concatenate([cells[block % 2 * 2 + i, 0:ATOMS, :] for i in range(2)], axis=0)
        mixed = features.astype(F32) + acc[rows, :] + recip
        power = jnp.mean(mixed * mixed, axis=-1, keepdims=True)
        normed = (mixed * lax.rsqrt(power + epsilon) * gain[...]).astype(BF16)
        v = jnp.dot(normed, w_in[...], preferred_element_type=F32)
        hidden = (v / (1.0 + jnp.exp(-v))).astype(BF16)
        result[rows, :] = (mixed + jnp.dot(hidden, w_out[...], preferred_element_type=F32)).astype(BF16)
        copy = pltpu.make_async_copy(result.at[rows], out.at[rows], sems.at[block])
        copy.start()
        copies.append(copy)
    for copy in copies:
        copy.wait()


def final(cos_table, sin_table, coef, upper, lower, acc, gain, w_in, w_out):
    whole = pl.BlockSpec(memory_space=VMEM)
    return pl.pallas_call(
        final_kernel,
        out_shape=pltpu.MemorySpace.HBM((1024, WIDTH), BF16),
        in_specs=[whole] * 9,
        out_specs=pl.BlockSpec(memory_space=pl.ANY),
        scratch_shapes=[VMEM((HALF, 2 * WIDTH), BF16), VMEM((1024, WIDTH), BF16), pltpu.SemaphoreType.DMA((4,))],
        compiler_params=pltpu.CompilerParams(vmem_limit_bytes=14 * 1024 * 1024),
        cost_estimate=pl.CostEstimate(flops=3_000_000_000, bytes_accessed=8_000_000, transcendentals=0),
        name="mix_and_network",
    )(cos_table, sin_table, coef, upper, lower, acc, gain, w_in, w_out)


def row_pairs(first):
    def other(gx):
        return (gx + 1) % 16 if (gx % 2 == 0) == first else (gx - 1) % 16

    return [(i, other(i)) for i in range(16)]


def column_pairs(first):
    return row_pairs(first)


def first_blocks(rows):
    return jnp.concatenate([rows[0:64], rows[128:192]], axis=0)


def second_blocks(rows):
    return jnp.concatenate([rows[64:128], rows[192:256]], axis=0)


def per_device(
    features,
    coords,
    nbr_cells,
    nbr_count,
    miller,
    gammas,
    radial_filter,
    reciprocal_filter,
    norm_gain,
    w_in,
    w_out,
):
    gx, gy = lax.axis_index("gx"), lax.axis_index("gy")
    place = jnp.stack([gx, gy]).astype(jnp.int32)
    own_rows = features.reshape(1024, WIDTH)
    turned = coords.transpose(0, 2, 1, 3)
    order = vector_order()
    barrier = lax.optimization_barrier

    cos_far, sin_far, send, across, upper, lower = waves(place, turned, miller, order[:, HALF:], own_rows, True)
    got = permute(send, HALVING[0])
    even_x, even_y = gx % 2 == 0, gy % 2 == 0
    sides = jnp.stack(
        [jnp.where(even_x, 1, -1), jnp.where(even_x, -1, 1), jnp.where(even_y, 1, -1), jnp.where(even_y, -1, 1)]
    ).astype(jnp.int32)
    row_a = lax.ppermute(jnp.where(even_x, lower, upper), "gx", row_pairs(True))
    row_b = lax.ppermute(jnp.where(even_x, upper, lower), "gx", row_pairs(False))
    cos_next, sin_next, keep_next = waves(place, turned, miller, order[:, 256:HALF], across, False)

    acc = None

    def own_piece(jb, acc):
        near_cells = tuple(((ja, jb), (ja, jb)) for ja in range(CX))
        return radial_piece(near_cells, gammas, live, radial_filter, mine, (upper, lower), acc)

    def beyond(along_x, which, block, acc):
        return edge_piece(along_x, which, sides, gammas, live, radial_filter, mine, block, acc)

    for step, height in ((1, 256), (2, 128), (3, 64)):
        if step == 2:
            send = (second_blocks(keep) + second_blocks(got).astype(F32)).astype(BF16)
        else:
            send = ((keep_next if step == 1 else keep[height:]) + got[height:].astype(F32)).astype(BF16)
        if step == 2:
            send, live, mine, filters = barrier((send, live, mine, filters))
        elif step == 3:
            send, acc = barrier((send, acc))
        fresh = permute(send, HALVING[step])
        if step == 1:
            across, place, send = barrier((across, place, send))
            cos_near, sin_near, keep = waves(place, turned, miller, order[:, :256], across, False)
            live, mine, filters = prepare(
                place, nbr_count.reshape(8), nbr_cells.reshape(8, 9), turned, reciprocal_filter
            )
        else:
            acc = own_piece(step - 2, acc)
        if step == 2:
            keep = first_blocks(keep) + first_blocks(got).astype(F32)
        else:
            keep = keep[:height] + got[:height].astype(F32)
        got = fresh
    total = jnp.concatenate([keep + got.astype(F32), filters], axis=1)
    for step in range(4):
        total, acc = barrier((total, acc))
        fresh = permute(total.astype(BF16), DOUBLING[step])
        if step < 2:
            acc = own_piece(step + 2, acc)
        else:
            acc = beyond(True, step - 2, row_a if step == 2 else row_b, acc)
        total = total + fresh.astype(F32)
    scale = total[:, 2 * WIDTH :]
    chunk = jnp.concatenate([total[:, :WIDTH] * scale, total[:, WIDTH : 2 * WIDTH] * scale], axis=1).astype(BF16)
    chunk, row_a, row_b = barrier((chunk, row_a, row_b))
    for turn, step in enumerate((2, 1, 3, 0)):
        chunk, acc = barrier((chunk, acc))
        fresh = permute(chunk, HALVING[step])
        if turn == 0:
            ends = [
                (jnp.where(even_x, row_b[b : b + 1], row_a[b : b + 1]), jnp.where(even_x, row_a[b : b + 1], row_b[b : b + 1]))
                for b in (0, CY - 1)
            ]
            left, right = (
                jnp.concatenate([low, upper[b : b + 1], lower[b : b + 1], high], axis=0)
                for b, (low, high) in zip((0, CY - 1), ends)
            )
            far_send, near_send = jnp.where(even_y, left, right), jnp.where(even_y, right, left)
            column_b = lax.ppermute(far_send, "gy", column_pairs(False))
        elif turn == 1:
            near_send, chunk = barrier((near_send, chunk))
            column_a = lax.ppermute(near_send, "gy", column_pairs(True))
        elif turn == 2:
            acc = beyond(False, 2, column_a, acc)
        elif turn == 3:
            acc = beyond(False, 3, column_b, acc)
        parts = (
            (),
            ((cos_near, sin_near, 0, 0),),
            ((cos_next, sin_next, 0, 128),),
            ((cos_near, sin_near, 128, 256), (cos_next, sin_next, 128, 384)),
        )[turn]
        if parts:
            far = (cos_far, sin_far, w_in, w_out) if turn > 1 else ()
            acc = recip_piece(parts, far, chunk, acc.reshape(1024, WIDTH)).reshape(CX * CY, ATOMS, WIDTH)
        if step:
            chunk = jnp.concatenate([chunk, fresh], axis=0)
    acc = acc.reshape(1024, WIDTH)

    out = final(
        cos_far, sin_far, fresh, upper, lower, acc, norm_gain.reshape(1, WIDTH), w_in, w_out
    )
    return out.reshape(CX, CY, ATOMS, WIDTH)


def solution(mesh):
    in_specs = (
        P("gx", "gy", None, None),
        P("gx", "gy", None, None),
        P("gx", "gy", None),
        P("gx", "gy"),
        P(),
        P(),
        P(),
        P(("gx", "gy"), None),
        P(),
        P(),
        P(),
    )
    out_specs = P("gx", "gy", None, None)
    return jax.shard_map(
        per_device, mesh=mesh, in_specs=in_specs, out_specs=out_specs, check_vma=False
    )
```

```python
import functools

import jax
import jax.numpy as jnp
from jax import lax
from jax.experimental import pallas as pl
from jax.experimental.pallas import tpu as pltpu
from jax.sharding import PartitionSpec as P

slab_depth = 2.0
epsilon = 1e-06
LOG2E = 1.4426950408889634
AXES = ("gx", "gy")
F32 = jnp.float32
BF16 = jnp.bfloat16
CX, CY, ATOMS, WIDTH = 2, 4, 128, 256
PACK = 144
VMEM = pltpu.VMEM

SIN_COEF = (3.14159027, -5.16740673, 2.54401052, -0.55946246)
COS_COEF = (0.99999325, -4.93393467, 4.0412481, -1.22203176)


def linear(x, y, z, core):
    return (x * 4 + z % 4) * 16 + y * 4 + (z // 4) * 2 + core


def partner_list(step):
    pairs = []
    for x in range(4):
        for y in range(4):
            for z in range(8):
                for core in range(2):
                    pairs.append((linear(x, y, z, core), linear(*step(x, y, z, core))))
    return pairs


def flip_core(x, y, z, core):
    return x, y, z, 1 - core


def flip_x(first, second):
    def step(x, y, z, core):
        return x ^ (second if core else first), y, z, core

    return step


def flip_y(first, second):
    def step(x, y, z, core):
        return x, y ^ (second if core else first), z, core

    return step


def flip_z(which):
    table = ((1, 0, 3, 2, 5, 4, 7, 6), (7, 2, 1, 4, 3, 6, 5, 0), (3, 6, 5, 0, 7, 2, 1, 4))[which]

    def step(x, y, z, core):
        return x, y, table[z] if core == 0 else (table[(z - 1) % 8] + 1) % 8, core

    return step


HALVING = (flip_core, flip_y(1, 3), flip_y(3, 1), flip_x(1, 3))
DOUBLING = (flip_x(3, 1), flip_z(0), flip_z(1), flip_z(2))
CHUNK = 64


def permute(value, step):
    return lax.ppermute(value, AXES, partner_list(step))


def my_place():
    gx, gy = lax.axis_index("gx"), lax.axis_index("gy")
    return gx // 4, gy // 4, (gx % 4) + 4 * ((gy // 2) % 2), gy % 2


def vector_order():
    x, y, z, core = my_place()
    pos = lax.broadcasted_iota(jnp.int32, (1, 1024), 1)
    rest = pos % 4
    mz = (pos // 4) % 8
    mb = (pos // 32) % 2
    b2 = (pos // 64) % 2
    b3 = (pos // 128) % 2
    b1 = (pos // 256) % 2
    owner = core ^ (pos // 512)
    oy = y ^ jnp.where(owner == 0, b1 ^ (3 * b2), (3 * b1) ^ b2)
    coset = jnp.where(owner == 0, (x ^ (x >> 1)) & 1, x >> 1) ^ b3
    ox = jnp.where(owner == 0, coset ^ (3 * mb), 2 * coset + mb)
    return linear(ox, oy, mz, owner) * 4 + rest


HALF = 512


def wave_kernel(first, place, coords, miller, order, source, cos_out, sin_out, sums, *rest):
    cos_ref, sin_ref, copies = cos_out, sin_out, []
    if first:
        turned, packed, features = rest[0], rest[1:3], rest[3]
        coords_in, miller_in = coords, miller
        coords, miller, cos_ref, sin_ref, sems, table_sems = rest[4:]
        fetch = [
            pltpu.make_async_copy(coords_in, coords, sems.at[1]),
            pltpu.make_async_copy(miller_in, miller, sems.at[2]),
        ]
        load = pltpu.make_async_copy(source, features, sems.at[0])
        for copy in fetch + [load]:
            copy.start()
    else:
        turned, fetch = source, ()
    size = order.shape[1]
    natural = lax.broadcasted_iota(jnp.int32, (1024, size), 0)
    pick = jnp.where(natural == order[...], 1.0, 0.0).astype(BF16)
    for copy in fetch:
        copy.wait()
    number = miller[...].astype(F32)
    five = jnp.concatenate([number, number[0:2], jnp.zeros((3, 1024), F32)], axis=0).astype(BF16)
    placed = jnp.dot(five, pick, preferred_element_type=F32).astype(BF16)
    ones = jnp.ones((1, ATOMS), F32)

    for cell in range(CX * CY):
        rows_at = pl.ds(cell * ATOMS, ATOMS)
        ia, ib = cell // CY, cell % CY
        block = [coords[ia, d, ib : ib + 1, :].astype(F32) for d in range(3)]
        along = (place[0] * CX + ia).astype(F32) / 32.0
        across = (place[1] * CY + ib).astype(F32) / 64.0
        rows = jnp.concatenate(
            [
                block[0] / 32.0,
                block[1] / 64.0,
                block[2] / slab_depth,
                along * ones,
                across * ones,
                jnp.zeros((3, ATOMS), F32),
            ],
            axis=0,
        )
        at = rows.T.astype(BF16)
        for j in range(size // 256):
            lanes = slice(j * 256, (j + 1) * 256)
            angle = jnp.dot(at, placed[:, lanes], preferred_element_type=F32)
            r = angle - jnp.round(angle)
            s = r * r
            sine = SIN_COEF[3]
            cosine = COS_COEF[3]
            for a in (2, 1, 0):
                sine = sine * s + SIN_COEF[a]
                cosine = cosine * s + COS_COEF[a]
            sine = sine * r
            double = sine + sine
            cos_ref[rows_at, lanes] = (1.0 - double * sine).astype(BF16)
            sin_ref[rows_at, lanes] = (double * cosine).astype(BF16)

        if first:
            for i, (table, target) in enumerate(((cos_ref, cos_out), (sin_ref, sin_out))):
                copy = pltpu.make_async_copy(table.at[rows_at], target.at[rows_at], table_sems.at[i, cell])
                copy.start()
                copies.append(copy)

    if first:
        load.wait()
        turned[...] = features[...].astype(F32).T.astype(BF16)
        for cell in range(CX * CY):
            ia, ib = cell // CY, cell % CY
            packed[ia][ib, 0:ATOMS, :] = features[cell * ATOMS : (cell + 1) * ATOMS, :]
            rows = [coords[ia, d, ib : ib + 1, :].astype(F32) for d in range(3)]
            rows = jnp.concatenate(rows + [jnp.zeros((PACK - ATOMS - 3, ATOMS), F32)], axis=0).astype(BF16)
            packed[ia][ib, ATOMS:PACK, :] = jnp.concatenate([rows, jnp.zeros_like(rows)], axis=1)
    for col, table in ((0, cos_ref), (1, sin_ref)):
        total = jnp.dot(turned[...], table[...], preferred_element_type=F32)
        sums[:, col * WIDTH : (col + 1) * WIDTH] = total.T.astype(sums.dtype)
    for copy in copies:
        copy.wait()


def waves(place, coords, miller, order, source, first):
    vm = pl.BlockSpec(memory_space=VMEM)
    hbm = pl.BlockSpec(memory_space=pl.ANY)
    place_of = hbm if first else vm
    size = order.shape[1]
    out_shape = [
        (pltpu.MemorySpace.HBM if first else pltpu.MemorySpace.VMEM)((1024, size), BF16),
        (pltpu.MemorySpace.HBM if first else pltpu.MemorySpace.VMEM)((1024, size), BF16),
        jax.ShapeDtypeStruct((size, 2 * WIDTH), BF16 if first else F32),
    ]
    scratch = []
    if first:
        source, coords, miller = (
            pltpu.with_memory_space_constraint(value, pltpu.MemorySpace.HBM) for value in (source, coords, miller)
        )
        out_shape.append(jax.ShapeDtypeStruct((WIDTH, 1024), BF16))
        out_shape += [jax.ShapeDtypeStruct((CY, PACK, WIDTH), BF16)] * CX
        scratch = [VMEM((1024, WIDTH), BF16), VMEM(coords.shape, BF16), VMEM(miller.shape, jnp.int32)]
        scratch += [VMEM((1024, size), BF16)] * 2 + [pltpu.SemaphoreType.DMA((3,)), pltpu.SemaphoreType.DMA((2, CX * CY))]
    return pl.pallas_call(
        functools.partial(wave_kernel, first),
        out_shape=out_shape,
        in_specs=[pl.BlockSpec(memory_space=pltpu.SMEM), place_of, place_of, vm, place_of],
        out_specs=[place_of, place_of] + [vm] * (len(out_shape) - 2),
        scratch_shapes=scratch,
        compiler_params=pltpu.CompilerParams(vmem_limit_bytes=14 * 1024 * 1024),
        cost_estimate=pl.CostEstimate(flops=size * 4_000_000, bytes_accessed=3_000_000, transcendentals=0),
        name="wave_tables",
    )(place, coords, miller, order, source)


def prepare_kernel(place, near_count, near_list, coords, row_filter, live, mine, filters):
    shape = (CX * CY, 9)
    cell = lax.broadcasted_iota(jnp.int32, shape, 0)
    slot = lax.broadcasted_iota(jnp.int32, shape, 1)
    entry = near_list[...]
    step_x = ((entry >> 6) - (place[0] * CX + cell // CY) + 1) & 31
    step_y = ((entry & 63) - (place[1] * CY + cell % CY) + 1) & 63
    count = jnp.zeros(shape, jnp.int32)
    for c in range(CX * CY):
        count = jnp.where(cell == c, near_count[c], count)
    code = jnp.where(slot < count, step_x * 3 + step_y, -1)
    for o in range(9):
        live[:, o : o + 1] = jnp.max(jnp.where(code == o, 1.0, 0.0), axis=1, keepdims=True)
    for c in range(CX * CY):
        ia, ib = c // CY, c % CY
        rows = [coords[ia, d, ib : ib + 1, :].astype(F32) for d in range(3)]
        columns = jnp.concatenate(rows + [jnp.zeros((5, ATOMS), F32)], axis=0).T
        for d in range(3):
            mine[c, d] = jnp.broadcast_to(columns[:, d : d + 1], (ATOMS, ATOMS))
    x, z = place[0] // 4, place[0] % 4 + 4 * ((place[1] // 2) % 2)
    member = jnp.where(place[1] % 2 == 0, x // 2, x % 2) * 8 + z
    whole = jnp.concatenate([row_filter[...].astype(F32)] * (CHUNK // 4), axis=0)
    slots = lax.broadcasted_iota(jnp.int32, (CHUNK, WIDTH), 0) // 4
    filters[...] = jnp.where(slots == member, whole, 0.0)


def prepare(place, near_count, near_list, coords, row_filter):
    vm = pl.BlockSpec(memory_space=VMEM)
    sm = pl.BlockSpec(memory_space=pltpu.SMEM)
    return pl.pallas_call(
        prepare_kernel,
        out_shape=(
            jax.ShapeDtypeStruct((CX * CY, 9), F32),
            jax.ShapeDtypeStruct((CX * CY, 3, ATOMS, ATOMS), F32),
            jax.ShapeDtypeStruct((CHUNK, WIDTH), F32),
        ),
        in_specs=[sm, sm, vm, vm, vm],
        out_specs=(vm, vm, vm),
        compiler_params=pltpu.CompilerParams(vmem_limit_bytes=6 * 1024 * 1024),
        cost_estimate=pl.CostEstimate(flops=500_000_000, bytes_accessed=100_000, transcendentals=0),
        name="radial_prepare",
    )(place, near_count, near_list, coords, row_filter)


def radial_kernel(near_cells, fresh, rates, live, filters, mine, *rest):
    acc, scaled = rest[-2:]
    start = rest[-3]
    done = set()
    for i, ((na, nb), (source, at)) in enumerate(near_cells):
        cell_block = rest[source].at[at]
        values = cell_block[0:ATOMS, :]
        for k in range(8):
            scaled[i % 2, k * ATOMS : (k + 1) * ATOMS, :] = values * filters[k : k + 1, :]
        near = cell_block[ATOMS:PACK, 0:ATOMS].astype(F32)
        for ia in range(max(0, na - 1), min(CX, na + 2)):
            for ib in range(max(0, nb - 1), min(CY, nb + 2)):
                u, v = na - ia, nb - ib
                cell = ia * CY + ib
                dx = (near[0:1] + float(u)) - mine[cell, 0]
                dy = (near[1:2] + float(v)) - mine[cell, 1]
                dz = near[2:3] - mine[cell, 2]
                dist = dx * dx + dy * dy + dz * dz
                kernel = jnp.concatenate(
                    [jnp.exp2(dist * (rates[k] * -LOG2E)).astype(BF16) for k in range(8)], axis=1
                )
                o = (u + 1) * 3 + v + 1
                part = jnp.dot(kernel, scaled[i % 2], preferred_element_type=F32) * live[cell : cell + 1, o : o + 1]
                if cell in done:
                    acc[cell] += part
                elif fresh:
                    acc[cell] = part
                else:
                    acc[cell] = start[cell] + part
                done.add(cell)
    for cell in range(CX * CY):
        if cell not in done:
            acc[cell] = jnp.zeros((ATOMS, WIDTH), F32) if fresh else start[cell]


def radial_piece(near_cells, gammas, live, filters, mine, blocks, acc):
    vm = pl.BlockSpec(memory_space=VMEM)
    sm = pl.BlockSpec(memory_space=pltpu.SMEM)
    fresh = acc is None
    arrays = (gammas, live, filters, mine) + blocks + (() if fresh else (acc,))
    return pl.pallas_call(
        functools.partial(radial_kernel, near_cells, fresh),
        out_shape=jax.ShapeDtypeStruct((CX * CY, ATOMS, WIDTH), F32),
        in_specs=[sm] + [vm] * (len(arrays) - 1),
        out_specs=vm,
        scratch_shapes=[VMEM((2, 8 * ATOMS, WIDTH), BF16)],
        input_output_aliases={} if fresh else {len(arrays) - 1: 0},
        compiler_params=pltpu.CompilerParams(vmem_limit_bytes=10 * 1024 * 1024),
        cost_estimate=pl.CostEstimate(flops=2_000_000_000, bytes_accessed=2_000_000, transcendentals=0),
        name="radial_piece",
    )(*arrays)


def edge_kernel(along_x, which, sides, rates, live, filters, mine, block, start, acc, scaled):
    low_side = sides[which] < 0
    step = jnp.where(low_side, -1.0, 1.0)
    across = CY if along_x else CX
    totals = [None] * across
    places = []
    for own in range(across):
        at = (own, (CX - 1) * CY + own) if along_x else (own * CY, own * CY + CY - 1)
        places.append((at, jnp.where(low_side, at[0], at[1])))
    for i in range(CY if along_x else CX + 2):
        line = i if along_x else i - 1
        values = block[i, 0:ATOMS, :]
        for k in range(8):
            scaled[i % 2, k * ATOMS : (k + 1) * ATOMS, :] = values * filters[k : k + 1, :]
        near = block[i, ATOMS:PACK, 0:ATOMS].astype(F32)
        for own in range(max(0, line - 1), min(across, line + 2)):
            shift = line - own
            (cell_low, cell_high), cell = places[own]
            u, v = (step, float(shift)) if along_x else (float(shift), step)
            dx = (near[0:1] + u) - mine[cell, 0]
            dy = (near[1:2] + v) - mine[cell, 1]
            dz = near[2:3] - mine[cell, 2]
            dist = dx * dx + dy * dy + dz * dz
            kernel = jnp.concatenate([jnp.exp2(dist * (rates[k] * -LOG2E)).astype(BF16) for k in range(8)], axis=1)
            o_low, o_high = (shift + 1, 7 + shift) if along_x else (3 * shift + 3, 3 * shift + 5)
            weight = jnp.where(
                low_side,
                live[cell_low : cell_low + 1, o_low : o_low + 1],
                live[cell_high : cell_high + 1, o_high : o_high + 1],
            )
            part = jnp.dot(kernel, scaled[i % 2], preferred_element_type=F32) * weight
            totals[own] = part if totals[own] is None else totals[own] + part
            if line == min(across - 1 + (0 if along_x else 1), own + 1):
                acc[cell] = start[cell] + totals[own]
    for cell in range(CX * CY):
        at_low = cell < CY if along_x else cell % CY == 0
        at_high = cell >= CY if along_x else cell % CY == CY - 1
        if along_x:
            keep_it = jnp.logical_not(low_side) if at_low else low_side
        elif at_low:
            keep_it = jnp.logical_not(low_side)
        elif at_high:
            keep_it = low_side
        else:
            keep_it = None

        def keep_cell(cell=cell):
            acc[cell] = start[cell]

        if keep_it is None:
            keep_cell()
        else:
            pl.when(keep_it)(keep_cell)


def edge_piece(along_x, which, sides, gammas, live, filters, mine, block, acc):
    flops = 20_000_000_000
    vm = pl.BlockSpec(memory_space=VMEM)
    sm = pl.BlockSpec(memory_space=pltpu.SMEM)
    return pl.pallas_call(
        functools.partial(edge_kernel, along_x, which),
        out_shape=jax.ShapeDtypeStruct((CX * CY, ATOMS, WIDTH), F32),
        in_specs=[sm, sm] + [vm] * 5,
        out_specs=vm,
        scratch_shapes=[VMEM((2, 8 * ATOMS, WIDTH), BF16)],
        input_output_aliases={6: 0},
        compiler_params=pltpu.CompilerParams(vmem_limit_bytes=10 * 1024 * 1024),
        cost_estimate=pl.CostEstimate(flops=flops, bytes_accessed=2_000_000, transcendentals=0),
        name="radial_edge",
    )(sides, gammas, live, filters, mine, block, acc)


def recip_kernel(spots, *refs):
    coef, start, acc = refs[-3:]
    for row in range(4):
        rows = slice(row * 256, row * 256 + 256)
        total = start[rows]
        for i, (column, at) in enumerate(spots):
            lanes, span = slice(column, column + 128), slice(at, at + 128)
            total += jnp.dot(refs[2 * i][rows, lanes], coef[span, 0:WIDTH], preferred_element_type=F32)
            total += jnp.dot(refs[2 * i + 1][rows, lanes], coef[span, WIDTH:], preferred_element_type=F32)
        acc[rows] = total


def recip_piece(parts, far, coef, acc):
    vm = pl.BlockSpec(memory_space=VMEM)
    tables = [table for part in parts for table in part[:2]] + list(far)
    return pl.pallas_call(
        functools.partial(recip_kernel, tuple(part[2:] for part in parts)),
        out_shape=jax.ShapeDtypeStruct((1024, WIDTH), F32),
        in_specs=[vm] * (len(tables) + 2),
        out_specs=vm,
        input_output_aliases={len(tables) + 1: 0},
        compiler_params=pltpu.CompilerParams(vmem_limit_bytes=10 * 1024 * 1024),
        cost_estimate=pl.CostEstimate(flops=10_000_000_000, bytes_accessed=2_000_000, transcendentals=0),
        name="recip_piece",
    )(*tables, coef, acc)


def final_kernel(cos_ref, sin_ref, coef_in, upper, lower, acc, gain, w_in, w_out, out, coef, result, sems):
    for block, source in enumerate((0, 2, 1, 3)):
        coef[block * 128 : block * 128 + 128, :] = coef_in[source * 128 : source * 128 + 128, :]
    copies = []
    for block in range(4):
        rows = pl.ds(block * 256, 256)
        recip = jnp.dot(cos_ref[rows, :], coef[:, 0:WIDTH], preferred_element_type=F32)
        recip += jnp.dot(sin_ref[rows, :], coef[:, WIDTH:], preferred_element_type=F32)
        cells = (upper, lower)[block // 2]
        features = jnp.concatenate([cells[block % 2 * 2 + i, 0:ATOMS, :] for i in range(2)], axis=0)
        mixed = features.astype(F32) + acc[rows, :] + recip
        power = jnp.mean(mixed * mixed, axis=-1, keepdims=True)
        normed = (mixed * lax.rsqrt(power + epsilon) * gain[...]).astype(BF16)
        v = jnp.dot(normed, w_in[...], preferred_element_type=F32)
        hidden = (v / (1.0 + jnp.exp(-v))).astype(BF16)
        result[rows, :] = (mixed + jnp.dot(hidden, w_out[...], preferred_element_type=F32)).astype(BF16)
        copy = pltpu.make_async_copy(result.at[rows], out.at[rows], sems.at[block])
        copy.start()
        copies.append(copy)
    for copy in copies:
        copy.wait()


def final(cos_table, sin_table, coef, upper, lower, acc, gain, w_in, w_out):
    whole = pl.BlockSpec(memory_space=VMEM)
    return pl.pallas_call(
        final_kernel,
        out_shape=pltpu.MemorySpace.HBM((1024, WIDTH), BF16),
        in_specs=[whole] * 9,
        out_specs=pl.BlockSpec(memory_space=pl.ANY),
        scratch_shapes=[VMEM((HALF, 2 * WIDTH), BF16), VMEM((1024, WIDTH), BF16), pltpu.SemaphoreType.DMA((4,))],
        compiler_params=pltpu.CompilerParams(vmem_limit_bytes=14 * 1024 * 1024),
        cost_estimate=pl.CostEstimate(flops=3_000_000_000, bytes_accessed=8_000_000, transcendentals=0),
        name="mix_and_network",
    )(cos_table, sin_table, coef, upper, lower, acc, gain, w_in, w_out)


def row_pairs(first):
    def other(gx):
        return (gx + 1) % 16 if (gx % 2 == 0) == first else (gx - 1) % 16

    return [(i, other(i)) for i in range(16)]


def column_pairs(first):
    return row_pairs(first)


def first_blocks(rows):
    return jnp.concatenate([rows[0:64], rows[128:192]], axis=0)


def second_blocks(rows):
    return jnp.concatenate([rows[64:128], rows[192:256]], axis=0)


def per_device(
    features,
    coords,
    nbr_cells,
    nbr_count,
    miller,
    gammas,
    radial_filter,
    reciprocal_filter,
    norm_gain,
    w_in,
    w_out,
):
    gx, gy = lax.axis_index("gx"), lax.axis_index("gy")
    place = jnp.stack([gx, gy]).astype(jnp.int32)
    own_rows = features.reshape(1024, WIDTH)
    turned = coords.transpose(0, 2, 1, 3)
    order = vector_order()
    barrier = lax.optimization_barrier

    cos_far, sin_far, send, across, upper, lower = waves(place, turned, miller, order[:, HALF:], own_rows, True)
    got = permute(send, HALVING[0])
    even_x, even_y = gx % 2 == 0, gy % 2 == 0
    sides = jnp.stack(
        [jnp.where(even_x, 1, -1), jnp.where(even_x, -1, 1), jnp.where(even_y, 1, -1), jnp.where(even_y, -1, 1)]
    ).astype(jnp.int32)
    row_a = lax.ppermute(jnp.where(even_x, lower, upper), "gx", row_pairs(True))
    row_b = lax.ppermute(jnp.where(even_x, upper, lower), "gx", row_pairs(False))
    cos_next, sin_next, keep_next = waves(place, turned, miller, order[:, 256:HALF], across, False)

    acc = None

    def own_piece(jb, acc):
        near_cells = tuple(((ja, jb), (ja, jb)) for ja in range(CX))
        return radial_piece(near_cells, gammas, live, radial_filter, mine, (upper, lower), acc)

    def beyond(along_x, which, block, acc):
        return edge_piece(along_x, which, sides, gammas, live, radial_filter, mine, block, acc)

    for step, height in ((1, 256), (2, 128), (3, 64)):
        if step == 2:
            send = (second_blocks(keep) + second_blocks(got).astype(F32)).astype(BF16)
        else:
            send = ((keep_next if step == 1 else keep[height:]) + got[height:].astype(F32)).astype(BF16)
        if step == 2:
            send, live, mine, filters = barrier((send, live, mine, filters))
        elif step == 3:
            send, acc = barrier((send, acc))
        fresh = permute(send, HALVING[step])
        if step == 1:
            across, place, send = barrier((across, place, send))
            cos_near, sin_near, keep = waves(place, turned, miller, order[:, :256], across, False)
            live, mine, filters = prepare(
                place, nbr_count.reshape(8), nbr_cells.reshape(8, 9), turned, reciprocal_filter
            )
        else:
            acc = own_piece(step - 2, acc)
        if step == 2:
            keep = first_blocks(keep) + first_blocks(got).astype(F32)
        else:
            keep = keep[:height] + got[:height].astype(F32)
        got = fresh
    total = jnp.concatenate([keep + got.astype(F32), filters], axis=1)
    for step in range(4):
        total, acc = barrier((total, acc))
        fresh = permute(total.astype(BF16), DOUBLING[step])
        if step < 2:
            acc = own_piece(step + 2, acc)
        else:
            acc = beyond(True, step - 2, row_a if step == 2 else row_b, acc)
        total = total + fresh.astype(F32)
    scale = total[:, 2 * WIDTH :]
    chunk = jnp.concatenate([total[:, :WIDTH] * scale, total[:, WIDTH : 2 * WIDTH] * scale], axis=1).astype(BF16)
    chunk, row_a, row_b = barrier((chunk, row_a, row_b))
    for turn, step in enumerate((2, 1, 3, 0)):
        chunk, acc = barrier((chunk, acc))
        fresh = permute(chunk, HALVING[step])
        if turn == 0:
            ends = [
                (jnp.where(even_x, row_b[b : b + 1], row_a[b : b + 1]), jnp.where(even_x, row_a[b : b + 1], row_b[b : b + 1]))
                for b in (0, CY - 1)
            ]
            left, right = (
                jnp.concatenate([low, upper[b : b + 1], lower[b : b + 1], high], axis=0)
                for b, (low, high) in zip((0, CY - 1), ends)
            )
            far_send, near_send = jnp.where(even_y, left, right), jnp.where(even_y, right, left)
            column_b = lax.ppermute(far_send, "gy", column_pairs(False))
        elif turn == 1:
            near_send, chunk = barrier((near_send, chunk))
            column_a = lax.ppermute(near_send, "gy", column_pairs(True))
        elif turn == 2:
            acc = beyond(False, 2, column_a, acc)
        parts = (
            (),
            ((cos_near, sin_near, 0, 0),),
            ((cos_next, sin_next, 0, 128),),
            ((cos_near, sin_near, 128, 256), (cos_next, sin_next, 128, 384)),
        )[turn]
        if parts:
            far = (cos_far, sin_far, w_in, w_out) if turn > 1 else ()
            acc = recip_piece(parts, far, chunk, acc.reshape(1024, WIDTH)).reshape(CX * CY, ATOMS, WIDTH)
        if turn == 2:
            acc = beyond(False, 3, column_b, acc)
        if step:
            chunk = jnp.concatenate([chunk, fresh], axis=0)
    acc = acc.reshape(1024, WIDTH)

    out = final(
        cos_far, sin_far, fresh, upper, lower, acc, norm_gain.reshape(1, WIDTH), w_in, w_out
    )
    return out.reshape(CX, CY, ATOMS, WIDTH)


def solution(mesh):
    in_specs = (
        P("gx", "gy", None, None),
        P("gx", "gy", None, None),
        P("gx", "gy", None),
        P("gx", "gy"),
        P(),
        P(),
        P(),
        P(("gx", "gy"), None),
        P(),
        P(),
        P(),
    )
    out_specs = P("gx", "gy", None, None)
    return jax.shard_map(
        per_device, mesh=mesh, in_specs=in_specs, out_specs=out_specs, check_vma=False
    )
```
